32 devices in a mesh: dp: 4 (over y, x), row: 4 (over z), col: 2 (over core).
Axes of the slice: x: 2, y: 2, z: 4, core: 2. Of those that a mesh axis runs over, the one named last changes fastest.
Arguments:
- tokens: bfloat16 [4096, 1088], P(('dp', 'row'), 'col'), may hold values from -64 to 64
- lengths: int32 [4, 2], P('dp'), may hold values from 0 to 1024, as said below
- first_gain: float32 [1088], P('col'), may hold values from 0.1 to 1.9
- first_shift: float32 [1088], P('col'), may hold values from -1.75 to 1.75
- qkv_weight: bfloat16 [1088, 3264], P('col', 'row'), may hold values from -0.1875 to 0.1875
- query_bias: float32 [1088], replicated, may hold values from -1.75 to 1.75
- value_bias: float32 [1088], replicated, may hold values from -1.75 to 1.75
- out_weight: bfloat16 [1088, 1088], P('row', 'col'), may hold values from -1 to 1
- out_bias: float32 [1088], P('col'), may hold values from -1.75 to 1.75
- second_gain: float32 [1088], P('col'), may hold values from 0.1 to 1.9
- second_shift: float32 [1088], P('col'), may hold values from -1.75 to 1.75
- up_weight: bfloat16 [1088, 4352], P('col', 'row'), may hold values from -0.1875 to 0.1875
- up_bias: float32 [4352], P('row'), may hold values from -1.75 to 1.75
- down_weight: bfloat16 [4352, 1088], P('row', 'col'), may hold values from -0.09375 to 0.09375
- down_bias: float32 [1088], P('col'), may hold values from -1.75 to 1.75
- cotangent: float32 [4096, 1088], P(('dp', 'row'), 'col'), may hold values from -6 to 6
Outputs:
- block_out: bfloat16 [4096, 1088], P(('dp', 'row'), 'col')
- input_grad: float32 [4096, 1088], P(('dp', 'row'), 'col')
- first_gain_grad: float32 [1088], P('col')
- first_shift_grad: float32 [1088], P('col')
- qkv_weight_grad: float32 [1088, 3264], P('col', 'row')
- query_bias_grad: float32 [1088], replicated
- value_bias_grad: float32 [1088], replicated
- out_weight_grad: float32 [1088, 1088], P('row', 'col')
- out_bias_grad: float32 [1088], P('col')
- second_gain_grad: float32 [1088], P('col')
- second_shift_grad: float32 [1088], P('col')
- up_weight_grad: float32 [1088, 4352], P('col', 'row')
- up_bias_grad: float32 [4352], P('row')
- down_weight_grad: float32 [4352, 1088], P('row', 'col')
- down_bias_grad: float32 [1088], P('col')
The draws below stay inside these ranges and needn't reach their ends.
Inputs may be any that keep to these rules, and one draw needn't show every extreme that they name: Row g holds the lengths of the two sequences packed from the first slot of data group g; the first is longer than 896, the two together take at most 1024 slots, and the slots after them are padding.
All inputs are finite; a program needn't handle non-finite values.
Results may differ from the reference program's by a relative error of at most 0.012.
Values may be sent and summed in bfloat16 or wider, within the bound.
No kernel may reach another device: no remote copies, remote signals or barrier semaphores. Data moves between devices by JAX's collectives and lax.ppermute only.
A program may use at most 128 MiB of HBM per device.

```python
import jax
import jax.numpy as jnp
from jax import lax

D = 1088
HEADS = 17
HEAD_DIM = 64
FF = 4352
TOK_G = 1024
BLOCK = 128
TOKENS = 4096
N_DP = 4


def draw_tokens(key, part):
    key = jax.random.fold_in(key, 11)
    row_key, col_key, noise_key = jax.random.split(key, 3)
    row_scales = jnp.exp(jax.random.uniform(row_key, (TOKENS, 1), jnp.float32, jnp.log(0.3), jnp.log(3.0)))
    ramp = jnp.exp(jnp.log(3.0) * (jnp.arange(D, dtype=jnp.float32) / D - 0.5))
    col_scales = jnp.exp(jax.random.uniform(col_key, (1, D), jnp.float32, jnp.log(0.3), jnp.log(3.0))) * ramp[None, :]
    values = jax.random.normal(noise_key, (TOKENS, D), jnp.float32)
    return jnp.clip(values * row_scales * col_scales, -64.0, 64.0).astype(jnp.bfloat16)


def draw_lengths(key, part):
    key = jax.random.fold_in(key, 7)
    spare_key, chosen_key, second_key = jax.random.split(key, 3)
    spare_rows = jax.random.randint(spare_key, (N_DP,), 0, BLOCK)
    chosen = jax.random.randint(chosen_key, (), 0, N_DP)
    spare_rows = jnp.where(jnp.arange(N_DP) == chosen, 0, spare_rows)
    second = jax.random.randint(second_key, (N_DP,), 0, spare_rows + 1)
    return jnp.stack([TOK_G - spare_rows, second], axis=1).astype(jnp.int32)


def level_of(key, shape, cuts, least, high):
    def one(dim, parts):
        heights = jax.random.uniform(jax.random.fold_in(jax.random.fold_in(key, 6), dim), (parts,), jnp.float32, least / len(cuts), high / len(cuts))
        return jnp.repeat(jnp.exp(heights), shape[dim] // parts).reshape((-1,) + (1,) * (len(shape) - dim - 1))

    factor_of = one(*cuts[0])
    for cut in cuts[1:]:
        factor_of = factor_of * one(*cut)
    return factor_of


def gaussian(stream_key, dims, width, most, shards=(), kind=jnp.bfloat16):
    gain = level_of(stream_key, dims, shards, -0.22, 0.18) if shards else 1.0
    values = jax.random.normal(stream_key, dims, jnp.float32) * width * gain
    return jnp.minimum(jnp.maximum(values, -most), most).astype(kind)


def setup_inputs(seed: int = 0) -> dict:
    key_list = jax.random.split(jax.random.key(seed), 17)
    return {
        "tokens": draw_tokens(jax.random.fold_in(key_list[16], 71), 0),
        "lengths": draw_lengths(jax.random.fold_in(key_list[16], 71), 0),
        "first_gain": jnp.clip(1.0 + 0.18 * jax.random.normal(key_list[2], (D,), jnp.float32), 0.1, 1.9),
        "first_shift": gaussian(key_list[3], (D,), 0.3, 1.75, ((0, 2),), jnp.float32),
        "qkv_weight": gaussian(key_list[4], (D, 3 * D), D ** -0.5, 0.1875, ((0, 2), (1, 4))),
        "query_bias": gaussian(key_list[5], (D,), 0.3, 1.75, (), jnp.float32),
        "value_bias": gaussian(key_list[6], (D,), 0.3, 1.75, (), jnp.float32),
        "out_weight": gaussian(key_list[7], (D, D), (D // 32) ** -0.5, 1.0, ((0, 4), (1, 2))),
        "out_bias": gaussian(key_list[8], (D,), 0.3, 1.75, ((0, 2),), jnp.float32),
        "second_gain": jnp.clip(1.0 + 0.18 * jax.random.normal(key_list[9], (D,), jnp.float32), 0.1, 1.9),
        "second_shift": gaussian(key_list[10], (D,), 0.3, 1.75, ((0, 2),), jnp.float32),
        "up_weight": gaussian(key_list[11], (D, FF), D ** -0.5, 0.1875, ((0, 2), (1, 4))),
        "up_bias": gaussian(key_list[12], (FF,), 0.3, 1.75, ((0, 4),), jnp.float32),
        "down_weight": gaussian(key_list[13], (FF, D), FF ** -0.5, 0.09375, ((0, 4), (1, 2))),
        "down_bias": gaussian(key_list[14], (D,), 0.3, 1.75, ((0, 2),), jnp.float32),
        "cotangent": gaussian(key_list[15], (TOKENS, D), 1.0, 6.0, ((0, 16), (1, 2)), jnp.float32),
    }


EPSILON = 1e-05
MASKED = -1e+30
HIGHEST = lax.Precision.HIGHEST

@jax.custom_vjp
def low(v):
    return lax.optimization_barrier(v.astype(jnp.bfloat16)).astype(jnp.float32)

@jax.custom_vjp
def low_back(v):
    return v

def low_keep(v):
    return (low(v), None)

def low_pass(kept, grad):
    return (grad,)

def back_keep(v):
    return (v, None)

def back_low(kept, grad):
    return (low(grad),)
low.defvjp(low_keep, low_pass)
low_back.defvjp(back_keep, back_low)

def matmul(operand, weights):
    return jnp.dot(operand, weights, precision=HIGHEST, preferred_element_type=jnp.float32)

def layer_norm(resid_in, norm_gain, norm_shift):
    mean_value = lax.optimization_barrier(jnp.mean(resid_in, axis=-1, keepdims=True))
    variance = lax.optimization_barrier(jnp.mean(resid_in * resid_in, axis=-1, keepdims=True)) - mean_value * mean_value
    return (resid_in - mean_value) * lax.rsqrt(variance + EPSILON) * norm_gain + norm_shift

def segments_of(positions, lengths_row):
    first_len = lengths_row[0]
    return (positions >= first_len).astype(jnp.int32) + (positions >= first_len + lengths_row[1]).astype(jnp.int32)

def attend_head(query_head, key_head, value_head, allowed_pairs):
    scores = low_back(matmul(query_head, key_head.T) * HEAD_DIM ** (-0.5))
    scores = jnp.where(allowed_pairs, scores, MASKED)
    top_score = lax.optimization_barrier(jnp.max(scores, axis=-1, keepdims=True))
    exponent = jnp.exp(scores - top_score)
    attn_probs = exponent / lax.optimization_barrier(jnp.sum(exponent, axis=-1, keepdims=True))
    return matmul(low(attn_probs), value_head)

def split_heads(matrix):
    return matrix.reshape(TOK_G, HEADS, HEAD_DIM).transpose(1, 0, 2)

def group_layer(params, resid_in, lengths_row):
    first_gain, first_shift, qkv_weight, query_bias, value_bias, out_weight, out_bias, second_gain, second_shift, up_weight, up_bias, down_weight, down_bias = params
    positions = jnp.arange(TOK_G, dtype=jnp.int32)
    segment = segments_of(positions, lengths_row)
    allowed_pairs = (positions[None, :] <= positions[:, None]) & (segment[None, :] == segment[:, None])
    normed_attn = low(layer_norm(resid_in, first_gain, first_shift))
    qkv_full = matmul(normed_attn, qkv_weight)
    queries = low_back(low(qkv_full[:, :D] + query_bias))
    keys_all = low_back(low(qkv_full[:, D:2 * D]))
    values_all = low_back(low(qkv_full[:, 2 * D:] + value_bias))

    def one_head(triple):
        return attend_head(triple[0], triple[1], triple[2], allowed_pairs)
    per_head = lax.map(jax.checkpoint(one_head), (split_heads(queries), split_heads(keys_all), split_heads(values_all)))
    attention = low_back(low(per_head.transpose(1, 0, 2).reshape(TOK_G, D)))
    resid_mid = resid_in + low_back(matmul(attention, out_weight) + out_bias)
    normed_mlp = low(layer_norm(resid_mid, second_gain, second_shift))
    pre_act = low_back(matmul(normed_mlp, up_weight) + up_bias)
    activated = low(jax.nn.gelu(pre_act, approximate=True))
    return resid_mid + low_back(matmul(activated, down_weight) + down_bias)

def reference(tokens, lengths, first_gain, first_shift, qkv_weight, query_bias, value_bias, out_weight, out_bias, second_gain, second_shift, up_weight, up_bias, down_weight, down_bias, cotangent):
    params = tuple((item.astype(jnp.float32) for item in (first_gain, first_shift, qkv_weight, query_bias, value_bias, out_weight, out_bias, second_gain, second_shift, up_weight, up_bias, down_weight, down_bias)))
    inputs = tokens.astype(jnp.float32).reshape(N_DP, TOK_G, D)
    layer = jax.checkpoint(group_layer)

    def forward(weights_in, inputs_in):

        def step(carried, pieces):
            return (carried, layer(weights_in, pieces[0], pieces[1]))
        return lax.scan(step, jnp.zeros((), jnp.float32), (inputs_in, lengths))[1]
    outputs, pullback = jax.vjp(forward, params, inputs)
    positions = jnp.arange(TOK_G, dtype=jnp.int32)

    def live_of(lengths_row):
        return (segments_of(positions, lengths_row) < 2).astype(jnp.float32)
    live_rows = jax.vmap(live_of)(lengths)
    grad_out = cotangent.astype(jnp.float32).reshape(N_DP, TOK_G, D) * live_rows[:, :, None]
    param_grads, input_grad = pullback(grad_out)
    g_first_gain, g_first_shift, g_qkv, g_query_bias, g_value_bias, g_out, g_out_bias, g_second_gain, g_second_shift, g_up, g_up_bias, g_down, g_down_bias = param_grads
    return (outputs.reshape(TOKENS, D).astype(jnp.bfloat16), input_grad.reshape(TOKENS, D), g_first_gain, g_first_shift, g_qkv, g_query_bias, g_value_bias, g_out, g_out_bias, g_second_gain, g_second_shift, g_up, g_up_bias, g_down, g_down_bias)
```

```python
import functools

import jax
import jax.numpy as jnp
import numpy as np
from jax import lax
from jax.experimental import pallas as pl
from jax.experimental.pallas import tpu as pltpu
from jax.sharding import PartitionSpec as P

D = 1088
HEADS = 17
HEAD_DIM = 64
FF = 4352
TOK_G = 1024

EPSILON = 1e-05
MASKED = -1e30
CHUNK = 256
BF16 = jnp.bfloat16
F32 = jnp.float32


def swap(payload, axis, distance):
    size = lax.axis_size(axis)
    return lax.ppermute(payload, axis, [(i, i ^ distance) for i in range(size)])


def gather_blocks(payload, axis):
    return [payload] + [swap(payload, axis, k) for k in range(1, lax.axis_size(axis))]


def send_blocks(blocks, axis):
    return [blocks[0]] + [swap(blocks[k], axis, k) for k in range(1, len(blocks))]


def scatter_sum(blocks, axis):
    received = [swap(blocks[k].astype(BF16), axis, k) for k in range(1, len(blocks))]
    total = blocks[0]
    for item in received:
        total = total + item.astype(F32)
    return total


def rows_of(matrix, parts):
    size = matrix.shape[0] // parts
    return [matrix[k * size : (k + 1) * size] for k in range(parts)]


def head_starts(rows):
    return [int(np.floor(HEADS * r / rows + 0.5)) for r in range(rows + 1)]


def most_heads(rows):
    starts = head_starts(rows)
    return max(b - a for a, b in zip(starts[:-1], starts[1:]))


def window_columns(rows, copies):
    starts = head_starts(rows)
    width = most_heads(rows) * HEAD_DIM
    table = np.full((rows, copies * width), -1, np.int64)
    for r in range(rows):
        count = (starts[r + 1] - starts[r]) * HEAD_DIM
        for t in range(copies):
            table[r, t * width : t * width + count] = t * D + starts[r] * HEAD_DIM + np.arange(count)
    return table


def move_tables(rows, copies):
    windows = window_columns(rows, copies)
    shard = copies * D // rows
    moves = []
    for k in range(rows):
        places, columns = [], []
        for r in range(rows):
            place = [p for p in range(windows.shape[1]) if windows[r, p] >= 0 and windows[r, p] // shard == r ^ k]
            places.append(place)
            columns.append([int(windows[r, p] % shard) for p in place])
        longest = max(len(place) for place in places)
        if longest == 0:
            continue
        longest = -(-longest // 16) * 16
        at = np.full((rows, longest), -1, np.int32)
        frm = np.full((rows, longest), -1, np.int32)
        for r in range(rows):
            at[r, : len(places[r])] = places[r]
            frm[r ^ k, : len(columns[r])] = columns[r]
        moves.append((k, at, frm))
    return moves, windows.shape[1], shard


def one_hot(table, row_index, size):
    chosen = lax.dynamic_index_in_dim(jnp.asarray(table), row_index, 0, keepdims=True)
    return (lax.broadcasted_iota(jnp.int32, (size, table.shape[1]), 0) == chosen).astype(BF16)


def mm(a, b):
    return jnp.dot(a, b, preferred_element_type=F32)


def mm_nt(a, b):
    return lax.dot_general(a, b, (((1,), (1,)), ((), ())), preferred_element_type=F32)


def mm_tn(a, b):
    return lax.dot_general(a, b, (((0,), (0,)), ((), ())), preferred_element_type=F32)


def to_window(matrix, moves, window, shard, row_index):
    total = 0.0
    for k, at, frm in moves:
        if k == 0:
            pick = mm_nt(one_hot(frm, row_index, shard), one_hot(at, row_index, window)).astype(BF16)
            total = total + mm(matrix, pick)
        else:
            slab = swap(mm(matrix, one_hot(frm, row_index, shard)).astype(BF16), "row", k)
            total = total + mm_nt(slab, one_hot(at, row_index, window))
    return total.astype(BF16)


def from_window(matrix, moves, window, shard, row_index):
    total = 0.0
    for k, at, frm in moves:
        if k == 0:
            pick = mm_nt(one_hot(at, row_index, window), one_hot(frm, row_index, shard)).astype(BF16)
            total = total + mm(matrix, pick)
        else:
            slab = swap(mm(matrix, one_hot(at, row_index, window)).astype(BF16), "row", k)
            total = total + mm_nt(slab, one_hot(frm, row_index, shard))
    return total.astype(BF16)


def positions(start, shape, dim, block, col):
    at = lax.broadcasted_iota(jnp.int32, shape, dim) + start
    shift = block.bit_length() - 1
    return lax.shift_left(lax.shift_right_logical(at, shift), shift + 1) + (at & (block - 1)) + col * block


def segments(pos, scal_ref):
    first = scal_ref[2]
    return (pos >= first).astype(jnp.int32) + (pos >= first + scal_ref[3]).astype(jnp.int32)


def mask_bias(scal_ref, query_at, query_shape, query_dim, key_shape, key_dim, block, key_col):
    query_pos = positions(query_at, query_shape, query_dim, block, scal_ref[1])
    key_pos = positions(0, key_shape, key_dim, block, key_col)
    allowed = (key_pos <= query_pos) & (segments(key_pos, scal_ref) == segments(query_pos, scal_ref))
    return jnp.where(allowed, 0.0, MASKED)


def in_order(source_ref, target_ref, row, blocks, block):
    for j in range(blocks):
        target_ref[j * block : (j + 1) * block, :] = source_ref[j ^ row]


def forward_kernel(blocks, block, heads, scal_ref, q_ref, kv0_ref, kv1_ref, out_ref, lse_ref, q_s, kv0_s, kv1_s, o_s):
    row = scal_ref[0]
    width = heads * HEAD_DIM
    in_order(q_ref, q_s, row, blocks, block)
    in_order(kv0_ref, kv0_s, row, blocks, block)
    in_order(kv1_ref, kv1_s, row, blocks, block)
    own = scal_ref[1]
    for i in range(blocks * block // CHUNK):
        span = slice(i * CHUNK, (i + 1) * CHUNK)
        keys = (i + 1) * CHUNK
        shape = (CHUNK, keys)
        bias0 = mask_bias(scal_ref, i * CHUNK, (CHUNK, 1), 0, (1, keys), 1, block, own)
        bias1 = mask_bias(scal_ref, i * CHUNK, (CHUNK, 1), 0, (1, keys), 1, block, 1 - own)
        for h in range(heads):
            at = slice(h * HEAD_DIM, (h + 1) * HEAD_DIM)
            va = slice(width + h * HEAD_DIM, width + (h + 1) * HEAD_DIM)
            query = q_s[span, at]
            s0 = mm_nt(query, kv0_s[:keys, at]) + bias0
            s1 = mm_nt(query, kv1_s[:keys, at]) + bias1
            top = jnp.maximum(jnp.max(s0, axis=1, keepdims=True), jnp.max(s1, axis=1, keepdims=True))
            e0 = jnp.exp(s0 - top)
            e1 = jnp.exp(s1 - top)
            total = jnp.sum(e0, axis=1, keepdims=True) + jnp.sum(e1, axis=1, keepdims=True)
            result = mm(e0.astype(BF16), kv0_s[:keys, va]) + mm(e1.astype(BF16), kv1_s[:keys, va])
            o_s[span, at] = (result / total).astype(BF16)
            lse_ref[span, h : h + 1] = top + jnp.log(total)
    for j in range(blocks):
        out_ref[j ^ row] = o_s[j * block : (j + 1) * block, :]


def backward_kernel(
    blocks,
    block,
    heads,
    scal_ref,
    q_ref,
    kv0_ref,
    kv1_ref,
    g_ref,
    lse_ref,
    dq_ref,
    own_ref,
    other_ref,
    q_s,
    kv0_s,
    kv1_s,
    g_s,
    dq_s,
    d0_s,
    d1_s,
):
    row = scal_ref[0]
    width = heads * HEAD_DIM
    in_order(q_ref, q_s, row, blocks, block)
    in_order(kv0_ref, kv0_s, row, blocks, block)
    in_order(kv1_ref, kv1_s, row, blocks, block)
    in_order(g_ref, g_s, row, blocks, block)
    own = scal_ref[1]
    chunks = blocks * block // CHUNK
    for i in reversed(range(chunks)):
        span = slice(i * CHUNK, (i + 1) * CHUNK)
        keys = (i + 1) * CHUNK
        bias0 = mask_bias(scal_ref, i * CHUNK, (1, CHUNK), 1, (keys, 1), 0, block, own)
        bias1 = mask_bias(scal_ref, i * CHUNK, (1, CHUNK), 1, (keys, 1), 0, block, 1 - own)
        for h in range(heads):
            at = slice(h * HEAD_DIM, (h + 1) * HEAD_DIM)
            va = slice(width + h * HEAD_DIM, width + (h + 1) * HEAD_DIM)
            query = q_s[span, at]
            grad = g_s[span, at]
            lse = lse_ref[h : h + 1, span]
            p0 = jnp.exp(mm_nt(kv0_s[:keys, at], query) + bias0 - lse)
            p1 = jnp.exp(mm_nt(kv1_s[:keys, at], query) + bias1 - lse)
            dp0 = mm_nt(kv0_s[:keys, va], grad)
            dp1 = mm_nt(kv1_s[:keys, va], grad)
            delta = jnp.sum(p0 * dp0, axis=0, keepdims=True) + jnp.sum(p1 * dp1, axis=0, keepdims=True)
            ds0 = (p0 * (dp0 - delta)).astype(BF16)
            ds1 = (p1 * (dp1 - delta)).astype(BF16)
            if i == chunks - 1:
                d0_s[:keys, at] = mm(ds0, query)
                d1_s[:keys, at] = mm(ds1, query)
                d0_s[:keys, va] = mm(p0.astype(BF16), grad)
                d1_s[:keys, va] = mm(p1.astype(BF16), grad)
            else:
                d0_s[:keys, at] += mm(ds0, query)
                d1_s[:keys, at] += mm(ds1, query)
                d0_s[:keys, va] += mm(p0.astype(BF16), grad)
                d1_s[:keys, va] += mm(p1.astype(BF16), grad)
            dquery = mm_tn(ds0, kv0_s[:keys, at]) + mm_tn(ds1, kv1_s[:keys, at])
            dq_s[span, at] = (dquery * HEAD_DIM ** (-0.5)).astype(BF16)
    for j in range(blocks):
        piece = slice(j * block, (j + 1) * block)
        dq_ref[j ^ row] = dq_s[piece, :]
        own_ref[j ^ row] = d0_s[piece, :]
        other_ref[j ^ row] = d1_s[piece, :].astype(BF16)


def vmem():
    return pl.BlockSpec(memory_space=pltpu.VMEM)


def smem():
    return pl.BlockSpec(memory_space=pltpu.SMEM)


def attend_forward(scal, queries, kv_own, kv_other, heads):
    blocks, block, width = queries.shape
    tokens = blocks * block
    return pl.pallas_call(
        functools.partial(forward_kernel, blocks, block, heads),
        out_shape=(
            jax.ShapeDtypeStruct((blocks, block, width), BF16),
            jax.ShapeDtypeStruct((tokens, heads), F32),
        ),
        in_specs=[smem(), vmem(), vmem(), vmem()],
        out_specs=(vmem(), vmem()),
        scratch_shapes=[
            pltpu.VMEM((tokens, width), BF16),
            pltpu.VMEM((tokens, 2 * width), BF16),
            pltpu.VMEM((tokens, 2 * width), BF16),
            pltpu.VMEM((tokens, width), BF16),
        ],
        compiler_params=pltpu.CompilerParams(vmem_limit_bytes=40 * 2**20),
        cost_estimate=pl.CostEstimate(
            flops=4 * tokens * 3 * tokens // 2 * width, bytes_accessed=6 * tokens * width * 2, transcendentals=heads * tokens * tokens
        ),
        name="attend_forward",
    )(scal, queries, kv_own, kv_other)


def attend_backward(scal, queries, kv_own, kv_other, grads, lse, heads):
    blocks, block, width = queries.shape
    tokens = blocks * block
    return pl.pallas_call(
        functools.partial(backward_kernel, blocks, block, heads),
        out_shape=(
            jax.ShapeDtypeStruct((blocks, block, width), BF16),
            jax.ShapeDtypeStruct((blocks, block, 2 * width), F32),
            jax.ShapeDtypeStruct((blocks, block, 2 * width), BF16),
        ),
        in_specs=[smem(), vmem(), vmem(), vmem(), vmem(), vmem()],
        out_specs=(vmem(), vmem(), vmem()),
        scratch_shapes=[
            pltpu.VMEM((tokens, width), BF16),
            pltpu.VMEM((tokens, 2 * width), BF16),
            pltpu.VMEM((tokens, 2 * width), BF16),
            pltpu.VMEM((tokens, width), BF16),
            pltpu.VMEM((tokens, width), BF16),
            pltpu.VMEM((tokens, 2 * width), F32),
            pltpu.VMEM((tokens, 2 * width), F32),
        ],
        compiler_params=pltpu.CompilerParams(vmem_limit_bytes=44 * 2**20),
        cost_estimate=pl.CostEstimate(
            flops=10 * tokens * 3 * tokens // 2 * width, bytes_accessed=14 * tokens * width * 2, transcendentals=heads * tokens * tokens
        ),
        name="attend_backward",
    )(scal, queries, kv_own, kv_other, grads, lse)


def norm_parts(resid_in):
    mean_value = jnp.sum(resid_in, axis=1, keepdims=True) / D
    square = jnp.sum(resid_in * resid_in, axis=1, keepdims=True) / D
    inverse = lax.rsqrt(square - mean_value * mean_value + EPSILON)
    return ((resid_in - mean_value) * inverse, inverse)


def norm_back(grad_in, normal, inverse, norm_gain):
    scaled = grad_in * norm_gain
    mean_scaled = jnp.sum(scaled, axis=1, keepdims=True) / D
    mean_cross = jnp.sum(scaled * normal, axis=1, keepdims=True) / D
    return inverse * (scaled - mean_scaled - normal * mean_cross)


def gelu_tanh(pre_value):
    return jax.nn.gelu(pre_value, approximate=True)


def on_device(
    tokens,
    lengths,
    first_gain,
    first_shift,
    qkv_weight,
    query_bias,
    value_bias,
    out_weight,
    out_bias,
    second_gain,
    second_shift,
    up_weight,
    up_bias,
    down_weight,
    down_bias,
    cotangent,
):
    rows = lax.axis_size("row")
    row = lax.axis_index("row")
    col = lax.axis_index("col")
    half = tokens.shape[1]
    block = tokens.shape[0] // 2
    heads = most_heads(rows)
    width = heads * HEAD_DIM

    def halves(matrix):
        pair = matrix.reshape(2, block, half)
        mine = lax.dynamic_index_in_dim(pair, col, 0, keepdims=False)
        other = lax.dynamic_index_in_dim(pair, 1 - col, 0, keepdims=False)
        return jnp.concatenate([mine, swap(other, "col", 1)], axis=1)

    def unhalves(matrix):
        mine = matrix[:, :half]
        other = swap(matrix[:, half:], "col", 1)
        return jnp.concatenate([jnp.where(col == 0, mine, other), jnp.where(col == 0, other, mine)], axis=0)

    x_own = halves(tokens)
    x_all = jnp.concatenate(gather_blocks(x_own, "row"), axis=0).astype(F32)

    vectors = jnp.stack([first_gain, first_shift, out_bias, second_gain, second_shift, down_bias])
    vectors = jnp.concatenate([vectors, swap(vectors, "col", 1)], axis=1)
    gain1, shift1, out_b, gain2, shift2, down_b = [vectors[i] for i in range(6)]

    qkv_moves = move_tables(rows, 3)
    out_moves = move_tables(rows, 1)
    qkv_head = to_window(qkv_weight, *qkv_moves, row)
    w_qkv = jnp.concatenate([qkv_head, swap(qkv_head, "col", 1)], axis=0)

    starts = jnp.asarray(np.array(head_starts(rows), np.int32))
    head_at = starts[row] * HEAD_DIM
    live_cols = jnp.arange(width, dtype=jnp.int32) < (starts[row + 1] - starts[row]) * HEAD_DIM

    def bias_window(vector):
        padded = jnp.concatenate([vector, jnp.zeros((width,), F32)])
        return jnp.where(live_cols, lax.dynamic_slice_in_dim(padded, head_at, width), 0.0)

    normal1, inverse1 = norm_parts(x_all)
    normed1 = (normal1 * gain1 + shift1).astype(BF16)
    qkv = mm(normed1, w_qkv)
    queries = (qkv[:, :width] + bias_window(query_bias)).astype(BF16) * BF16(HEAD_DIM ** (-0.5))
    bias_kv = jnp.concatenate([jnp.zeros((width,), F32), bias_window(value_bias)])
    kv_own = (qkv[:, width:] + bias_kv).astype(BF16)
    kv_other = swap(kv_own, "col", 1)
    queries = queries.reshape(rows, block, width)
    kv_own = kv_own.reshape(rows, block, 2 * width)
    kv_other = kv_other.reshape(rows, block, 2 * width)
    scal = jnp.stack([row.astype(jnp.int32), col.astype(jnp.int32), lengths[0, 0], lengths[0, 1]])
    attention, lse = attend_forward(scal, queries, kv_own, kv_other, heads)

    att_own = jnp.concatenate(send_blocks([attention[k] for k in range(rows)], "row"), axis=1)
    out_window = to_window(out_weight.T, *out_moves, row).T
    out_all = jnp.concatenate(gather_blocks(out_window, "row"), axis=0)
    w_out = jnp.concatenate([out_all, swap(out_all, "col", 1)], axis=1)
    resid_mid = x_own.astype(F32) + (mm(att_own, w_out) + out_b)

    normal2, inverse2 = norm_parts(resid_mid)
    normed2 = (normal2 * gain2 + shift2).astype(BF16)
    mlp_in = jnp.concatenate(gather_blocks(normed2, "row"), axis=0)
    w_up = jnp.concatenate([up_weight, swap(up_weight, "col", 1)], axis=0)
    w_down = jnp.concatenate([down_weight, swap(down_weight, "col", 1)], axis=1)

    cot_own = halves(cotangent)
    own_pos = (row * 2 + col) * block + jnp.arange(block, dtype=jnp.int32)
    live = own_pos < lengths[0, 0] + lengths[0, 1]
    grad_out = jnp.where(live[:, None], cot_own, 0.0)
    grad_out_low = grad_out.astype(BF16)
    g_all = jnp.concatenate(gather_blocks(grad_out_low, "row"), axis=0)
    down_bias_part = jnp.sum(grad_out_low.astype(F32), axis=0)

    pre_act = mm(mlp_in, w_up) + up_bias
    act, gelu_back = jax.vjp(gelu_tanh, pre_act)
    act = act.astype(BF16)
    grad_act = mm_nt(g_all, w_down)
    grad_pre = gelu_back(grad_act)[0].astype(BF16)
    up_bias_part = jnp.sum(grad_pre.astype(F32), axis=0)
    grad_normed2 = scatter_sum(rows_of(mm_nt(grad_pre, w_up), rows), "row")
    second_gain_part = jnp.sum(grad_normed2 * normal2, axis=0)
    second_shift_part = jnp.sum(grad_normed2, axis=0)
    grad_mid = grad_out + norm_back(grad_normed2, normal2, inverse2, gain2)
    grad_mid_low = grad_mid.astype(BF16)
    out_bias_part = jnp.sum(grad_mid_low.astype(F32), axis=0)

    grad_att = mm_nt(grad_mid_low, w_out).astype(BF16)
    grad_att = jnp.stack(send_blocks([grad_att[:, k * width : (k + 1) * width] for k in range(rows)], "row"))
    mid_all = jnp.concatenate(gather_blocks(grad_mid_low, "row"), axis=0)

    block_out = scatter_sum(rows_of(mm(act, w_down), rows), "row")
    block_out = unhalves((resid_mid + (block_out + down_b)).astype(BF16))

    def over_cols(matrix, axis):
        mine, other = jnp.split(matrix, 2, axis=axis)
        return (mine + swap(other.astype(BF16), "col", 1).astype(F32)).astype(BF16)

    down_grad = over_cols(mm_tn(act, g_all), 1)
    up_grad = over_cols(mm_tn(mlp_in, grad_pre), 0)
    out_grad = over_cols(mm_tn(attention.reshape(-1, width), mid_all), 1)
    out_grad = from_window(out_grad.T, *out_moves, row).T
    up_grad, down_grad, out_grad = [g.astype(F32) for g in lax.psum((up_grad, down_grad, out_grad), "dp")]

    dq, dkv_own, dkv_other = attend_backward(scal, queries, kv_own, kv_other, grad_att, lse.T, heads)
    dkv = (dkv_own + swap(dkv_other, "col", 1).astype(F32)).astype(BF16)
    grad_qkv = jnp.concatenate([dq, dkv], axis=2).reshape(-1, 3 * width)
    qkv_bias_part = jnp.sum(grad_qkv.astype(F32), axis=0)
    normed_part = mm_nt(grad_qkv, w_qkv)
    first_gain_part = jnp.sum(normed_part * normal1, axis=0)
    first_shift_part = jnp.sum(normed_part, axis=0)
    grad_normed1 = scatter_sum(rows_of(normed_part, rows), "row")
    back1 = norm_back(grad_normed1, normal1[:block], inverse1[:block], gain1)
    input_grad = unhalves(grad_mid + back1)

    qkv_grad = over_cols(mm_tn(normed1, grad_qkv), 0)
    qkv_grad = from_window(qkv_grad, *qkv_moves, row)
    qkv_grad = lax.psum(qkv_grad, "dp").astype(F32)

    def place(vector):
        mine, other = vector[:half], vector[half:]
        return jnp.concatenate([jnp.where(col == 0, mine, other), jnp.where(col == 0, other, mine)])

    def place_window(vector):
        padded = lax.dynamic_update_slice_in_dim(jnp.zeros((D + width,), F32), vector, head_at, 0)
        return padded[:D]

    def place_rows(vector):
        return lax.dynamic_update_slice_in_dim(jnp.zeros((FF,), F32), vector, row * vector.shape[0], 0)

    every = ("dp", "row", "col")
    early = lax.psum(
        jnp.concatenate(
            [
                place_rows(up_bias_part),
                place(down_bias_part),
                place(second_gain_part),
                place(second_shift_part),
                place(out_bias_part),
            ]
        ),
        every,
    )
    late = lax.psum(
        jnp.concatenate(
            [
                place(first_gain_part),
                place(first_shift_part),
                place_window(qkv_bias_part[:width]),
                place_window(qkv_bias_part[2 * width :]),
            ]
        ),
        every,
    )

    def own_half(vector, at):
        return lax.dynamic_slice_in_dim(vector, at + col * half, half)

    up_width = up_bias.shape[0]
    return (
        block_out,
        input_grad,
        own_half(late, 0),
        own_half(late, D),
        qkv_grad,
        late[2 * D : 3 * D],
        late[3 * D :],
        out_grad,
        own_half(early, FF + 3 * D),
        own_half(early, FF + D),
        own_half(early, FF + 2 * D),
        up_grad,
        lax.dynamic_slice_in_dim(early, row * up_width, up_width),
        down_grad,
        own_half(early, FF),
    )


def solution(mesh):
    in_specs = (
        P(("dp", "row"), "col"),
        P("dp", None),
        P("col"),
        P("col"),
        P("col", "row"),
        P(),
        P(),
        P("row", "col"),
        P("col"),
        P("col"),
        P("col"),
        P("col", "row"),
        P("row"),
        P("row", "col"),
        P("col"),
        P(("dp", "row"), "col"),
    )
    out_specs = (
        P(("dp", "row"), "col"),
        P(("dp", "row"), "col"),
        P("col"),
        P("col"),
        P("col", "row"),
        P(),
        P(),
        P("row", "col"),
        P("col"),
        P("col"),
        P("col"),
        P("col", "row"),
        P("row"),
        P("row", "col"),
        P("col"),
    )
    return jax.shard_map(
        on_device, mesh=mesh, in_specs=in_specs, out_specs=out_specs, check_vma=False
    )
```

```python
import functools

import jax
import jax.numpy as jnp
import numpy as np
from jax import lax
from jax.experimental import pallas as pl
from jax.experimental.pallas import tpu as pltpu
from jax.sharding import PartitionSpec as P

D = 1088
HEADS = 17
HEAD_DIM = 64
FF = 4352
TOK_G = 1024

EPSILON = 1e-05
MASKED = -1e30
CHUNK = 256
BF16 = jnp.bfloat16
F32 = jnp.float32


def swap(payload, axis, distance):
    size = lax.axis_size(axis)
    return lax.ppermute(payload, axis, [(i, i ^ distance) for i in range(size)])


def after(payload, *others):
    return lax.optimization_barrier((payload, *others))[0]


def gather_blocks(payload, axis):
    if lax.axis_size(axis) == 4 and axis == "row":
        far = swap(payload, axis, 2)
        near = swap(payload, axis, 1)
        return [payload, near, far, swap(far, axis, 1)]
    return [payload] + [swap(payload, axis, k) for k in range(1, lax.axis_size(axis))]


def send_blocks(blocks, axis):
    return [blocks[0]] + [swap(blocks[k], axis, k) for k in range(1, len(blocks))]


def scatter_sum(blocks, axis):
    if len(blocks) == 4 and axis == "row":
        relayed = swap(blocks[3].astype(BF16), axis, 1)
        far = swap((blocks[2] + relayed.astype(F32)).astype(BF16), axis, 2)
        near = swap(blocks[1].astype(BF16), axis, 1)
        return blocks[0] + near.astype(F32) + far.astype(F32)
    received = [swap(blocks[k].astype(BF16), axis, k) for k in range(1, len(blocks))]
    total = blocks[0]
    for item in received:
        total = total + item.astype(F32)
    return total


def sum_all(vector):
    for axis in ("row", "dp", "col"):
        distance = 1
        while distance < lax.axis_size(axis):
            vector = vector + swap(vector, axis, distance)
            distance *= 2
    return vector


def share_of(matrix, index, parts):
    size = matrix.shape[0] // parts
    return lax.dynamic_slice_in_dim(matrix, index * size, size, 0)


def by_index(blocks, index):
    size = blocks[0].shape[0]
    total = jnp.zeros((size * len(blocks),) + blocks[0].shape[1:], blocks[0].dtype)
    for k, item in enumerate(blocks):
        total = lax.dynamic_update_slice_in_dim(total, item, (index ^ k) * size, 0)
    return total


def rows_of(matrix, parts):
    size = matrix.shape[0] // parts
    return [matrix[k * size : (k + 1) * size] for k in range(parts)]


def head_starts(rows):
    return [int(np.floor(HEADS * r / rows + 0.5)) for r in range(rows + 1)]


def most_heads(rows):
    starts = head_starts(rows)
    return max(b - a for a, b in zip(starts[:-1], starts[1:]))


def window_columns(rows, copies):
    starts = head_starts(rows)
    width = most_heads(rows) * HEAD_DIM
    table = np.full((rows, copies * width), -1, np.int64)
    for r in range(rows):
        count = (starts[r + 1] - starts[r]) * HEAD_DIM
        for t in range(copies):
            table[r, t * width : t * width + count] = t * D + starts[r] * HEAD_DIM + np.arange(count)
    return table


def move_tables(rows, parts):
    moves = []
    for k in range(rows):
        places = [[] for _ in range(rows)]
        columns = [[] for _ in range(rows)]
        for copies, place_at, column_at in parts:
            windows = window_columns(rows, copies)
            shard = copies * D // rows
            for r in range(rows):
                for p in range(windows.shape[1]):
                    if windows[r, p] >= 0 and windows[r, p] // shard == r ^ k:
                        places[r].append(place_at + p)
                        columns[r].append(column_at + int(windows[r, p] % shard))
        longest = -(-max(len(place) for place in places) // 16) * 16
        at = np.full((rows, longest), -1, np.int32)
        frm = np.full((rows, longest), -1, np.int32)
        for r in range(rows):
            at[r, : len(places[r])] = places[r]
            frm[r ^ k, : len(columns[r])] = columns[r]
        moves.append((at, frm))
    return moves


def table_row(table, index):
    return lax.dynamic_index_in_dim(jnp.asarray(table), index, 0, keepdims=True)


def one_hot(places, size):
    return (lax.broadcasted_iota(jnp.int32, (size, places.shape[1]), 0) == places).astype(BF16)


def move_columns(matrix, from_tables, to_tables, width, row):
    counts = [table.shape[1] for table in from_tables]
    picked = mm(matrix, one_hot(table_row(np.concatenate(from_tables, 1), row), matrix.shape[1])).astype(BF16)
    slabs, at = [], 0
    for k, count in enumerate(counts):
        slab = picked[:, at : at + count]
        at += count
        if count:
            slabs.append(swap(slab, "row", k) if k else slab)
    return mm_nt(jnp.concatenate(slabs, axis=1), one_hot(table_row(np.concatenate(to_tables, 1), row), width)).astype(BF16)


def mm(a, b):
    return jnp.dot(a, b, preferred_element_type=F32)


def mm_nt(a, b):
    return lax.dot_general(a, b, (((1,), (1,)), ((), ())), preferred_element_type=F32)


def mm_tn(a, b):
    return lax.dot_general(a, b, (((0,), (0,)), ((), ())), preferred_element_type=F32)


def positions(start, shape, dim, block, col):
    at = lax.broadcasted_iota(jnp.int32, shape, dim) + start
    shift = block.bit_length() - 1
    return lax.shift_left(lax.shift_right_logical(at, shift), shift + 1) + (at & (block - 1)) + col * block


def segments(pos, scal_ref):
    first = scal_ref[2]
    return (pos >= first).astype(jnp.int32) + (pos >= first + scal_ref[3]).astype(jnp.int32)


def mask_bias(scal_ref, query_at, query_shape, query_dim, key_shape, key_dim, block, key_col):
    query_pos = positions(query_at, query_shape, query_dim, block, scal_ref[1])
    key_pos = positions(0, key_shape, key_dim, block, key_col)
    allowed = (key_pos <= query_pos) & (segments(key_pos, scal_ref) == segments(query_pos, scal_ref))
    return jnp.where(allowed, 0.0, MASKED)


def in_order(source_ref, target_ref, row, blocks, block):
    for j in range(blocks):
        target_ref[j * block : (j + 1) * block, :] = source_ref[j ^ row]


def forward_kernel(blocks, block, heads, scal_ref, q_ref, kv0_ref, kv1_ref, out_ref, lse_ref, q_s, kv0_s, kv1_s, o_s):
    row = scal_ref[0]
    width = heads * HEAD_DIM
    in_order(q_ref, q_s, row, blocks, block)
    in_order(kv0_ref, kv0_s, row, blocks, block)
    in_order(kv1_ref, kv1_s, row, blocks, block)
    own = scal_ref[1]
    for i in range(blocks * block // CHUNK):
        span = slice(i * CHUNK, (i + 1) * CHUNK)
        keys = (i + 1) * CHUNK
        shape = (CHUNK, keys)
        bias0 = mask_bias(scal_ref, i * CHUNK, (CHUNK, 1), 0, (1, keys), 1, block, own)
        bias1 = mask_bias(scal_ref, i * CHUNK, (CHUNK, 1), 0, (1, keys), 1, block, 1 - own)
        for h in range(heads):
            at = slice(h * HEAD_DIM, (h + 1) * HEAD_DIM)
            va = slice(width + h * HEAD_DIM, width + (h + 1) * HEAD_DIM)
            query = q_s[span, at]
            s0 = mm_nt(query, kv0_s[:keys, at]) + bias0
            s1 = mm_nt(query, kv1_s[:keys, at]) + bias1
            top = jnp.maximum(jnp.max(s0, axis=1, keepdims=True), jnp.max(s1, axis=1, keepdims=True))
            e0 = jnp.exp(s0 - top)
            e1 = jnp.exp(s1 - top)
            total = jnp.sum(e0, axis=1, keepdims=True) + jnp.sum(e1, axis=1, keepdims=True)
            result = mm(e0.astype(BF16), kv0_s[:keys, va]) + mm(e1.astype(BF16), kv1_s[:keys, va])
            o_s[span, at] = (result / total).astype(BF16)
            lse_ref[span, h : h + 1] = top + jnp.log(total)
    for j in range(blocks):
        out_ref[j ^ row] = o_s[j * block : (j + 1) * block, :]


def backward_kernel(
    blocks,
    block,
    heads,
    scal_ref,
    q_ref,
    kv0_ref,
    kv1_ref,
    g_ref,
    lse_ref,
    dq_ref,
    own_ref,
    other_ref,
    q_s,
    kv0_s,
    kv1_s,
    g_s,
    dq_s,
    d0_s,
    d1_s,
):
    row = scal_ref[0]
    width = heads * HEAD_DIM
    in_order(q_ref, q_s, row, blocks, block)
    in_order(kv0_ref, kv0_s, row, blocks, block)
    in_order(kv1_ref, kv1_s, row, blocks, block)
    in_order(g_ref, g_s, row, blocks, block)
    own = scal_ref[1]
    chunks = blocks * block // CHUNK
    for i in reversed(range(chunks)):
        span = slice(i * CHUNK, (i + 1) * CHUNK)
        keys = (i + 1) * CHUNK
        bias0 = mask_bias(scal_ref, i * CHUNK, (1, CHUNK), 1, (keys, 1), 0, block, own)
        bias1 = mask_bias(scal_ref, i * CHUNK, (1, CHUNK), 1, (keys, 1), 0, block, 1 - own)
        for h in range(heads):
            at = slice(h * HEAD_DIM, (h + 1) * HEAD_DIM)
            va = slice(width + h * HEAD_DIM, width + (h + 1) * HEAD_DIM)
            query = q_s[span, at]
            grad = g_s[span, at]
            lse = lse_ref[h : h + 1, span]
            p0 = jnp.exp(mm_nt(kv0_s[:keys, at], query) + bias0 - lse)
            p1 = jnp.exp(mm_nt(kv1_s[:keys, at], query) + bias1 - lse)
            dp0 = mm_nt(kv0_s[:keys, va], grad)
            dp1 = mm_nt(kv1_s[:keys, va], grad)
            delta = jnp.sum(p0 * dp0, axis=0, keepdims=True) + jnp.sum(p1 * dp1, axis=0, keepdims=True)
            ds0 = (p0 * (dp0 - delta)).astype(BF16)
            ds1 = (p1 * (dp1 - delta)).astype(BF16)
            if i == chunks - 1:
                d0_s[:keys, at] = mm(ds0, query)
                d1_s[:keys, at] = mm(ds1, query)
                d0_s[:keys, va] = mm(p0.astype(BF16), grad)
                d1_s[:keys, va] = mm(p1.astype(BF16), grad)
            else:
                d0_s[:keys, at] += mm(ds0, query)
                d1_s[:keys, at] += mm(ds1, query)
                d0_s[:keys, va] += mm(p0.astype(BF16), grad)
                d1_s[:keys, va] += mm(p1.astype(BF16), grad)
            dquery = mm_tn(ds0, kv0_s[:keys, at]) + mm_tn(ds1, kv1_s[:keys, at])
            dq_s[span, at] = (dquery * HEAD_DIM ** (-0.5)).astype(BF16)
    for j in range(blocks):
        piece = slice(j * block, (j + 1) * block)
        dq_ref[j ^ row] = dq_s[piece, :]
        own_ref[j ^ row] = d0_s[piece, :]
        other_ref[j ^ row] = d1_s[piece, :].astype(BF16)


def vmem():
    return pl.BlockSpec(memory_space=pltpu.VMEM)


def smem():
    return pl.BlockSpec(memory_space=pltpu.SMEM)


def attend_forward(scal, queries, kv_own, kv_other, heads):
    blocks, block, width = queries.shape
    tokens = blocks * block
    return pl.pallas_call(
        functools.partial(forward_kernel, blocks, block, heads),
        out_shape=(
            jax.ShapeDtypeStruct((blocks, block, width), BF16),
            jax.ShapeDtypeStruct((tokens, heads), F32),
        ),
        in_specs=[smem(), vmem(), vmem(), vmem()],
        out_specs=(vmem(), vmem()),
        scratch_shapes=[
            pltpu.VMEM((tokens, width), BF16),
            pltpu.VMEM((tokens, 2 * width), BF16),
            pltpu.VMEM((tokens, 2 * width), BF16),
            pltpu.VMEM((tokens, width), BF16),
        ],
        compiler_params=pltpu.CompilerParams(vmem_limit_bytes=40 * 2**20),
        cost_estimate=pl.CostEstimate(
            flops=4 * tokens * 3 * tokens // 2 * width, bytes_accessed=6 * tokens * width * 2, transcendentals=heads * tokens * tokens
        ),
        name="attend_forward",
    )(scal, queries, kv_own, kv_other)


def attend_backward(scal, queries, kv_own, kv_other, grads, lse, heads):
    blocks, block, width = queries.shape
    tokens = blocks * block
    return pl.pallas_call(
        functools.partial(backward_kernel, blocks, block, heads),
        out_shape=(
            jax.ShapeDtypeStruct((blocks, block, width), BF16),
            jax.ShapeDtypeStruct((blocks, block, 2 * width), F32),
            jax.ShapeDtypeStruct((blocks, block, 2 * width), BF16),
        ),
        in_specs=[smem(), vmem(), vmem(), vmem(), vmem(), vmem()],
        out_specs=(vmem(), vmem(), vmem()),
        scratch_shapes=[
            pltpu.VMEM((tokens, width), BF16),
            pltpu.VMEM((tokens, 2 * width), BF16),
            pltpu.VMEM((tokens, 2 * width), BF16),
            pltpu.VMEM((tokens, width), BF16),
            pltpu.VMEM((tokens, width), BF16),
            pltpu.VMEM((tokens, 2 * width), F32),
            pltpu.VMEM((tokens, 2 * width), F32),
        ],
        compiler_params=pltpu.CompilerParams(vmem_limit_bytes=44 * 2**20),
        cost_estimate=pl.CostEstimate(
            flops=10 * tokens * 3 * tokens // 2 * width, bytes_accessed=14 * tokens * width * 2, transcendentals=heads * tokens * tokens
        ),
        name="attend_backward",
    )(scal, queries, kv_own, kv_other, grads, lse)


def norm_parts(resid_in):
    mean_value = jnp.sum(resid_in, axis=1, keepdims=True) / D
    square = jnp.sum(resid_in * resid_in, axis=1, keepdims=True) / D
    inverse = lax.rsqrt(square - mean_value * mean_value + EPSILON)
    return ((resid_in - mean_value) * inverse, inverse)


def norm_back(grad_in, normal, inverse, norm_gain):
    scaled = grad_in * norm_gain
    mean_scaled = jnp.sum(scaled, axis=1, keepdims=True) / D
    mean_cross = jnp.sum(scaled * normal, axis=1, keepdims=True) / D
    return inverse * (scaled - mean_scaled - normal * mean_cross)


def gelu_tanh(pre_value):
    return jax.nn.gelu(pre_value, approximate=True)


def on_device(
    tokens,
    lengths,
    first_gain,
    first_shift,
    qkv_weight,
    query_bias,
    value_bias,
    out_weight,
    out_bias,
    second_gain,
    second_shift,
    up_weight,
    up_bias,
    down_weight,
    down_bias,
    cotangent,
):
    rows = lax.axis_size("row")
    row = lax.axis_index("row")
    col = lax.axis_index("col")
    half = tokens.shape[1]
    block = tokens.shape[0] // 2
    heads = most_heads(rows)
    width = heads * HEAD_DIM

    def halves(matrix):
        pair = matrix.reshape(2, block, half)
        mine = lax.dynamic_index_in_dim(pair, col, 0, keepdims=False)
        other = lax.dynamic_index_in_dim(pair, 1 - col, 0, keepdims=False)
        return jnp.concatenate([mine, swap(other, "col", 1)], axis=1)

    def unhalves(matrix):
        mine = matrix[:, :half]
        other = swap(matrix[:, half:], "col", 1)
        return jnp.concatenate([jnp.where(col == 0, mine, other), jnp.where(col == 0, other, mine)], axis=0)

    dps = lax.axis_size("dp")
    dp = lax.axis_index("dp")

    x_own = halves(tokens)
    x_all = jnp.concatenate(gather_blocks(x_own, "row"), axis=0).astype(F32)

    vectors = after(jnp.stack([first_gain, first_shift, out_bias, second_gain, second_shift, down_bias]), x_own)
    vectors = jnp.concatenate([vectors, swap(vectors, "col", 1)], axis=1)
    gain1, shift1, out_b, gain2, shift2, down_b = [vectors[i] for i in range(6)]

    qkv_moves = move_tables(rows, [(3, 0, 0)])
    share = share_of(qkv_weight, dp, dps)
    share = move_columns(after(share, x_own), [m[1] for m in qkv_moves], [m[0] for m in qkv_moves], 3 * width, row)
    qkv_head = by_index(gather_blocks(share, "dp"), dp)
    w_qkv = jnp.concatenate([qkv_head, swap(qkv_head, "col", 1)], axis=0)

    out_share = after(share_of(out_weight.T, dp, dps), share)
    out_share = jnp.concatenate(gather_blocks(out_share, "row"), axis=1)
    windows = window_columns(rows, 1)
    out_shard = D // rows
    relative = np.full((rows, rows * width), -1, np.int32)
    for r in range(rows):
        for k in range(rows):
            held = windows[r ^ k]
            relative[r, k * width : (k + 1) * width] = np.where(held >= 0, ((held // out_shard) ^ r) * out_shard + held % out_shard, -1)
    out_share = mm(out_share, one_hot(table_row(relative, row), D)).astype(BF16)
    out_head = by_index(gather_blocks(out_share, "dp"), dp)
    w_out = jnp.concatenate([out_head, swap(out_head, "col", 1)], axis=0)

    starts = jnp.asarray(np.array(head_starts(rows), np.int32))
    head_at = starts[row] * HEAD_DIM
    live_cols = jnp.arange(width, dtype=jnp.int32) < (starts[row + 1] - starts[row]) * HEAD_DIM

    def bias_window(vector):
        padded = jnp.concatenate([vector, jnp.zeros((width,), F32)])
        return jnp.where(live_cols, lax.dynamic_slice_in_dim(padded, head_at, width), 0.0)

    normal1, inverse1 = norm_parts(x_all)
    normed1 = (normal1 * gain1 + shift1).astype(BF16)
    kv_own = mm(normed1, w_qkv[:, width:])
    bias_kv = jnp.concatenate([jnp.zeros((width,), F32), bias_window(value_bias)])
    kv_own = (kv_own + bias_kv).astype(BF16)
    kv_other = swap(kv_own, "col", 1)
    queries = mm(normed1, w_qkv[:, :width])
    queries = (queries + bias_window(query_bias)).astype(BF16) * BF16(HEAD_DIM ** (-0.5))
    queries = queries.reshape(rows, block, width)
    kv_own = kv_own.reshape(rows, block, 2 * width)
    kv_other = kv_other.reshape(rows, block, 2 * width)
    scal = jnp.stack([row.astype(jnp.int32), col.astype(jnp.int32), lengths[0, 0], lengths[0, 1]])

    cot_own = halves(after(cotangent, x_all))
    own_pos = (row * 2 + col) * block + jnp.arange(block, dtype=jnp.int32)
    live = own_pos < lengths[0, 0] + lengths[0, 1]
    grad_out = jnp.where(live[:, None], cot_own, 0.0)
    grad_out_low = after(grad_out.astype(BF16), normed1)
    g_blocks = gather_blocks(grad_out_low, "row")

    attention, lse = attend_forward(scal, queries, kv_own, kv_other, heads)

    att_own = jnp.concatenate(send_blocks([attention[k] for k in range(rows)], "row"), axis=1)
    resid_mid = x_own.astype(F32) + (mm_nt(att_own, w_out) + out_b)

    normal2, inverse2 = norm_parts(resid_mid)
    normed2 = (normal2 * gain2 + shift2).astype(BF16)
    mlp_in = jnp.concatenate(gather_blocks(normed2, "row"), axis=0)
    w_up = jnp.concatenate([up_weight, swap(after(up_weight, x_all), "col", 1)], axis=0)
    w_down = jnp.concatenate([down_weight, swap(after(down_weight, normed1), "col", 1)], axis=1)
    g_all = jnp.concatenate(g_blocks, axis=0)
    down_bias_part = jnp.sum(grad_out_low.astype(F32), axis=0)

    pre_act = mm(mlp_in, w_up) + up_bias
    act, gelu_back = jax.vjp(gelu_tanh, pre_act)
    act = act.astype(BF16)
    grad_act = mm_nt(g_all, w_down)
    grad_pre = gelu_back(grad_act)[0].astype(BF16)
    up_bias_part = jnp.sum(grad_pre.astype(F32), axis=0)
    grad_normed2 = scatter_sum(rows_of(mm_nt(grad_pre, w_up), rows), "row")
    second_gain_part = jnp.sum(grad_normed2 * normal2, axis=0)
    second_shift_part = jnp.sum(grad_normed2, axis=0)
    grad_mid = grad_out + norm_back(grad_normed2, normal2, inverse2, gain2)
    grad_mid_low = grad_mid.astype(BF16)
    out_bias_part = jnp.sum(grad_mid_low.astype(F32), axis=0)

    grad_att = mm(grad_mid_low, w_out).astype(BF16)
    grad_att = jnp.stack(send_blocks([grad_att[:, k * width : (k + 1) * width] for k in range(rows)], "row"))
    mid_all = jnp.concatenate(gather_blocks(after(grad_mid_low, grad_att), "row"), axis=0)

    def over_cols(matrix):
        return (matrix[:half] + swap(matrix[half:].astype(BF16), "col", 1).astype(F32)).astype(BF16)

    down_grad = over_cols(mm_tn(g_all, act))
    up_grad = over_cols(mm_tn(mlp_in, grad_pre))
    up_grad, down_grad = lax.psum((up_grad, down_grad), "dp")

    dq, dkv_own, dkv_other = attend_backward(scal, queries, kv_own, kv_other, grad_att, lse.T, heads)
    dkv = (dkv_own + swap(dkv_other, "col", 1).astype(F32)).astype(BF16)
    grad_qkv = jnp.concatenate([dq, dkv], axis=2).reshape(-1, 3 * width)
    qkv_bias_part = jnp.sum(grad_qkv.astype(F32), axis=0)
    normed_part = mm_nt(grad_qkv, w_qkv)
    first_gain_part = jnp.sum(normed_part * normal1, axis=0)
    first_shift_part = jnp.sum(normed_part, axis=0)
    grad_normed1 = scatter_sum(rows_of(normed_part, rows), "row")
    back1 = norm_back(grad_normed1, normal1[:block], inverse1[:block], gain1)
    input_grad = unhalves(grad_mid + back1)

    out_grad = mm_tn(mid_all, attention.reshape(-1, width))
    qkv_grad = mm_tn(normed1, after(grad_qkv, normed_part))
    both = over_cols(jnp.concatenate([qkv_grad, out_grad], axis=1))
    shares = [share_of(both, dp ^ k, dps) for k in range(dps)]
    both = scatter_sum([shares[0].astype(F32)] + shares[1:], "dp").astype(BF16)
    both_moves = move_tables(rows, [(3, 0, 0), (1, 3 * width, 3 * out_shard)])
    both = move_columns(both, [m[0] for m in both_moves], [m[1] for m in both_moves], 4 * out_shard, row)
    both = by_index(gather_blocks(both, "dp"), dp)
    qkv_grad = both[:, : 3 * out_shard].astype(F32)
    out_grad = both[:, 3 * out_shard :].T.astype(F32)

    down_out = mm(act, w_down)
    block_out = scatter_sum(rows_of(after(down_out, grad_normed1), rows), "row")
    block_out = unhalves((resid_mid + (block_out + down_b)).astype(BF16))

    def place(vector):
        mine, other = vector[:half], vector[half:]
        return jnp.concatenate([jnp.where(col == 0, mine, other), jnp.where(col == 0, other, mine)])

    def place_window(vector):
        padded = lax.dynamic_update_slice_in_dim(jnp.zeros((D + width,), F32), vector, head_at, 0)
        return padded[:D]

    def place_rows(vector):
        return lax.dynamic_update_slice_in_dim(jnp.zeros((FF,), F32), vector, row * vector.shape[0], 0)

    small = sum_all(
        jnp.concatenate(
            [
                place_rows(up_bias_part),
                place(down_bias_part),
                place(second_gain_part),
                place(second_shift_part),
                place(out_bias_part),
                place(first_gain_part),
                place(first_shift_part),
                place_window(qkv_bias_part[:width]),
                place_window(qkv_bias_part[2 * width :]),
            ]
        )
    )

    def own_half(part):
        return lax.dynamic_slice_in_dim(small, FF + part * D + col * half, half)

    up_width = up_bias.shape[0]
    return (
        block_out,
        input_grad,
        own_half(4),
        own_half(5),
        qkv_grad,
        small[FF + 6 * D : FF + 7 * D],
        small[FF + 7 * D :],
        out_grad,
        own_half(3),
        own_half(1),
        own_half(2),
        up_grad.astype(F32),
        lax.dynamic_slice_in_dim(small, row * up_width, up_width),
        down_grad.T.astype(F32),
        own_half(0),
    )


def solution(mesh):
    in_specs = (
        P(("dp", "row"), "col"),
        P("dp", None),
        P("col"),
        P("col"),
        P("col", "row"),
        P(),
        P(),
        P("row", "col"),
        P("col"),
        P("col"),
        P("col"),
        P("col", "row"),
        P("row"),
        P("row", "col"),
        P("col"),
        P(("dp", "row"), "col"),
    )
    out_specs = (
        P(("dp", "row"), "col"),
        P(("dp", "row"), "col"),
        P("col"),
        P("col"),
        P("col", "row"),
        P(),
        P(),
        P("row", "col"),
        P("col"),
        P("col"),
        P("col"),
        P("col", "row"),
        P("row"),
        P("row", "col"),
        P("col"),
    )
    return jax.shard_map(
        on_device, mesh=mesh, in_specs=in_specs, out_specs=out_specs, check_vma=False
    )
```

```python
import functools

import jax
import jax.numpy as jnp
import numpy as np
from jax import lax
from jax.experimental import pallas as pl
from jax.experimental.pallas import tpu as pltpu
from jax.sharding import PartitionSpec as P

D = 1088
HEADS = 17
HEAD_DIM = 64
FF = 4352
TOK_G = 1024

EPSILON = 1e-05
MASKED = -1e30
CHUNK = 256
BF16 = jnp.bfloat16
F32 = jnp.float32


def swap(payload, axis, distance):
    size = lax.axis_size(axis)
    return lax.ppermute(payload, axis, [(i, i ^ distance) for i in range(size)])


def after(payload, *others):
    return lax.optimization_barrier((payload, *others))[0]


def gather_blocks(payload, axis):
    if lax.axis_size(axis) == 4 and axis == "row":
        far = swap(payload, axis, 2)
        near = swap(payload, axis, 1)
        return [payload, near, far, swap(far, axis, 1)]
    return [payload] + [swap(payload, axis, k) for k in range(1, lax.axis_size(axis))]


def send_blocks(blocks, axis):
    return [blocks[0]] + [swap(blocks[k], axis, k) for k in range(1, len(blocks))]


def scatter_sum(blocks, axis):
    received = [swap(blocks[k].astype(BF16), axis, k) for k in range(1, len(blocks))]
    total = blocks[0]
    for item in received:
        total = total + item.astype(F32)
    return total


def sum_all(vector):
    for axis in ("row", "dp", "col"):
        distance = 1
        while distance < lax.axis_size(axis):
            vector = vector + swap(vector, axis, distance)
            distance *= 2
    return vector


def share_of(matrix, index, parts):
    size = matrix.shape[0] // parts
    return lax.dynamic_slice_in_dim(matrix, index * size, size, 0)


def by_index(blocks, index):
    count = len(blocks)
    total = jnp.zeros((count,) + blocks[0].shape, blocks[0].dtype)
    for k, item in enumerate(blocks):
        total = lax.dynamic_update_index_in_dim(total, item, index ^ k, 0)
    return total.reshape((count * blocks[0].shape[0],) + blocks[0].shape[1:])


def rows_of(matrix, parts):
    size = matrix.shape[0] // parts
    return [matrix[k * size : (k + 1) * size] for k in range(parts)]


def head_starts(rows):
    return [int(np.floor(HEADS * r / rows + 0.5)) for r in range(rows + 1)]


def most_heads(rows):
    starts = head_starts(rows)
    return max(b - a for a, b in zip(starts[:-1], starts[1:]))


def window_columns(rows, copies):
    starts = head_starts(rows)
    width = most_heads(rows) * HEAD_DIM
    table = np.full((rows, copies * width), -1, np.int64)
    for r in range(rows):
        count = (starts[r + 1] - starts[r]) * HEAD_DIM
        for t in range(copies):
            table[r, t * width : t * width + count] = t * D + starts[r] * HEAD_DIM + np.arange(count)
    return table


def move_tables(rows, parts):
    moves = []
    for k in range(rows):
        places = [[] for _ in range(rows)]
        columns = [[] for _ in range(rows)]
        for copies, place_at, column_at in parts:
            windows = window_columns(rows, copies)
            shard = copies * D // rows
            for r in range(rows):
                for p in range(windows.shape[1]):
                    if windows[r, p] >= 0 and windows[r, p] // shard == r ^ k:
                        places[r].append(place_at + p)
                        columns[r].append(column_at + int(windows[r, p] % shard))
        longest = -(-max(len(place) for place in places) // 16) * 16
        at = np.full((rows, longest), -1, np.int32)
        frm = np.full((rows, longest), -1, np.int32)
        for r in range(rows):
            at[r, : len(places[r])] = places[r]
            frm[r ^ k, : len(columns[r])] = columns[r]
        moves.append((at, frm))
    return moves


def table_row(table, index):
    return lax.dynamic_index_in_dim(jnp.asarray(table), index, 0, keepdims=True)


def one_hot(places, size):
    return (lax.broadcasted_iota(jnp.int32, (size, places.shape[1]), 0) == places).astype(BF16)


def move_columns(matrix, from_tables, to_tables, width, row):
    counts = [table.shape[1] for table in from_tables]
    picked = mm(matrix, one_hot(table_row(np.concatenate(from_tables, 1), row), matrix.shape[1])).astype(BF16)
    slabs, at = [], 0
    for k, count in enumerate(counts):
        slab = picked[:, at : at + count]
        at += count
        if count:
            slabs.append(swap(slab, "row", k) if k else slab)
    return mm_nt(jnp.concatenate(slabs, axis=1), one_hot(table_row(np.concatenate(to_tables, 1), row), width)).astype(BF16)


def mm(a, b):
    return jnp.dot(a, b, preferred_element_type=F32)


def mm_nt(a, b):
    return lax.dot_general(a, b, (((1,), (1,)), ((), ())), preferred_element_type=F32)


def mm_tn(a, b):
    return lax.dot_general(a, b, (((0,), (0,)), ((), ())), preferred_element_type=F32)


def positions(start, shape, dim, block, col):
    at = lax.broadcasted_iota(jnp.int32, shape, dim) + start
    shift = block.bit_length() - 1
    return lax.shift_left(lax.shift_right_logical(at, shift), shift + 1) + (at & (block - 1)) + col * block


def segments(pos, scal_ref):
    first = scal_ref[2]
    return (pos >= first).astype(jnp.int32) + (pos >= first + scal_ref[3]).astype(jnp.int32)


def mask_bias(scal_ref, query_at, query_shape, query_dim, key_shape, key_dim, block, key_col):
    query_pos = positions(query_at, query_shape, query_dim, block, scal_ref[1])
    key_pos = positions(0, key_shape, key_dim, block, key_col)
    allowed = (key_pos <= query_pos) & (segments(key_pos, scal_ref) == segments(query_pos, scal_ref))
    return jnp.where(allowed, 0.0, MASKED)


def in_order(source_ref, target_ref, row, blocks, block):
    for j in range(blocks):
        target_ref[j * block : (j + 1) * block, :] = source_ref[j ^ row]


def forward_kernel(blocks, block, heads, scal_ref, q_ref, kv0_ref, kv1_ref, out_ref, lse_ref, q_s, kv0_s, kv1_s, o_s):
    row = scal_ref[0]
    width = heads * HEAD_DIM
    in_order(q_ref, q_s, row, blocks, block)
    in_order(kv0_ref, kv0_s, row, blocks, block)
    in_order(kv1_ref, kv1_s, row, blocks, block)
    own = scal_ref[1]
    for i in range(blocks * block // CHUNK):
        span = slice(i * CHUNK, (i + 1) * CHUNK)
        keys = (i + 1) * CHUNK
        shape = (CHUNK, keys)
        bias0 = mask_bias(scal_ref, i * CHUNK, (CHUNK, 1), 0, (1, keys), 1, block, own)
        bias1 = mask_bias(scal_ref, i * CHUNK, (CHUNK, 1), 0, (1, keys), 1, block, 1 - own)
        for h in range(heads):
            at = slice(h * HEAD_DIM, (h + 1) * HEAD_DIM)
            va = slice(width + h * HEAD_DIM, width + (h + 1) * HEAD_DIM)
            query = q_s[span, at]
            s0 = mm_nt(query, kv0_s[:keys, at]) + bias0
            s1 = mm_nt(query, kv1_s[:keys, at]) + bias1
            top = jnp.maximum(jnp.max(s0, axis=1, keepdims=True), jnp.max(s1, axis=1, keepdims=True))
            e0 = jnp.exp(s0 - top)
            e1 = jnp.exp(s1 - top)
            total = jnp.sum(e0, axis=1, keepdims=True) + jnp.sum(e1, axis=1, keepdims=True)
            result = mm(e0.astype(BF16), kv0_s[:keys, va]) + mm(e1.astype(BF16), kv1_s[:keys, va])
            o_s[span, at] = (result / total).astype(BF16)
            lse_ref[span, h : h + 1] = top + jnp.log(total)
    for j in range(blocks):
        out_ref[j ^ row] = o_s[j * block : (j + 1) * block, :]


def backward_kernel(
    blocks,
    block,
    heads,
    scal_ref,
    q_ref,
    kv0_ref,
    kv1_ref,
    g_ref,
    lse_ref,
    dq_ref,
    own_ref,
    other_ref,
    q_s,
    kv0_s,
    kv1_s,
    g_s,
    dq_s,
    d0_s,
    d1_s,
):
    row = scal_ref[0]
    width = heads * HEAD_DIM
    in_order(q_ref, q_s, row, blocks, block)
    in_order(kv0_ref, kv0_s, row, blocks, block)
    in_order(kv1_ref, kv1_s, row, blocks, block)
    in_order(g_ref, g_s, row, blocks, block)
    own = scal_ref[1]
    chunks = blocks * block // CHUNK
    for i in reversed(range(chunks)):
        span = slice(i * CHUNK, (i + 1) * CHUNK)
        keys = (i + 1) * CHUNK
        bias0 = mask_bias(scal_ref, i * CHUNK, (1, CHUNK), 1, (keys, 1), 0, block, own)
        bias1 = mask_bias(scal_ref, i * CHUNK, (1, CHUNK), 1, (keys, 1), 0, block, 1 - own)
        for h in range(heads):
            at = slice(h * HEAD_DIM, (h + 1) * HEAD_DIM)
            va = slice(width + h * HEAD_DIM, width + (h + 1) * HEAD_DIM)
            query = q_s[span, at]
            grad = g_s[span, at]
            lse = lse_ref[h : h + 1, span]
            p0 = jnp.exp(mm_nt(kv0_s[:keys, at], query) + bias0 - lse)
            p1 = jnp.exp(mm_nt(kv1_s[:keys, at], query) + bias1 - lse)
            dp0 = mm_nt(kv0_s[:keys, va], grad)
            dp1 = mm_nt(kv1_s[:keys, va], grad)
            delta = jnp.sum(p0 * dp0, axis=0, keepdims=True) + jnp.sum(p1 * dp1, axis=0, keepdims=True)
            ds0 = (p0 * (dp0 - delta)).astype(BF16)
            ds1 = (p1 * (dp1 - delta)).astype(BF16)
            if i == chunks - 1:
                d0_s[:keys, at] = mm(ds0, query)
                d1_s[:keys, at] = mm(ds1, query)
                d0_s[:keys, va] = mm(p0.astype(BF16), grad)
                d1_s[:keys, va] = mm(p1.astype(BF16), grad)
            else:
                d0_s[:keys, at] += mm(ds0, query)
                d1_s[:keys, at] += mm(ds1, query)
                d0_s[:keys, va] += mm(p0.astype(BF16), grad)
                d1_s[:keys, va] += mm(p1.astype(BF16), grad)
            dquery = mm_tn(ds0, kv0_s[:keys, at]) + mm_tn(ds1, kv1_s[:keys, at])
            dq_s[span, at] = (dquery * HEAD_DIM ** (-0.5)).astype(BF16)
    for j in range(blocks):
        piece = slice(j * block, (j + 1) * block)
        dq_ref[j ^ row] = dq_s[piece, :]
        own_ref[j ^ row] = d0_s[piece, :]
        other_ref[j ^ row] = d1_s[piece, :].astype(BF16)


def vmem():
    return pl.BlockSpec(memory_space=pltpu.VMEM)


def smem():
    return pl.BlockSpec(memory_space=pltpu.SMEM)


def attend_forward(scal, queries, kv_own, kv_other, heads):
    blocks, block, width = queries.shape
    tokens = blocks * block
    return pl.pallas_call(
        functools.partial(forward_kernel, blocks, block, heads),
        out_shape=(
            jax.ShapeDtypeStruct((blocks, block, width), BF16),
            jax.ShapeDtypeStruct((tokens, heads), F32),
        ),
        in_specs=[smem(), vmem(), vmem(), vmem()],
        out_specs=(vmem(), vmem()),
        scratch_shapes=[
            pltpu.VMEM((tokens, width), BF16),
            pltpu.VMEM((tokens, 2 * width), BF16),
            pltpu.VMEM((tokens, 2 * width), BF16),
            pltpu.VMEM((tokens, width), BF16),
        ],
        compiler_params=pltpu.CompilerParams(vmem_limit_bytes=40 * 2**20),
        cost_estimate=pl.CostEstimate(
            flops=4 * tokens * 3 * tokens // 2 * width, bytes_accessed=6 * tokens * width * 2, transcendentals=heads * tokens * tokens
        ),
        name="attend_forward",
    )(scal, queries, kv_own, kv_other)


def attend_backward(scal, queries, kv_own, kv_other, grads, lse, heads):
    blocks, block, width = queries.shape
    tokens = blocks * block
    return pl.pallas_call(
        functools.partial(backward_kernel, blocks, block, heads),
        out_shape=(
            jax.ShapeDtypeStruct((blocks, block, width), BF16),
            jax.ShapeDtypeStruct((blocks, block, 2 * width), F32),
            jax.ShapeDtypeStruct((blocks, block, 2 * width), BF16),
        ),
        in_specs=[smem(), vmem(), vmem(), vmem(), vmem(), vmem()],
        out_specs=(vmem(), vmem(), vmem()),
        scratch_shapes=[
            pltpu.VMEM((tokens, width), BF16),
            pltpu.VMEM((tokens, 2 * width), BF16),
            pltpu.VMEM((tokens, 2 * width), BF16),
            pltpu.VMEM((tokens, width), BF16),
            pltpu.VMEM((tokens, width), BF16),
            pltpu.VMEM((tokens, 2 * width), F32),
            pltpu.VMEM((tokens, 2 * width), F32),
        ],
        compiler_params=pltpu.CompilerParams(vmem_limit_bytes=44 * 2**20),
        cost_estimate=pl.CostEstimate(
            flops=10 * tokens * 3 * tokens // 2 * width, bytes_accessed=14 * tokens * width * 2, transcendentals=heads * tokens * tokens
        ),
        name="attend_backward",
    )(scal, queries, kv_own, kv_other, grads, lse)


def norm_parts(resid_in):
    mean_value = jnp.sum(resid_in, axis=1, keepdims=True) / D
    square = jnp.sum(resid_in * resid_in, axis=1, keepdims=True) / D
    inverse = lax.rsqrt(square - mean_value * mean_value + EPSILON)
    return ((resid_in - mean_value) * inverse, inverse)


def norm_back(grad_in, normal, inverse, norm_gain):
    scaled = grad_in * norm_gain
    mean_scaled = jnp.sum(scaled, axis=1, keepdims=True) / D
    mean_cross = jnp.sum(scaled * normal, axis=1, keepdims=True) / D
    return inverse * (scaled - mean_scaled - normal * mean_cross)


def gelu_tanh(pre_value):
    return jax.nn.gelu(pre_value, approximate=True)


def on_device(
    tokens,
    lengths,
    first_gain,
    first_shift,
    qkv_weight,
    query_bias,
    value_bias,
    out_weight,
    out_bias,
    second_gain,
    second_shift,
    up_weight,
    up_bias,
    down_weight,
    down_bias,
    cotangent,
):
    rows = lax.axis_size("row")
    row = lax.axis_index("row")
    col = lax.axis_index("col")
    half = tokens.shape[1]
    block = tokens.shape[0] // 2
    heads = most_heads(rows)
    width = heads * HEAD_DIM

    def halves(matrix):
        pair = matrix.reshape(2, block, half)
        mine = lax.dynamic_index_in_dim(pair, col, 0, keepdims=False)
        other = lax.dynamic_index_in_dim(pair, 1 - col, 0, keepdims=False)
        return jnp.concatenate([mine, swap(other, "col", 1)], axis=1)

    def unhalves(matrix):
        mine = matrix[:, :half]
        other = swap(matrix[:, half:], "col", 1)
        return jnp.concatenate([jnp.where(col == 0, mine, other), jnp.where(col == 0, other, mine)], axis=0)

    dps = lax.axis_size("dp")
    dp = lax.axis_index("dp")

    def over_cols(matrix, other):
        return (matrix[:half] + swap(other, "col", 1).astype(F32)).astype(BF16)

    def over_dp(matrix):
        shares = [share_of(matrix, dp ^ k, dps) for k in range(dps)]
        return scatter_sum([shares[0].astype(F32)] + shares[1:], "dp")

    x_own = halves(tokens)
    x_blocks = gather_blocks(x_own, "row")
    x_all = jnp.concatenate(x_blocks, axis=0).astype(F32)

    vectors = after(jnp.stack([first_gain, first_shift, out_bias, second_gain, second_shift, down_bias]), x_own)
    vectors = jnp.concatenate([vectors, swap(vectors, "col", 1)], axis=1)
    gain1, shift1, out_b, gain2, shift2, down_b = [vectors[i] for i in range(6)]

    qkv_moves = move_tables(rows, [(3, 0, 0)])
    share = share_of(qkv_weight, dp, dps)
    share = move_columns(share, [m[1] for m in qkv_moves], [m[0] for m in qkv_moves], 3 * width, row)
    share = after(share, x_blocks[1])
    qkv_head = by_index(gather_blocks(share, "dp"), dp)
    w_qkv = jnp.concatenate([qkv_head, swap(qkv_head, "col", 1)], axis=0)

    out_share = after(share_of(out_weight.T, dp, dps), share)
    out_share = jnp.concatenate(gather_blocks(out_share, "row"), axis=1)
    windows = window_columns(rows, 1)
    out_shard = D // rows
    relative = np.full((rows, rows * width), -1, np.int32)
    for r in range(rows):
        for k in range(rows):
            held = windows[r ^ k]
            relative[r, k * width : (k + 1) * width] = np.where(held >= 0, ((held // out_shard) ^ r) * out_shard + held % out_shard, -1)
    out_share = mm(out_share, one_hot(table_row(relative, row), D)).astype(BF16)
    out_head = by_index(gather_blocks(out_share, "dp"), dp)
    w_out = jnp.concatenate([out_head, swap(out_head, "col", 1)], axis=0)

    starts = jnp.asarray(np.array(head_starts(rows), np.int32))
    head_at = starts[row] * HEAD_DIM
    live_cols = jnp.arange(width, dtype=jnp.int32) < (starts[row + 1] - starts[row]) * HEAD_DIM

    def bias_window(vector):
        padded = jnp.concatenate([vector, jnp.zeros((width,), F32)])
        return jnp.where(live_cols, lax.dynamic_slice_in_dim(padded, head_at, width), 0.0)

    normal1, inverse1 = norm_parts(x_all)
    normed1 = (normal1 * gain1 + shift1).astype(BF16)
    kv_own = mm(normed1, w_qkv[:, width:])
    bias_kv = jnp.concatenate([jnp.zeros((width,), F32), bias_window(value_bias)])
    kv_own = (kv_own + bias_kv).astype(BF16)
    kv_other = swap(kv_own, "col", 1)
    queries = mm(normed1, w_qkv[:, :width])
    queries = (queries + bias_window(query_bias)).astype(BF16) * BF16(HEAD_DIM ** (-0.5))
    queries = queries.reshape(rows, block, width)
    kv_own = kv_own.reshape(rows, block, 2 * width)
    kv_other = kv_other.reshape(rows, block, 2 * width)
    scal = jnp.stack([row.astype(jnp.int32), col.astype(jnp.int32), lengths[0, 0], lengths[0, 1]])

    cot_own = halves(after(cotangent, x_all))
    own_pos = (row * 2 + col) * block + jnp.arange(block, dtype=jnp.int32)
    live = own_pos < lengths[0, 0] + lengths[0, 1]
    grad_out = jnp.where(live[:, None], cot_own, 0.0)
    grad_out_low = after(grad_out.astype(BF16), normed1)
    g_blocks = lax.all_gather(grad_out_low, "row", tiled=True)

    attention, lse = attend_forward(scal, queries, kv_own, kv_other, heads)

    att_own = jnp.concatenate(send_blocks([attention[k] for k in range(rows)], "row"), axis=1)
    resid_mid = x_own.astype(F32) + (mm_nt(att_own, w_out) + out_b)

    normal2, inverse2 = norm_parts(resid_mid)
    normed2 = (normal2 * gain2 + shift2).astype(BF16)
    mlp_in = jnp.concatenate(gather_blocks(normed2, "row"), axis=0)
    up_own = after(up_weight, x_all)
    down_own = after(down_weight, kv_own)
    w_up = jnp.concatenate([up_own, swap(up_own, "col", 1)], axis=0)
    w_down = jnp.concatenate([down_own, swap(down_own, "col", 1)], axis=1)
    g_blocks = after(g_blocks, normed2)
    g_all = jnp.concatenate([share_of(g_blocks, row ^ k, rows) for k in range(rows)], axis=0)
    down_bias_part = jnp.sum(grad_out_low.astype(F32), axis=0)

    pre_act = mm(mlp_in, w_up) + up_bias
    act, gelu_back = jax.vjp(gelu_tanh, pre_act)
    grad_act = mm_nt(g_all, w_down)
    act, grad_pre = lax.optimization_barrier((act.astype(BF16), gelu_back(grad_act)[0].astype(BF16)))
    up_bias_part = jnp.sum(grad_pre.astype(F32), axis=0)
    grad_normed2 = mm_nt(grad_pre, w_up)

    late_g, late_act, late_in, late_pre, _ = lax.optimization_barrier((g_all, act, mlp_in, grad_pre, grad_normed2))
    down_grad = mm_tn(late_g, late_act)
    up_grad = mm_tn(late_in, late_pre)
    down_grad = over_cols(down_grad, down_grad[half:].astype(BF16))
    up_grad = over_cols(up_grad, up_grad[half:].astype(BF16))

    grad_normed2 = after(scatter_sum(rows_of(grad_normed2, rows), "row"), down_grad, up_grad)
    second_gain_part = jnp.sum(grad_normed2 * normal2, axis=0)
    second_shift_part = jnp.sum(grad_normed2, axis=0)
    grad_mid = grad_out + norm_back(grad_normed2, normal2, inverse2, gain2)
    grad_mid_low = grad_mid.astype(BF16)
    out_bias_part = jnp.sum(grad_mid_low.astype(F32), axis=0)

    grad_att = mm(grad_mid_low, w_out).astype(BF16)
    grad_att = jnp.stack(send_blocks([grad_att[:, k * width : (k + 1) * width] for k in range(rows)], "row"))
    att_shards = mm_nt(att_own, one_hot(table_row(relative, row), D)).astype(BF16)
    out_grad = mm_tn(grad_mid_low, att_shards)
    out_other = out_grad[half:].astype(BF16)
    grad_att = after(grad_att, out_other)
    up_grad, down_grad = lax.psum((up_grad, down_grad), "dp")

    dq, dkv_own, dkv_other = attend_backward(scal, queries, kv_own, kv_other, grad_att, lse.T, heads)
    out_grad = over_cols(after(out_grad, dq), out_other)
    dkv = (dkv_own + swap(dkv_other, "col", 1).astype(F32)).astype(BF16)
    grad_qkv = jnp.concatenate([dq, dkv], axis=2).reshape(-1, 3 * width)
    qkv_bias_part = jnp.sum(grad_qkv.astype(F32), axis=0)
    normed_part = mm_nt(grad_qkv, w_qkv)
    first_gain_part = jnp.sum(normed_part * normal1, axis=0)
    first_shift_part = jnp.sum(normed_part, axis=0)
    qkv_grad = mm_tn(normed1, after(grad_qkv, normed_part))
    qkv_grad = over_cols(qkv_grad, qkv_grad[half:].astype(BF16))
    grad_normed1 = after(scatter_sum(rows_of(normed_part, rows), "row"), qkv_grad)
    back1 = norm_back(grad_normed1, normal1[:block], inverse1[:block], gain1)
    input_grad = unhalves(grad_mid + back1)

    out_grad = over_dp(out_grad)
    qkv_grad = over_dp(after(qkv_grad, out_grad)).astype(BF16)
    out_grad = after(out_grad, qkv_grad)
    qkv_summed = qkv_grad
    qkv_grad = move_columns(qkv_grad, [m[0] for m in qkv_moves], [m[1] for m in qkv_moves], 3 * out_shard, row)
    out_grad = scatter_sum([out_grad[:, k * out_shard : (k + 1) * out_shard] for k in range(rows)], "row").astype(BF16)
    both = jnp.concatenate([qkv_grad, out_grad], axis=1)
    both = by_index([item.astype(F32) for item in gather_blocks(both, "dp")], dp)
    qkv_grad = both[:, : 3 * out_shard]
    out_grad = both[:, 3 * out_shard :].T

    down_out = mm(act, w_down)
    block_out = scatter_sum(rows_of(after(down_out, grad_normed1), rows), "row")
    block_out = unhalves((resid_mid + (block_out + down_b)).astype(BF16))

    def place(vector):
        mine, other = vector[:half], vector[half:]
        return jnp.concatenate([jnp.where(col == 0, mine, other), jnp.where(col == 0, other, mine)])

    def place_window(vector):
        padded = lax.dynamic_update_slice_in_dim(jnp.zeros((D + width,), F32), vector, head_at, 0)
        return padded[:D]

    def place_rows(vector):
        return lax.dynamic_update_slice_in_dim(jnp.zeros((FF,), F32), vector, row * vector.shape[0], 0)

    small = sum_all(
        after(
            jnp.concatenate(
            [
                place_rows(up_bias_part),
                place(down_bias_part),
                place(second_gain_part),
                place(second_shift_part),
                place(out_bias_part),
                place(first_gain_part),
                place(first_shift_part),
                place_window(qkv_bias_part[:width]),
                place_window(qkv_bias_part[2 * width :]),
            ]
            ),
            grad_normed1,
            qkv_summed,
        )
    )

    def own_half(part):
        return lax.dynamic_slice_in_dim(small, FF + part * D + col * half, half)

    up_width = up_bias.shape[0]
    return (
        block_out,
        input_grad,
        own_half(4),
        own_half(5),
        qkv_grad,
        small[FF + 6 * D : FF + 7 * D],
        small[FF + 7 * D :],
        out_grad,
        own_half(3),
        own_half(1),
        own_half(2),
        up_grad.astype(F32),
        lax.dynamic_slice_in_dim(small, row * up_width, up_width),
        down_grad.T.astype(F32),
        own_half(0),
    )


def solution(mesh):
    in_specs = (
        P(("dp", "row"), "col"),
        P("dp", None),
        P("col"),
        P("col"),
        P("col", "row"),
        P(),
        P(),
        P("row", "col"),
        P("col"),
        P("col"),
        P("col"),
        P("col", "row"),
        P("row"),
        P("row", "col"),
        P("col"),
        P(("dp", "row"), "col"),
    )
    out_specs = (
        P(("dp", "row"), "col"),
        P(("dp", "row"), "col"),
        P("col"),
        P("col"),
        P("col", "row"),
        P(),
        P(),
        P("row", "col"),
        P("col"),
        P("col"),
        P("col"),
        P("col", "row"),
        P("row"),
        P("row", "col"),
        P("col"),
    )
    return jax.shard_map(
        on_device, mesh=mesh, in_specs=in_specs, out_specs=out_specs, check_vma=False
    )
```

```python
import functools

import jax
import jax.numpy as jnp
import numpy as np
from jax import lax
from jax.experimental import pallas as pl
from jax.experimental.pallas import tpu as pltpu
from jax.sharding import PartitionSpec as P

D = 1088
HEADS = 17
HEAD_DIM = 64
FF = 4352
TOK_G = 1024

EPSILON = 1e-05
MASKED = -1e30
CHUNK = 256
BF16 = jnp.bfloat16
F32 = jnp.float32


def swap(payload, axis, distance):
    size = lax.axis_size(axis)
    return lax.ppermute(payload, axis, [(i, i ^ distance) for i in range(size)])


def after(payload, *others):
    return lax.optimization_barrier((payload, *others))[0]


def gather_blocks(payload, axis):
    if lax.axis_size(axis) == 4 and axis == "row":
        far = swap(payload, axis, 2)
        near = swap(payload, axis, 1)
        return [payload, near, far, swap(far, axis, 1)]
    return [payload] + [swap(payload, axis, k) for k in range(1, lax.axis_size(axis))]


def send_blocks(blocks, axis):
    return [blocks[0]] + [swap(blocks[k], axis, k) for k in range(1, len(blocks))]


def scatter_sum(blocks, axis):
    received = [swap(blocks[k].astype(BF16), axis, k) for k in range(1, len(blocks))]
    total = blocks[0]
    for item in received:
        total = total + item.astype(F32)
    return total


def sum_all(vector):
    for axis in ("row", "dp", "col"):
        distance = 1
        while distance < lax.axis_size(axis):
            vector = vector + swap(vector, axis, distance)
            distance *= 2
    return vector


def share_of(matrix, index, parts):
    size = matrix.shape[0] // parts
    return lax.dynamic_slice_in_dim(matrix, index * size, size, 0)


def by_index(blocks, index):
    count = len(blocks)
    total = jnp.zeros((count,) + blocks[0].shape, blocks[0].dtype)
    for k, item in enumerate(blocks):
        total = lax.dynamic_update_index_in_dim(total, item, index ^ k, 0)
    return total.reshape((count * blocks[0].shape[0],) + blocks[0].shape[1:])


def rows_of(matrix, parts):
    size = matrix.shape[0] // parts
    return [matrix[k * size : (k + 1) * size] for k in range(parts)]


def head_starts(rows):
    return [int(np.floor(HEADS * r / rows + 0.5)) for r in range(rows + 1)]


def most_heads(rows):
    starts = head_starts(rows)
    return max(b - a for a, b in zip(starts[:-1], starts[1:]))


def window_columns(rows, copies):
    starts = head_starts(rows)
    width = most_heads(rows) * HEAD_DIM
    table = np.full((rows, copies * width), -1, np.int64)
    for r in range(rows):
        count = (starts[r + 1] - starts[r]) * HEAD_DIM
        for t in range(copies):
            table[r, t * width : t * width + count] = t * D + starts[r] * HEAD_DIM + np.arange(count)
    return table


def move_tables(rows, parts):
    moves = []
    for k in range(rows):
        places = [[] for _ in range(rows)]
        columns = [[] for _ in range(rows)]
        for copies, place_at, column_at in parts:
            windows = window_columns(rows, copies)
            shard = copies * D // rows
            for r in range(rows):
                for p in range(windows.shape[1]):
                    if windows[r, p] >= 0 and windows[r, p] // shard == r ^ k:
                        places[r].append(place_at + p)
                        columns[r].append(column_at + int(windows[r, p] % shard))
        longest = -(-max(len(place) for place in places) // 16) * 16
        at = np.full((rows, longest), -1, np.int32)
        frm = np.full((rows, longest), -1, np.int32)
        for r in range(rows):
            at[r, : len(places[r])] = places[r]
            frm[r ^ k, : len(columns[r])] = columns[r]
        moves.append((at, frm))
    return moves


def table_row(table, index):
    return lax.dynamic_index_in_dim(jnp.asarray(table), index, 0, keepdims=True)


def one_hot(places, size):
    return (lax.broadcasted_iota(jnp.int32, (size, places.shape[1]), 0) == places).astype(BF16)


def move_columns(matrix, from_tables, to_tables, width, row):
    counts = [table.shape[1] for table in from_tables]
    picked = mm(matrix, one_hot(table_row(np.concatenate(from_tables, 1), row), matrix.shape[1])).astype(BF16)
    slabs, at = [], 0
    for k, count in enumerate(counts):
        slab = picked[:, at : at + count]
        at += count
        if count:
            slabs.append(swap(slab, "row", k) if k else slab)
    return mm_nt(jnp.concatenate(slabs, axis=1), one_hot(table_row(np.concatenate(to_tables, 1), row), width)).astype(BF16)


def mm(a, b):
    return jnp.dot(a, b, preferred_element_type=F32)


def mm_nt(a, b):
    return lax.dot_general(a, b, (((1,), (1,)), ((), ())), preferred_element_type=F32)


def mm_tn(a, b):
    return lax.dot_general(a, b, (((0,), (0,)), ((), ())), preferred_element_type=F32)


def positions(start, shape, dim, block, col):
    at = lax.broadcasted_iota(jnp.int32, shape, dim) + start
    shift = block.bit_length() - 1
    return lax.shift_left(lax.shift_right_logical(at, shift), shift + 1) + (at & (block - 1)) + col * block


def segments(pos, scal_ref):
    first = scal_ref[2]
    return (pos >= first).astype(jnp.int32) + (pos >= first + scal_ref[3]).astype(jnp.int32)


def mask_bias(scal_ref, query_at, query_shape, query_dim, key_shape, key_dim, block, key_col):
    query_pos = positions(query_at, query_shape, query_dim, block, scal_ref[1])
    key_pos = positions(0, key_shape, key_dim, block, key_col)
    allowed = (key_pos <= query_pos) & (segments(key_pos, scal_ref) == segments(query_pos, scal_ref))
    return jnp.where(allowed, 0.0, MASKED)


def in_order(source_ref, target_ref, row, blocks, block):
    for j in range(blocks):
        target_ref[j * block : (j + 1) * block, :] = source_ref[j ^ row]


def forward_kernel(blocks, block, heads, scal_ref, q_ref, kv0_ref, kv1_ref, out_ref, lse_ref, q_s, kv0_s, kv1_s, o_s):
    row = scal_ref[0]
    width = heads * HEAD_DIM
    in_order(q_ref, q_s, row, blocks, block)
    in_order(kv0_ref, kv0_s, row, blocks, block)
    in_order(kv1_ref, kv1_s, row, blocks, block)
    own = scal_ref[1]
    for i in range(blocks * block // CHUNK):
        span = slice(i * CHUNK, (i + 1) * CHUNK)
        keys = (i + 1) * CHUNK
        shape = (CHUNK, keys)
        bias0 = mask_bias(scal_ref, i * CHUNK, (CHUNK, 1), 0, (1, keys), 1, block, own)
        bias1 = mask_bias(scal_ref, i * CHUNK, (CHUNK, 1), 0, (1, keys), 1, block, 1 - own)
        for h in range(heads):
            at = slice(h * HEAD_DIM, (h + 1) * HEAD_DIM)
            va = slice(width + h * HEAD_DIM, width + (h + 1) * HEAD_DIM)
            query = q_s[span, at]
            s0 = mm_nt(query, kv0_s[:keys, at]) + bias0
            s1 = mm_nt(query, kv1_s[:keys, at]) + bias1
            top = jnp.maximum(jnp.max(s0, axis=1, keepdims=True), jnp.max(s1, axis=1, keepdims=True))
            e0 = jnp.exp(s0 - top)
            e1 = jnp.exp(s1 - top)
            total = jnp.sum(e0, axis=1, keepdims=True) + jnp.sum(e1, axis=1, keepdims=True)
            result = mm(e0.astype(BF16), kv0_s[:keys, va]) + mm(e1.astype(BF16), kv1_s[:keys, va])
            o_s[span, at] = (result / total).astype(BF16)
            lse_ref[span, h : h + 1] = top + jnp.log(total)
    for j in range(blocks):
        out_ref[j ^ row] = o_s[j * block : (j + 1) * block, :]


def backward_kernel(
    blocks,
    block,
    heads,
    scal_ref,
    q_ref,
    kv0_ref,
    kv1_ref,
    g_ref,
    lse_ref,
    dq_ref,
    own_ref,
    other_ref,
    q_s,
    kv0_s,
    kv1_s,
    g_s,
    dq_s,
    d0_s,
    d1_s,
):
    row = scal_ref[0]
    width = heads * HEAD_DIM
    in_order(q_ref, q_s, row, blocks, block)
    in_order(kv0_ref, kv0_s, row, blocks, block)
    in_order(kv1_ref, kv1_s, row, blocks, block)
    in_order(g_ref, g_s, row, blocks, block)
    own = scal_ref[1]
    chunks = blocks * block // CHUNK
    for i in reversed(range(chunks)):
        span = slice(i * CHUNK, (i + 1) * CHUNK)
        keys = (i + 1) * CHUNK
        bias0 = mask_bias(scal_ref, i * CHUNK, (1, CHUNK), 1, (keys, 1), 0, block, own)
        bias1 = mask_bias(scal_ref, i * CHUNK, (1, CHUNK), 1, (keys, 1), 0, block, 1 - own)
        for h in range(heads):
            at = slice(h * HEAD_DIM, (h + 1) * HEAD_DIM)
            va = slice(width + h * HEAD_DIM, width + (h + 1) * HEAD_DIM)
            query = q_s[span, at]
            grad = g_s[span, at]
            lse = lse_ref[h : h + 1, span]
            p0 = jnp.exp(mm_nt(kv0_s[:keys, at], query) + bias0 - lse)
            p1 = jnp.exp(mm_nt(kv1_s[:keys, at], query) + bias1 - lse)
            dp0 = mm_nt(kv0_s[:keys, va], grad)
            dp1 = mm_nt(kv1_s[:keys, va], grad)
            delta = jnp.sum(p0 * dp0, axis=0, keepdims=True) + jnp.sum(p1 * dp1, axis=0, keepdims=True)
            ds0 = (p0 * (dp0 - delta)).astype(BF16)
            ds1 = (p1 * (dp1 - delta)).astype(BF16)
            if i == chunks - 1:
                d0_s[:keys, at] = mm(ds0, query)
                d1_s[:keys, at] = mm(ds1, query)
                d0_s[:keys, va] = mm(p0.astype(BF16), grad)
                d1_s[:keys, va] = mm(p1.astype(BF16), grad)
            else:
                d0_s[:keys, at] += mm(ds0, query)
                d1_s[:keys, at] += mm(ds1, query)
                d0_s[:keys, va] += mm(p0.astype(BF16), grad)
                d1_s[:keys, va] += mm(p1.astype(BF16), grad)
            dquery = mm_tn(ds0, kv0_s[:keys, at]) + mm_tn(ds1, kv1_s[:keys, at])
            dq_s[span, at] = (dquery * HEAD_DIM ** (-0.5)).astype(BF16)
    for j in range(blocks):
        piece = slice(j * block, (j + 1) * block)
        dq_ref[j ^ row] = dq_s[piece, :]
        own_ref[j ^ row] = d0_s[piece, :]
        other_ref[j ^ row] = d1_s[piece, :].astype(BF16)


def vmem():
    return pl.BlockSpec(memory_space=pltpu.VMEM)


def smem():
    return pl.BlockSpec(memory_space=pltpu.SMEM)


def attend_forward(scal, queries, kv_own, kv_other, heads):
    blocks, block, width = queries.shape
    tokens = blocks * block
    return pl.pallas_call(
        functools.partial(forward_kernel, blocks, block, heads),
        out_shape=(
            jax.ShapeDtypeStruct((blocks, block, width), BF16),
            jax.ShapeDtypeStruct((tokens, heads), F32),
        ),
        in_specs=[smem(), vmem(), vmem(), vmem()],
        out_specs=(vmem(), vmem()),
        scratch_shapes=[
            pltpu.VMEM((tokens, width), BF16),
            pltpu.VMEM((tokens, 2 * width), BF16),
            pltpu.VMEM((tokens, 2 * width), BF16),
            pltpu.VMEM((tokens, width), BF16),
        ],
        compiler_params=pltpu.CompilerParams(vmem_limit_bytes=40 * 2**20),
        cost_estimate=pl.CostEstimate(
            flops=4 * tokens * 3 * tokens // 2 * width, bytes_accessed=6 * tokens * width * 2, transcendentals=heads * tokens * tokens
        ),
        name="attend_forward",
    )(scal, queries, kv_own, kv_other)


def attend_backward(scal, queries, kv_own, kv_other, grads, lse, heads):
    blocks, block, width = queries.shape
    tokens = blocks * block
    return pl.pallas_call(
        functools.partial(backward_kernel, blocks, block, heads),
        out_shape=(
            jax.ShapeDtypeStruct((blocks, block, width), BF16),
            jax.ShapeDtypeStruct((blocks, block, 2 * width), F32),
            jax.ShapeDtypeStruct((blocks, block, 2 * width), BF16),
        ),
        in_specs=[smem(), vmem(), vmem(), vmem(), vmem(), vmem()],
        out_specs=(vmem(), vmem(), vmem()),
        scratch_shapes=[
            pltpu.VMEM((tokens, width), BF16),
            pltpu.VMEM((tokens, 2 * width), BF16),
            pltpu.VMEM((tokens, 2 * width), BF16),
            pltpu.VMEM((tokens, width), BF16),
            pltpu.VMEM((tokens, width), BF16),
            pltpu.VMEM((tokens, 2 * width), F32),
            pltpu.VMEM((tokens, 2 * width), F32),
        ],
        compiler_params=pltpu.CompilerParams(vmem_limit_bytes=44 * 2**20),
        cost_estimate=pl.CostEstimate(
            flops=10 * tokens * 3 * tokens // 2 * width, bytes_accessed=14 * tokens * width * 2, transcendentals=heads * tokens * tokens
        ),
        name="attend_backward",
    )(scal, queries, kv_own, kv_other, grads, lse)


def norm_parts(resid_in):
    mean_value = jnp.sum(resid_in, axis=1, keepdims=True) / D
    square = jnp.sum(resid_in * resid_in, axis=1, keepdims=True) / D
    inverse = lax.rsqrt(square - mean_value * mean_value + EPSILON)
    return ((resid_in - mean_value) * inverse, inverse)


def norm_back(grad_in, normal, inverse, norm_gain):
    scaled = grad_in * norm_gain
    mean_scaled = jnp.sum(scaled, axis=1, keepdims=True) / D
    mean_cross = jnp.sum(scaled * normal, axis=1, keepdims=True) / D
    return inverse * (scaled - mean_scaled - normal * mean_cross)


def gelu_tanh(pre_value):
    return jax.nn.gelu(pre_value, approximate=True)


def on_device(
    tokens,
    lengths,
    first_gain,
    first_shift,
    qkv_weight,
    query_bias,
    value_bias,
    out_weight,
    out_bias,
    second_gain,
    second_shift,
    up_weight,
    up_bias,
    down_weight,
    down_bias,
    cotangent,
):
    rows = lax.axis_size("row")
    row = lax.axis_index("row")
    col = lax.axis_index("col")
    half = tokens.shape[1]
    block = tokens.shape[0] // 2
    heads = most_heads(rows)
    width = heads * HEAD_DIM

    def halves(blocks):
        pairs = jnp.stack([item.reshape(2, block, half) for item in blocks])
        mine = lax.dynamic_index_in_dim(pairs, col, 1, keepdims=False)
        other = lax.dynamic_index_in_dim(pairs, 1 - col, 1, keepdims=False)
        whole = jnp.concatenate([mine, swap(other, "col", 1)], axis=2)
        return whole.reshape(len(blocks) * block, 2 * half)

    def unhalves(matrix):
        mine = matrix[:, :half]
        other = swap(matrix[:, half:], "col", 1)
        return jnp.concatenate([jnp.where(col == 0, mine, other), jnp.where(col == 0, other, mine)], axis=0)

    dps = lax.axis_size("dp")
    dp = lax.axis_index("dp")

    def over_cols(left, right, *others):
        other = after(mm_tn(left[:, half:], right).astype(BF16), *others)
        other = swap(other, "col", 1)
        return (mm_tn(left[:, :half], right) + other.astype(F32)).astype(BF16)

    def over_dp(matrix, *others):
        shares = [share_of(matrix, dp ^ k, dps) for k in range(dps)]
        return scatter_sum([after(shares[0].astype(F32), *others)] + shares[1:], "dp")

    x_blocks = gather_blocks(tokens, "row")
    x_first = halves(x_blocks[: rows // 2])
    x_own = x_first[:block]
    x_all = jnp.concatenate([x_first, halves(x_blocks[rows // 2 :])], axis=0).astype(F32)

    vectors = jnp.stack([first_gain, first_shift, out_bias, second_gain, second_shift, down_bias])
    vectors = jnp.concatenate([vectors, swap(after(vectors, x_blocks[1]), "col", 1)], axis=1)
    gain1, shift1, out_b, gain2, shift2, down_b = [vectors[i] for i in range(6)]

    qkv_moves = move_tables(rows, [(3, 0, 0)])
    share = share_of(qkv_weight, dp, dps)
    share = move_columns(share, [m[1] for m in qkv_moves], [m[0] for m in qkv_moves], 3 * width, row)
    share = after(share, x_blocks[1])
    qkv_head = by_index(gather_blocks(share, "dp"), dp)
    qkv_other = swap(qkv_head, "col", 1)
    w_qkv = jnp.concatenate([qkv_head, qkv_other], axis=0)

    out_share = after(share_of(out_weight.T, dp, dps), x_blocks[rows - 1])
    out_share = jnp.concatenate(gather_blocks(out_share, "row"), axis=1)
    windows = window_columns(rows, 1)
    out_shard = D // rows
    relative = np.full((rows, rows * width), -1, np.int32)
    for r in range(rows):
        for k in range(rows):
            held = windows[r ^ k]
            relative[r, k * width : (k + 1) * width] = np.where(held >= 0, ((held // out_shard) ^ r) * out_shard + held % out_shard, -1)
    out_share = mm(out_share, one_hot(table_row(relative, row), D)).astype(BF16)
    out_head = by_index(gather_blocks(after(out_share, qkv_other), "dp"), dp)
    w_out = jnp.concatenate([out_head, swap(out_head, "col", 1)], axis=0)

    starts = jnp.asarray(np.array(head_starts(rows), np.int32))
    head_at = starts[row] * HEAD_DIM
    live_cols = jnp.arange(width, dtype=jnp.int32) < (starts[row + 1] - starts[row]) * HEAD_DIM

    def bias_window(vector):
        padded = jnp.concatenate([vector, jnp.zeros((width,), F32)])
        return jnp.where(live_cols, lax.dynamic_slice_in_dim(padded, head_at, width), 0.0)

    normal1, inverse1 = norm_parts(x_all)
    normed1 = (normal1 * gain1 + shift1).astype(BF16)
    kv_own = mm(normed1, w_qkv[:, width:])
    bias_kv = jnp.concatenate([jnp.zeros((width,), F32), bias_window(value_bias)])
    kv_own = (kv_own + bias_kv).astype(BF16)
    kv_other = swap(kv_own, "col", 1)
    queries = mm(normed1, w_qkv[:, :width])
    queries = (queries + bias_window(query_bias)).astype(BF16) * BF16(HEAD_DIM ** (-0.5))
    queries = queries.reshape(rows, block, width)
    kv_own = kv_own.reshape(rows, block, 2 * width)
    kv_other = kv_other.reshape(rows, block, 2 * width)
    scal = jnp.stack([row.astype(jnp.int32), col.astype(jnp.int32), lengths[0, 0], lengths[0, 1]])

    def live_rows(matrix, start):
        live = start + jnp.arange(matrix.shape[0], dtype=jnp.int32) < lengths[0, 0] + lengths[0, 1]
        return jnp.where(live[:, None], matrix, 0.0)

    grad_slots = live_rows(cotangent, row * 2 * block).astype(BF16)
    g_blocks = lax.all_gather(after(grad_slots, x_blocks[rows - 1]), "row", tiled=True)

    attention, lse = attend_forward(scal, queries, kv_own, kv_other, heads)

    att_own = jnp.concatenate(send_blocks([attention[k] for k in range(rows)], "row"), axis=1)
    resid_mid = x_own.astype(F32) + (mm_nt(att_own, w_out) + out_b)

    normal2, inverse2 = norm_parts(resid_mid)
    normed2 = (normal2 * gain2 + shift2).astype(BF16)
    mlp_in = jnp.concatenate(gather_blocks(normed2, "row"), axis=0)
    up_own = after(up_weight, attention)
    down_own = after(down_weight, attention)
    w_up = jnp.concatenate([up_own, swap(up_own, "col", 1)], axis=0)
    w_down = jnp.concatenate([down_own, swap(down_own, "col", 1)], axis=1)
    g_blocks = after(g_blocks, normed2)
    g_all = halves([share_of(g_blocks, row ^ k, rows) for k in range(rows)])
    grad_out = halves([after(cotangent, normed2)])
    grad_out = live_rows(grad_out, (row * 2 + col) * block)
    grad_out_low = grad_out.astype(BF16)
    down_bias_part = jnp.sum(grad_out_low.astype(F32), axis=0)

    pre_act = mm(mlp_in, w_up) + up_bias
    act, gelu_back = jax.vjp(gelu_tanh, pre_act)
    grad_act = mm_nt(g_all, w_down)
    act, grad_pre = lax.optimization_barrier((act.astype(BF16), gelu_back(grad_act)[0].astype(BF16)))
    up_bias_part = jnp.sum(grad_pre.astype(F32), axis=0)
    grad_normed2 = mm_nt(grad_pre, w_up)

    late_g, late_act, late_in, late_pre, _ = lax.optimization_barrier((g_all, act, mlp_in, grad_pre, grad_normed2))
    down_grad = over_cols(late_g, late_act)
    up_grad = over_cols(late_in, late_pre)

    blocks = rows_of(grad_normed2, rows)
    grad_normed2 = scatter_sum([after(blocks[0], down_grad, up_grad)] + blocks[1:], "row")
    second_gain_part = jnp.sum(grad_normed2 * normal2, axis=0)
    second_shift_part = jnp.sum(grad_normed2, axis=0)
    grad_mid = grad_out + norm_back(grad_normed2, normal2, inverse2, gain2)
    grad_mid_low = grad_mid.astype(BF16)
    out_bias_part = jnp.sum(grad_mid_low.astype(F32), axis=0)

    grad_att = mm(grad_mid_low, w_out).astype(BF16)
    grad_att = jnp.stack(send_blocks([grad_att[:, k * width : (k + 1) * width] for k in range(rows)], "row"))
    att_shards = mm_nt(after(att_own, down_grad), one_hot(table_row(relative, row), D)).astype(BF16)
    out_other = mm_tn(grad_mid_low[:, half:], att_shards).astype(BF16)
    out_grad = mm_tn(grad_mid_low[:, :half], att_shards)
    out_grad = (out_grad + swap(out_other, "col", 1).astype(F32)).astype(BF16)
    grad_att = after(grad_att, out_grad)
    up_grad, down_grad = lax.psum((up_grad, down_grad), "dp")

    dq, dkv_own, dkv_other = attend_backward(scal, queries, kv_own, kv_other, grad_att, lse.T, heads)
    dkv = (dkv_own + swap(dkv_other, "col", 1).astype(F32)).astype(BF16)
    grad_qkv = jnp.concatenate([dq, dkv], axis=2).reshape(-1, 3 * width)
    qkv_bias_part = jnp.sum(grad_qkv.astype(F32), axis=0)
    normed_part = mm_nt(grad_qkv, w_qkv)
    first_gain_part = jnp.sum(normed_part * normal1, axis=0)
    first_shift_part = jnp.sum(normed_part, axis=0)
    qkv_grad = over_cols(normed1, after(grad_qkv, normed_part))
    blocks = rows_of(normed_part, rows)
    grad_normed1 = scatter_sum([after(blocks[0], qkv_grad)] + blocks[1:], "row")
    back1 = norm_back(grad_normed1, normal1[:block], inverse1[:block], gain1)
    input_grad = unhalves(grad_mid + back1)

    qkv_grad = over_dp(qkv_grad).astype(BF16)
    qkv_summed = qkv_grad
    out_grad = over_dp(out_grad, normed_part)
    out_grad = after(out_grad, qkv_summed)
    qkv_grad = move_columns(qkv_grad, [m[0] for m in qkv_moves], [m[1] for m in qkv_moves], 3 * out_shard, row)
    out_grad = scatter_sum([out_grad[:, k * out_shard : (k + 1) * out_shard] for k in range(rows)], "row").astype(BF16)
    both = gather_blocks(jnp.concatenate([qkv_grad, out_grad], axis=1), "dp")
    both[1], up_grad, down_grad = lax.optimization_barrier((both[1], up_grad, down_grad))
    both = by_index([item.astype(F32) for item in both], dp)
    qkv_grad = both[:, : 3 * out_shard]
    out_grad = both[:, 3 * out_shard :].T

    down_out = mm(act, w_down)
    blocks = by_index([after(item.astype(BF16), qkv_summed) for item in rows_of(down_out, rows)], row)
    block_out = lax.psum_scatter(blocks, "row", scatter_dimension=0, tiled=True)
    block_out = unhalves((resid_mid + (block_out.astype(F32) + down_b)).astype(BF16))

    def place(vector):
        mine, other = vector[:half], vector[half:]
        return jnp.concatenate([jnp.where(col == 0, mine, other), jnp.where(col == 0, other, mine)])

    def place_window(vector):
        padded = lax.dynamic_update_slice_in_dim(jnp.zeros((D + width,), F32), vector, head_at, 0)
        return padded[:D]

    def place_rows(vector):
        return lax.dynamic_update_slice_in_dim(jnp.zeros((FF,), F32), vector, row * vector.shape[0], 0)

    small = sum_all(
        after(
            jnp.concatenate(
            [
                place_rows(up_bias_part),
                place(down_bias_part),
                place(second_gain_part),
                place(second_shift_part),
                place(out_bias_part),
                place(first_gain_part),
                place(first_shift_part),
                place_window(qkv_bias_part[:width]),
                place_window(qkv_bias_part[2 * width :]),
            ]
            ),
            grad_normed1,
            qkv_summed,
        )
    )

    def own_half(part):
        return lax.dynamic_slice_in_dim(small, FF + part * D + col * half, half)

    up_width = up_bias.shape[0]
    return (
        block_out,
        input_grad,
        own_half(4),
        own_half(5),
        qkv_grad,
        small[FF + 6 * D : FF + 7 * D],
        small[FF + 7 * D :],
        out_grad,
        own_half(3),
        own_half(1),
        own_half(2),
        up_grad.astype(F32),
        lax.dynamic_slice_in_dim(small, row * up_width, up_width),
        down_grad.T.astype(F32),
        own_half(0),
    )


def solution(mesh):
    in_specs = (
        P(("dp", "row"), "col"),
        P("dp", None),
        P("col"),
        P("col"),
        P("col", "row"),
        P(),
        P(),
        P("row", "col"),
        P("col"),
        P("col"),
        P("col"),
        P("col", "row"),
        P("row"),
        P("row", "col"),
        P("col"),
        P(("dp", "row"), "col"),
    )
    out_specs = (
        P(("dp", "row"), "col"),
        P(("dp", "row"), "col"),
        P("col"),
        P("col"),
        P("col", "row"),
        P(),
        P(),
        P("row", "col"),
        P("col"),
        P("col"),
        P("col"),
        P("col", "row"),
        P("row"),
        P("row", "col"),
        P("col"),
    )
    return jax.shard_map(
        on_device, mesh=mesh, in_specs=in_specs, out_specs=out_specs, check_vma=False
    )
```

```python
import functools

import jax
import jax.numpy as jnp
import numpy as np
from jax import lax
from jax.experimental import pallas as pl
from jax.experimental.pallas import tpu as pltpu
from jax.sharding import PartitionSpec as P

D = 1088
HEADS = 17
HEAD_DIM = 64
FF = 4352
TOK_G = 1024

EPSILON = 1e-05
MASKED = -1e30
CHUNK = 256
BF16 = jnp.bfloat16
F32 = jnp.float32


def swap(payload, axis, distance):
    size = lax.axis_size(axis)
    return lax.ppermute(payload, axis, [(i, i ^ distance) for i in range(size)])


def after(payload, *others):
    return lax.optimization_barrier((payload, *others))[0]


def gather_blocks(payload, axis, relay=0):
    if lax.axis_size(axis) == relay:
        far = swap(payload, axis, 2)
        near = swap(payload, axis, 1)
        return [payload, near, far, swap(far, axis, 1)]
    return [payload] + [swap(payload, axis, k) for k in range(1, lax.axis_size(axis))]


def send_blocks(blocks, axis):
    return [blocks[0]] + [swap(blocks[k], axis, k) for k in range(1, len(blocks))]


def scatter_sum(blocks, axis):
    received = [swap(blocks[k].astype(BF16), axis, k) for k in range(1, len(blocks))]
    total = blocks[0]
    for item in received:
        total = total + item.astype(F32)
    return total


def share_of(matrix, index, parts):
    size = matrix.shape[0] // parts
    return lax.dynamic_slice_in_dim(matrix, index * size, size, 0)


def by_index(blocks, index):
    count = len(blocks)
    total = jnp.zeros((count,) + blocks[0].shape, blocks[0].dtype)
    for k, item in enumerate(blocks):
        total = lax.dynamic_update_index_in_dim(total, item, index ^ k, 0)
    return total.reshape((count * blocks[0].shape[0],) + blocks[0].shape[1:])


def rows_of(matrix, parts):
    size = matrix.shape[0] // parts
    return [matrix[k * size : (k + 1) * size] for k in range(parts)]


def head_starts(rows):
    return [int(np.floor(HEADS * r / rows + 0.5)) for r in range(rows + 1)]


def most_heads(rows):
    starts = head_starts(rows)
    return max(b - a for a, b in zip(starts[:-1], starts[1:]))


def window_columns(rows, copies):
    starts = head_starts(rows)
    width = most_heads(rows) * HEAD_DIM
    table = np.full((rows, copies * width), -1, np.int64)
    for r in range(rows):
        count = (starts[r + 1] - starts[r]) * HEAD_DIM
        for t in range(copies):
            table[r, t * width : t * width + count] = t * D + starts[r] * HEAD_DIM + np.arange(count)
    return table


def move_tables(rows, parts):
    moves = []
    for k in range(rows):
        places = [[] for _ in range(rows)]
        columns = [[] for _ in range(rows)]
        for copies, place_at, column_at in parts:
            windows = window_columns(rows, copies)
            shard = copies * D // rows
            for r in range(rows):
                for p in range(windows.shape[1]):
                    if windows[r, p] >= 0 and windows[r, p] // shard == r ^ k:
                        places[r].append(place_at + p)
                        columns[r].append(column_at + int(windows[r, p] % shard))
        longest = -(-max(len(place) for place in places) // 16) * 16
        at = np.full((rows, longest), -1, np.int32)
        frm = np.full((rows, longest), -1, np.int32)
        for r in range(rows):
            at[r, : len(places[r])] = places[r]
            frm[r ^ k, : len(columns[r])] = columns[r]
        moves.append((at, frm))
    return moves


def table_row(table, index):
    return lax.dynamic_index_in_dim(jnp.asarray(table), index, 0, keepdims=True)


def one_hot(places, size):
    return (lax.broadcasted_iota(jnp.int32, (size, places.shape[1]), 0) == places).astype(BF16)


def mm(a, b):
    return jnp.dot(a, b, preferred_element_type=F32)


def mm_nt(a, b):
    return lax.dot_general(a, b, (((1,), (1,)), ((), ())), preferred_element_type=F32)


def mm_tn(a, b):
    return lax.dot_general(a, b, (((0,), (0,)), ((), ())), preferred_element_type=F32)


def move_columns(matrix, from_tables, to_tables, width, row, riders):
    counts = [table.shape[1] for table in from_tables]
    picked = mm(matrix, one_hot(table_row(np.concatenate(from_tables, 1), row), matrix.shape[1])).astype(BF16)
    slabs, others, at = [], [], 0
    for k, count in enumerate(counts):
        slab = picked[:, at : at + count]
        at += count
        if k == 0:
            slabs.append(slab)
            others.append(riders[0])
        else:
            both = swap(jnp.concatenate([riders[k], slab], axis=1), "row", k)
            others.append(both[:, : riders[k].shape[1]])
            slabs.append(both[:, riders[k].shape[1] :])
    moved = mm_nt(jnp.concatenate(slabs, axis=1), one_hot(table_row(np.concatenate(to_tables, 1), row), width))
    return moved.astype(BF16), others


def positions(start, shape, dim, block, col):
    at = lax.broadcasted_iota(jnp.int32, shape, dim) + start
    shift = block.bit_length() - 1
    return lax.shift_left(lax.shift_right_logical(at, shift), shift + 1) + (at & (block - 1)) + col * block


def segments(pos, scal_ref):
    first = scal_ref[2]
    return (pos >= first).astype(jnp.int32) + (pos >= first + scal_ref[3]).astype(jnp.int32)


def mask_bias(scal_ref, query_at, query_shape, query_dim, key_shape, key_dim, block, key_col):
    query_pos = positions(query_at, query_shape, query_dim, block, scal_ref[1])
    key_pos = positions(0, key_shape, key_dim, block, key_col)
    allowed = (key_pos <= query_pos) & (segments(key_pos, scal_ref) == segments(query_pos, scal_ref))
    return jnp.where(allowed, 0.0, MASKED)


def in_order(source_ref, target_ref, row, blocks, block):
    for j in range(blocks):
        target_ref[j * block : (j + 1) * block, :] = source_ref[j ^ row]


def forward_kernel(blocks, block, heads, scal_ref, q_ref, kv0_ref, kv1_ref, out_ref, lse_ref, q_s, kv0_s, kv1_s, o_s):
    row = scal_ref[0]
    width = heads * HEAD_DIM
    in_order(q_ref, q_s, row, blocks, block)
    in_order(kv0_ref, kv0_s, row, blocks, block)
    in_order(kv1_ref, kv1_s, row, blocks, block)
    own = scal_ref[1]
    for i in range(blocks * block // CHUNK):
        span = slice(i * CHUNK, (i + 1) * CHUNK)
        keys = (i + 1) * CHUNK
        shape = (CHUNK, keys)
        bias0 = mask_bias(scal_ref, i * CHUNK, (CHUNK, 1), 0, (1, keys), 1, block, own)
        bias1 = mask_bias(scal_ref, i * CHUNK, (CHUNK, 1), 0, (1, keys), 1, block, 1 - own)
        for h in range(heads):
            at = slice(h * HEAD_DIM, (h + 1) * HEAD_DIM)
            va = slice(width + h * HEAD_DIM, width + (h + 1) * HEAD_DIM)
            query = q_s[span, at]
            s0 = mm_nt(query, kv0_s[:keys, at]) + bias0
            s1 = mm_nt(query, kv1_s[:keys, at]) + bias1
            top = jnp.maximum(jnp.max(s0, axis=1, keepdims=True), jnp.max(s1, axis=1, keepdims=True))
            e0 = jnp.exp(s0 - top)
            e1 = jnp.exp(s1 - top)
            total = jnp.sum(e0, axis=1, keepdims=True) + jnp.sum(e1, axis=1, keepdims=True)
            result = mm(e0.astype(BF16), kv0_s[:keys, va]) + mm(e1.astype(BF16), kv1_s[:keys, va])
            o_s[span, at] = (result / total).astype(BF16)
            lse_ref[span, h : h + 1] = top + jnp.log(total)
    for j in range(blocks):
        out_ref[j ^ row] = o_s[j * block : (j + 1) * block, :]


def backward_kernel(
    blocks,
    block,
    heads,
    scal_ref,
    q_ref,
    kv0_ref,
    kv1_ref,
    g_ref,
    lse_ref,
    dq_ref,
    own_ref,
    other_ref,
    q_s,
    kv0_s,
    kv1_s,
    g_s,
    dq_s,
    d0_s,
    d1_s,
):
    row = scal_ref[0]
    width = heads * HEAD_DIM
    in_order(q_ref, q_s, row, blocks, block)
    in_order(kv0_ref, kv0_s, row, blocks, block)
    in_order(kv1_ref, kv1_s, row, blocks, block)
    in_order(g_ref, g_s, row, blocks, block)
    own = scal_ref[1]
    chunks = blocks * block // CHUNK
    for i in reversed(range(chunks)):
        span = slice(i * CHUNK, (i + 1) * CHUNK)
        keys = (i + 1) * CHUNK
        bias0 = mask_bias(scal_ref, i * CHUNK, (1, CHUNK), 1, (keys, 1), 0, block, own)
        bias1 = mask_bias(scal_ref, i * CHUNK, (1, CHUNK), 1, (keys, 1), 0, block, 1 - own)
        for h in range(heads):
            at = slice(h * HEAD_DIM, (h + 1) * HEAD_DIM)
            va = slice(width + h * HEAD_DIM, width + (h + 1) * HEAD_DIM)
            query = q_s[span, at]
            grad = g_s[span, at]
            lse = lse_ref[h : h + 1, span]
            p0 = jnp.exp(mm_nt(kv0_s[:keys, at], query) + bias0 - lse)
            p1 = jnp.exp(mm_nt(kv1_s[:keys, at], query) + bias1 - lse)
            dp0 = mm_nt(kv0_s[:keys, va], grad)
            dp1 = mm_nt(kv1_s[:keys, va], grad)
            delta = jnp.sum(p0 * dp0, axis=0, keepdims=True) + jnp.sum(p1 * dp1, axis=0, keepdims=True)
            ds0 = (p0 * (dp0 - delta)).astype(BF16)
            ds1 = (p1 * (dp1 - delta)).astype(BF16)
            if i == chunks - 1:
                d0_s[:keys, at] = mm(ds0, query)
                d1_s[:keys, at] = mm(ds1, query)
                d0_s[:keys, va] = mm(p0.astype(BF16), grad)
                d1_s[:keys, va] = mm(p1.astype(BF16), grad)
            else:
                d0_s[:keys, at] += mm(ds0, query)
                d1_s[:keys, at] += mm(ds1, query)
                d0_s[:keys, va] += mm(p0.astype(BF16), grad)
                d1_s[:keys, va] += mm(p1.astype(BF16), grad)
            dquery = mm_tn(ds0, kv0_s[:keys, at]) + mm_tn(ds1, kv1_s[:keys, at])
            dq_s[span, at] = (dquery * HEAD_DIM ** (-0.5)).astype(BF16)
    for j in range(blocks):
        piece = slice(j * block, (j + 1) * block)
        dq_ref[j ^ row] = dq_s[piece, :]
        own_ref[j ^ row] = d0_s[piece, :]
        other_ref[j ^ row] = d1_s[piece, :].astype(BF16)


def vmem():
    return pl.BlockSpec(memory_space=pltpu.VMEM)


def smem():
    return pl.BlockSpec(memory_space=pltpu.SMEM)


def attend_forward(scal, queries, kv_own, kv_other, heads):
    blocks, block, width = queries.shape
    tokens = blocks * block
    return pl.pallas_call(
        functools.partial(forward_kernel, blocks, block, heads),
        out_shape=(
            jax.ShapeDtypeStruct((blocks, block, width), BF16),
            jax.ShapeDtypeStruct((tokens, heads), F32),
        ),
        in_specs=[smem(), vmem(), vmem(), vmem()],
        out_specs=(vmem(), vmem()),
        scratch_shapes=[
            pltpu.VMEM((tokens, width), BF16),
            pltpu.VMEM((tokens, 2 * width), BF16),
            pltpu.VMEM((tokens, 2 * width), BF16),
            pltpu.VMEM((tokens, width), BF16),
        ],
        compiler_params=pltpu.CompilerParams(vmem_limit_bytes=40 * 2**20),
        cost_estimate=pl.CostEstimate(
            flops=4 * tokens * 3 * tokens // 2 * width, bytes_accessed=6 * tokens * width * 2, transcendentals=heads * tokens * tokens
        ),
        name="attend_forward",
    )(scal, queries, kv_own, kv_other)


def attend_backward(scal, queries, kv_own, kv_other, grads, lse, heads):
    blocks, block, width = queries.shape
    tokens = blocks * block
    return pl.pallas_call(
        functools.partial(backward_kernel, blocks, block, heads),
        out_shape=(
            jax.ShapeDtypeStruct((blocks, block, width), BF16),
            jax.ShapeDtypeStruct((blocks, block, 2 * width), F32),
            jax.ShapeDtypeStruct((blocks, block, 2 * width), BF16),
        ),
        in_specs=[smem(), vmem(), vmem(), vmem(), vmem(), vmem()],
        out_specs=(vmem(), vmem(), vmem()),
        scratch_shapes=[
            pltpu.VMEM((tokens, width), BF16),
            pltpu.VMEM((tokens, 2 * width), BF16),
            pltpu.VMEM((tokens, 2 * width), BF16),
            pltpu.VMEM((tokens, width), BF16),
            pltpu.VMEM((tokens, width), BF16),
            pltpu.VMEM((tokens, 2 * width), F32),
            pltpu.VMEM((tokens, 2 * width), F32),
        ],
        compiler_params=pltpu.CompilerParams(vmem_limit_bytes=44 * 2**20),
        cost_estimate=pl.CostEstimate(
            flops=10 * tokens * 3 * tokens // 2 * width, bytes_accessed=14 * tokens * width * 2, transcendentals=heads * tokens * tokens
        ),
        name="attend_backward",
    )(scal, queries, kv_own, kv_other, grads, lse)


def norm_parts(resid_in):
    mean_value = jnp.sum(resid_in, axis=1, keepdims=True) / D
    square = jnp.sum(resid_in * resid_in, axis=1, keepdims=True) / D
    inverse = lax.rsqrt(square - mean_value * mean_value + EPSILON)
    return ((resid_in - mean_value) * inverse, inverse)


def norm_back(grad_in, normal, inverse, norm_gain):
    scaled = grad_in * norm_gain
    mean_scaled = jnp.sum(scaled, axis=1, keepdims=True) / D
    mean_cross = jnp.sum(scaled * normal, axis=1, keepdims=True) / D
    return inverse * (scaled - mean_scaled - normal * mean_cross)


def gelu_tanh(pre_value):
    return jax.nn.gelu(pre_value, approximate=True)


def on_device(
    tokens,
    lengths,
    first_gain,
    first_shift,
    qkv_weight,
    query_bias,
    value_bias,
    out_weight,
    out_bias,
    second_gain,
    second_shift,
    up_weight,
    up_bias,
    down_weight,
    down_bias,
    cotangent,
):
    rows = lax.axis_size("row")
    row = lax.axis_index("row")
    col = lax.axis_index("col")
    half = tokens.shape[1]
    block = tokens.shape[0] // 2
    heads = most_heads(rows)
    width = heads * HEAD_DIM

    def halves(blocks):
        mine = jnp.concatenate([share_of(item, col, 2) for item in blocks], axis=0)
        other = jnp.concatenate([share_of(item, 1 - col, 2) for item in blocks], axis=0)
        return jnp.concatenate([mine, swap(other, "col", 1)], axis=1)

    def unhalves(matrix):
        mine = matrix[:, :half]
        other = swap(matrix[:, half:], "col", 1)
        return jnp.concatenate([jnp.where(col == 0, mine, other), jnp.where(col == 0, other, mine)], axis=0)

    dps = lax.axis_size("dp")
    dp = lax.axis_index("dp")

    def over_cols(left, right, *others):
        other = after(mm_tn(left[:, half:], right).astype(BF16), *others)
        other = swap(other, "col", 1)
        return (mm_tn(left[:, :half], right) + other.astype(F32)).astype(BF16)

    def over_dp(matrix, *others):
        shares = [share_of(matrix, dp ^ k, dps) for k in range(dps)]
        return scatter_sum([after(shares[0].astype(F32), *others)] + shares[1:], "dp")

    x_blocks = gather_blocks(tokens, "row", 4)
    x_first = halves(x_blocks[: rows // 2])
    x_own = x_first[:block]
    x_all = jnp.concatenate([x_first, halves(x_blocks[rows // 2 :])], axis=0).astype(F32)

    vectors = jnp.stack([first_gain, first_shift, out_bias, second_gain, second_shift, down_bias])
    vectors = jnp.concatenate([vectors, swap(after(vectors, x_blocks[1]), "col", 1)], axis=1)
    gain1, shift1, out_b, gain2, shift2, down_b = [vectors[i] for i in range(6)]

    qkv_moves = move_tables(rows, [(3, 0, 0)])
    share = share_of(qkv_weight, dp, dps)
    out_share = share_of(out_weight.T, dp, dps)
    share, out_share = move_columns(share, [m[1] for m in qkv_moves], [m[0] for m in qkv_moves], 3 * width, row, [out_share] * rows)
    share = after(share, x_blocks[1])
    qkv_blocks = gather_blocks(share, "dp")
    qkv_head = by_index(qkv_blocks, dp)
    qkv_other = swap(qkv_head, "col", 1)
    w_qkv = jnp.concatenate([qkv_head, qkv_other], axis=0)

    out_share = jnp.concatenate(out_share, axis=1)
    windows = window_columns(rows, 1)
    out_shard = D // rows
    relative = np.full((rows, rows * width), -1, np.int32)
    for r in range(rows):
        for k in range(rows):
            held = windows[r ^ k]
            relative[r, k * width : (k + 1) * width] = np.where(held >= 0, ((held // out_shard) ^ r) * out_shard + held % out_shard, -1)
    out_share = mm(out_share, one_hot(table_row(relative, row), D)).astype(BF16)
    out_blocks = gather_blocks(after(out_share, qkv_blocks[dps - 1]), "dp", 4)

    starts = jnp.asarray(np.array(head_starts(rows), np.int32))
    head_at = starts[row] * HEAD_DIM
    live_cols = jnp.arange(width, dtype=jnp.int32) < (starts[row + 1] - starts[row]) * HEAD_DIM

    def bias_window(vector):
        padded = jnp.concatenate([vector, jnp.zeros((width,), F32)])
        return jnp.where(live_cols, lax.dynamic_slice_in_dim(padded, head_at, width), 0.0)

    normal1, inverse1 = norm_parts(x_all)
    normed1 = after((normal1 * gain1 + shift1).astype(BF16), out_share)
    kv_own = mm(normed1, w_qkv[:, width:])
    bias_kv = jnp.concatenate([jnp.zeros((width,), F32), bias_window(value_bias)])
    kv_own = (kv_own + bias_kv).astype(BF16)
    kv_other = swap(kv_own, "col", 1)
    queries = mm(normed1, w_qkv[:, :width])
    queries = (queries + bias_window(query_bias)).astype(BF16) * BF16(HEAD_DIM ** (-0.5))
    queries = queries.reshape(rows, block, width)
    kv_own = kv_own.reshape(rows, block, 2 * width)
    kv_other = kv_other.reshape(rows, block, 2 * width)
    scal = jnp.stack([row.astype(jnp.int32), col.astype(jnp.int32), lengths[0, 0], lengths[0, 1]])

    def live_rows(matrix, start):
        live = start + jnp.arange(matrix.shape[0], dtype=jnp.int32) < lengths[0, 0] + lengths[0, 1]
        return jnp.where(live[:, None], matrix, 0.0)

    grad_out = live_rows(halves([after(cotangent, x_blocks[rows - 1])]), (row * 2 + col) * block)
    grad_out_low = grad_out.astype(BF16)
    g_blocks = lax.all_gather(after(grad_out_low, kv_other), "row", tiled=True)

    attention, lse = attend_forward(scal, queries, kv_own, kv_other, heads)

    att_blocks = send_blocks([attention[k] for k in range(rows)], "row")
    att_own = jnp.concatenate(att_blocks, axis=1)
    out_head = by_index([after(item, *att_blocks[1:]) for item in out_blocks], dp)
    w_out = jnp.concatenate([out_head, swap(out_head, "col", 1)], axis=0)
    resid_mid = x_own.astype(F32) + (mm_nt(att_own, w_out) + out_b)

    normal2, inverse2 = norm_parts(resid_mid)
    normed2 = (normal2 * gain2 + shift2).astype(BF16)
    mlp_in = jnp.concatenate(gather_blocks(normed2, "row", 4), axis=0)
    up_own = after(up_weight, att_blocks[1])
    down_own = after(down_weight, att_blocks[1])
    w_up = jnp.concatenate([up_own, swap(up_own, "col", 1)], axis=0)
    w_down = jnp.concatenate([down_own, swap(down_own, "col", 1)], axis=1)
    g_blocks = after(g_blocks, normed2)
    g_all = jnp.concatenate([share_of(g_blocks, row ^ k, rows) for k in range(rows)], axis=0)
    down_bias_part = jnp.sum(grad_out_low.astype(F32), axis=0)

    pre_act = mm(mlp_in, w_up) + up_bias
    act, gelu_back = jax.vjp(gelu_tanh, pre_act)
    grad_act = mm_nt(g_all, w_down)
    act, grad_pre = lax.optimization_barrier((act.astype(BF16), gelu_back(grad_act)[0].astype(BF16)))
    up_bias_part = jnp.sum(grad_pre.astype(F32), axis=0)
    grad_normed2 = mm_nt(grad_pre, w_up)

    late_g, late_act, late_in, late_pre, _ = lax.optimization_barrier((g_all, act, mlp_in, grad_pre, grad_normed2))
    down_grad = over_cols(late_g, late_act)
    up_grad = over_cols(late_in, late_pre)

    blocks = rows_of(grad_normed2, rows)
    grad_normed2 = scatter_sum([after(blocks[0], down_grad, up_grad)] + blocks[1:], "row")
    second_gain_part = jnp.sum(grad_normed2 * normal2, axis=0)
    second_shift_part = jnp.sum(grad_normed2, axis=0)
    grad_mid = grad_out + norm_back(grad_normed2, normal2, inverse2, gain2)
    grad_mid_low = grad_mid.astype(BF16)
    out_bias_part = jnp.sum(grad_mid_low.astype(F32), axis=0)

    grad_att = mm(grad_mid_low, w_out).astype(BF16)
    grad_att = jnp.stack(send_blocks([grad_att[:, k * width : (k + 1) * width] for k in range(rows)], "row"))
    att_shards = mm_nt(after(att_own, down_grad), one_hot(table_row(relative, row), D)).astype(BF16)
    out_other = mm_tn(grad_mid_low[:, half:], att_shards).astype(BF16)
    out_grad = mm_tn(grad_mid_low[:, :half], att_shards)
    out_grad = (out_grad + swap(out_other, "col", 1).astype(F32)).astype(BF16)
    grad_att = after(grad_att, out_grad)
    up_grad, down_grad = lax.psum((up_grad, down_grad), "dp")

    dq, dkv_own, dkv_other = attend_backward(scal, queries, kv_own, kv_other, grad_att, lse.T, heads)
    dkv = (dkv_own + swap(dkv_other, "col", 1).astype(F32)).astype(BF16)
    out_grad = over_dp(out_grad)
    grad_qkv = after(jnp.concatenate([dq, dkv], axis=2).reshape(-1, 3 * width), out_grad)
    qkv_bias_part = jnp.sum(grad_qkv.astype(F32), axis=0)
    normed_part = mm_nt(grad_qkv, w_qkv)
    first_gain_part = jnp.sum(normed_part * normal1, axis=0)
    first_shift_part = jnp.sum(normed_part, axis=0)
    qkv_grad = over_cols(normed1, after(grad_qkv, normed_part))
    def place(vector):
        mine, other = vector[:half], vector[half:]
        return jnp.concatenate([jnp.where(col == 0, mine, other), jnp.where(col == 0, other, mine)])

    def place_window(vector):
        padded = lax.dynamic_update_slice_in_dim(jnp.zeros((D + width,), F32), vector, head_at, 0)
        return padded[:D]

    def place_rows(vector):
        return lax.dynamic_update_slice_in_dim(jnp.zeros((FF,), F32), vector, row * vector.shape[0], 0)

    small = jnp.concatenate(
        [
            place_rows(up_bias_part),
            place(down_bias_part),
            place(second_gain_part),
            place(second_shift_part),
            place(out_bias_part),
            place(first_gain_part),
            place(first_shift_part),
            place_window(qkv_bias_part[:width]),
            place_window(qkv_bias_part[2 * width :]),
        ]
    )

    def in_rows(vector, size):
        count = -(-vector.shape[0] // (16 * size)) * 16
        return jnp.pad(vector, (0, count * size - vector.shape[0])).reshape(count, size)

    small = in_rows(small, D)
    blocks = rows_of(normed_part, rows)
    own_block = jnp.concatenate([after(blocks[0], qkv_grad), small], axis=0)
    sent = [jnp.concatenate([item.astype(BF16), small.astype(BF16)], axis=0) for item in blocks[1:]]
    grad_normed1 = scatter_sum([own_block] + sent, "row")
    small = grad_normed1[block:]
    grad_normed1 = grad_normed1[:block]
    back1 = norm_back(grad_normed1, normal1[:block], inverse1[:block], gain1)
    input_grad = unhalves(grad_mid + back1)

    qkv_grad = over_dp(qkv_grad).astype(BF16)
    qkv_summed = qkv_grad
    out_grad = out_grad.astype(BF16)
    out_grad = [out_grad[:, k * out_shard : (k + 1) * out_shard] for k in range(rows)]
    qkv_grad, out_grad = move_columns(
        qkv_grad, [m[0] for m in qkv_moves], [m[1] for m in qkv_moves], 3 * out_shard, row, out_grad
    )
    out_grad = sum(item.astype(F32) for item in out_grad).astype(BF16)
    both = jnp.concatenate([qkv_grad, out_grad], axis=1)
    share_rows = both.shape[0]
    small = in_rows(small.reshape(-1), both.shape[1])
    both = gather_blocks(jnp.concatenate([both, small.astype(BF16)], axis=0), "dp")
    small = small + sum(item[share_rows:].astype(F32) for item in both[1:])
    small = (small + swap(small, "col", 1)).reshape(-1)
    both = [item[:share_rows] for item in both]
    both[1], up_grad, down_grad = lax.optimization_barrier((both[1], up_grad, down_grad))
    both = by_index([item.astype(F32) for item in both], dp)
    qkv_grad = both[:, : 3 * out_shard]
    out_grad = both[:, 3 * out_shard :].T

    down_out = mm(act, w_down)
    blocks = rows_of(down_out, rows)
    block_out = scatter_sum([blocks[0]] + [after(item.astype(BF16), input_grad) for item in blocks[1:]], "row")
    block_out = unhalves((resid_mid + (block_out + down_b)).astype(BF16))

    def own_half(part):
        return lax.dynamic_slice_in_dim(small, FF + part * D + col * half, half)

    up_width = up_bias.shape[0]
    return (
        block_out,
        input_grad,
        own_half(4),
        own_half(5),
        qkv_grad,
        small[FF + 6 * D : FF + 7 * D],
        small[FF + 7 * D : FF + 8 * D],
        out_grad,
        own_half(3),
        own_half(1),
        own_half(2),
        up_grad.astype(F32),
        lax.dynamic_slice_in_dim(small, row * up_width, up_width),
        down_grad.T.astype(F32),
        own_half(0),
    )


def solution(mesh):
    in_specs = (
        P(("dp", "row"), "col"),
        P("dp", None),
        P("col"),
        P("col"),
        P("col", "row"),
        P(),
        P(),
        P("row", "col"),
        P("col"),
        P("col"),
        P("col"),
        P("col", "row"),
        P("row"),
        P("row", "col"),
        P("col"),
        P(("dp", "row"), "col"),
    )
    out_specs = (
        P(("dp", "row"), "col"),
        P(("dp", "row"), "col"),
        P("col"),
        P("col"),
        P("col", "row"),
        P(),
        P(),
        P("row", "col"),
        P("col"),
        P("col"),
        P("col"),
        P("col", "row"),
        P("row"),
        P("row", "col"),
        P("col"),
    )
    return jax.shard_map(
        on_device, mesh=mesh, in_specs=in_specs, out_specs=out_specs, check_vma=False
    )
```

```python
import functools

import jax
import jax.numpy as jnp
import numpy as np
from jax import lax
from jax.experimental import pallas as pl
from jax.experimental.pallas import tpu as pltpu
from jax.sharding import PartitionSpec as P

D = 1088
HEADS = 17
HEAD_DIM = 64
FF = 4352
TOK_G = 1024

EPSILON = 1e-05
MASKED = -1e30
CHUNK = 256
BF16 = jnp.bfloat16
F32 = jnp.float32


def swap(payload, axis, distance):
    size = lax.axis_size(axis)
    return lax.ppermute(payload, axis, [(i, i ^ distance) for i in range(size)])


def after(payload, *others):
    return lax.optimization_barrier((payload, *others))[0]


def gather_blocks(payload, axis, relay=0):
    if lax.axis_size(axis) == relay:
        far = swap(payload, axis, 2)
        near = swap(payload, axis, 1)
        return [payload, near, far, swap(far, axis, 1)]
    return [payload] + [swap(payload, axis, k) for k in range(1, lax.axis_size(axis))]


def send_blocks(blocks, axis):
    return [blocks[0]] + [swap(blocks[k], axis, k) for k in range(1, len(blocks))]


def scatter_sum(blocks, axis):
    received = [swap(blocks[k].astype(BF16), axis, k) for k in range(1, len(blocks))]
    total = blocks[0]
    for item in received:
        total = total + item.astype(F32)
    return total


def share_of(matrix, index, parts):
    size = matrix.shape[0] // parts
    return lax.dynamic_slice_in_dim(matrix, index * size, size, 0)


def by_index(blocks, index):
    count = len(blocks)
    total = jnp.zeros((count,) + blocks[0].shape, blocks[0].dtype)
    for k, item in enumerate(blocks):
        total = lax.dynamic_update_index_in_dim(total, item, index ^ k, 0)
    return total.reshape((count * blocks[0].shape[0],) + blocks[0].shape[1:])


def rows_of(matrix, parts):
    size = matrix.shape[0] // parts
    return [matrix[k * size : (k + 1) * size] for k in range(parts)]


def head_starts(rows):
    return [int(np.floor(HEADS * r / rows + 0.5)) for r in range(rows + 1)]


def most_heads(rows):
    starts = head_starts(rows)
    return max(b - a for a, b in zip(starts[:-1], starts[1:]))


def window_columns(rows, copies):
    starts = head_starts(rows)
    width = most_heads(rows) * HEAD_DIM
    table = np.full((rows, copies * width), -1, np.int64)
    for r in range(rows):
        count = (starts[r + 1] - starts[r]) * HEAD_DIM
        for t in range(copies):
            table[r, t * width : t * width + count] = t * D + starts[r] * HEAD_DIM + np.arange(count)
    return table


def move_tables(rows, parts):
    moves = []
    for k in range(rows):
        places = [[] for _ in range(rows)]
        columns = [[] for _ in range(rows)]
        for copies, place_at, column_at in parts:
            windows = window_columns(rows, copies)
            shard = copies * D // rows
            for r in range(rows):
                for p in range(windows.shape[1]):
                    if windows[r, p] >= 0 and windows[r, p] // shard == r ^ k:
                        places[r].append(place_at + p)
                        columns[r].append(column_at + int(windows[r, p] % shard))
        longest = -(-max(len(place) for place in places) // 16) * 16
        at = np.full((rows, longest), -1, np.int32)
        frm = np.full((rows, longest), -1, np.int32)
        for r in range(rows):
            at[r, : len(places[r])] = places[r]
            frm[r ^ k, : len(columns[r])] = columns[r]
        moves.append((at, frm))
    return moves


def table_row(table, index):
    return lax.dynamic_index_in_dim(jnp.asarray(table), index, 0, keepdims=True)


def one_hot(places, size):
    return (lax.broadcasted_iota(jnp.int32, (size, places.shape[1]), 0) == places).astype(BF16)


def mm(a, b):
    return jnp.dot(a, b, preferred_element_type=F32)


def mm_nt(a, b):
    return lax.dot_general(a, b, (((1,), (1,)), ((), ())), preferred_element_type=F32)


def mm_tn(a, b):
    return lax.dot_general(a, b, (((0,), (0,)), ((), ())), preferred_element_type=F32)


def move_columns(matrix, from_tables, to_tables, width, row, riders=None):
    counts = [table.shape[1] for table in from_tables]
    picked = mm(matrix, one_hot(table_row(np.concatenate(from_tables, 1), row), matrix.shape[1])).astype(BF16)
    slabs, others, at = [], [], 0
    for k, count in enumerate(counts):
        slab = picked[:, at : at + count]
        at += count
        if k == 0:
            slabs.append(slab)
            others.append(riders and riders[0])
        elif riders is None:
            slabs.append(swap(slab, "row", k) if count else slab)
        else:
            both = swap(jnp.concatenate([riders[k], slab], axis=1), "row", k)
            others.append(both[:, : riders[k].shape[1]])
            slabs.append(both[:, riders[k].shape[1] :])
    moved = mm_nt(jnp.concatenate(slabs, axis=1), one_hot(table_row(np.concatenate(to_tables, 1), row), width))
    return moved.astype(BF16), others


def positions(start, shape, dim, block, col):
    at = lax.broadcasted_iota(jnp.int32, shape, dim) + start
    shift = block.bit_length() - 1
    return lax.shift_left(lax.shift_right_logical(at, shift), shift + 1) + (at & (block - 1)) + col * block


def segments(pos, scal_ref):
    first = scal_ref[2]
    return (pos >= first).astype(jnp.int32) + (pos >= first + scal_ref[3]).astype(jnp.int32)


def mask_bias(scal_ref, query_at, query_shape, query_dim, key_shape, key_dim, block, key_col):
    query_pos = positions(query_at, query_shape, query_dim, block, scal_ref[1])
    key_pos = positions(0, key_shape, key_dim, block, key_col)
    allowed = (key_pos <= query_pos) & (segments(key_pos, scal_ref) == segments(query_pos, scal_ref))
    return jnp.where(allowed, 0.0, MASKED)


def in_order(source_ref, target_ref, row, blocks, block):
    for j in range(blocks):
        target_ref[j * block : (j + 1) * block, :] = source_ref[j ^ row]


def forward_kernel(blocks, block, heads, scal_ref, q_ref, kv0_ref, kv1_ref, out_ref, lse_ref, q_s, kv0_s, kv1_s, o_s):
    row = scal_ref[0]
    width = heads * HEAD_DIM
    in_order(q_ref, q_s, row, blocks, block)
    in_order(kv0_ref, kv0_s, row, blocks, block)
    in_order(kv1_ref, kv1_s, row, blocks, block)
    own = scal_ref[1]
    for i in range(blocks * block // CHUNK):
        span = slice(i * CHUNK, (i + 1) * CHUNK)
        keys = (i + 1) * CHUNK
        shape = (CHUNK, keys)
        bias0 = mask_bias(scal_ref, i * CHUNK, (CHUNK, 1), 0, (1, keys), 1, block, own)
        bias1 = mask_bias(scal_ref, i * CHUNK, (CHUNK, 1), 0, (1, keys), 1, block, 1 - own)
        for h in range(heads):
            at = slice(h * HEAD_DIM, (h + 1) * HEAD_DIM)
            va = slice(width + h * HEAD_DIM, width + (h + 1) * HEAD_DIM)
            query = q_s[span, at]
            s0 = mm_nt(query, kv0_s[:keys, at]) + bias0
            s1 = mm_nt(query, kv1_s[:keys, at]) + bias1
            top = jnp.maximum(jnp.max(s0, axis=1, keepdims=True), jnp.max(s1, axis=1, keepdims=True))
            e0 = jnp.exp(s0 - top)
            e1 = jnp.exp(s1 - top)
            total = jnp.sum(e0, axis=1, keepdims=True) + jnp.sum(e1, axis=1, keepdims=True)
            result = mm(e0.astype(BF16), kv0_s[:keys, va]) + mm(e1.astype(BF16), kv1_s[:keys, va])
            o_s[span, at] = (result / total).astype(BF16)
            lse_ref[span, h : h + 1] = top + jnp.log(total)
    for j in range(blocks):
        out_ref[j ^ row] = o_s[j * block : (j + 1) * block, :]


def backward_kernel(
    blocks,
    block,
    heads,
    scal_ref,
    q_ref,
    kv0_ref,
    kv1_ref,
    g_ref,
    lse_ref,
    dq_ref,
    own_ref,
    other_ref,
    q_s,
    kv0_s,
    kv1_s,
    g_s,
    dq_s,
    d0_s,
    d1_s,
):
    row = scal_ref[0]
    width = heads * HEAD_DIM
    in_order(q_ref, q_s, row, blocks, block)
    in_order(kv0_ref, kv0_s, row, blocks, block)
    in_order(kv1_ref, kv1_s, row, blocks, block)
    in_order(g_ref, g_s, row, blocks, block)
    own = scal_ref[1]
    chunks = blocks * block // CHUNK
    for i in reversed(range(chunks)):
        span = slice(i * CHUNK, (i + 1) * CHUNK)
        keys = (i + 1) * CHUNK
        bias0 = mask_bias(scal_ref, i * CHUNK, (1, CHUNK), 1, (keys, 1), 0, block, own)
        bias1 = mask_bias(scal_ref, i * CHUNK, (1, CHUNK), 1, (keys, 1), 0, block, 1 - own)
        for h in range(heads):
            at = slice(h * HEAD_DIM, (h + 1) * HEAD_DIM)
            va = slice(width + h * HEAD_DIM, width + (h + 1) * HEAD_DIM)
            query = q_s[span, at]
            grad = g_s[span, at]
            lse = lse_ref[h : h + 1, span]
            p0 = jnp.exp(mm_nt(kv0_s[:keys, at], query) + bias0 - lse)
            p1 = jnp.exp(mm_nt(kv1_s[:keys, at], query) + bias1 - lse)
            dp0 = mm_nt(kv0_s[:keys, va], grad)
            dp1 = mm_nt(kv1_s[:keys, va], grad)
            delta = jnp.sum(p0 * dp0, axis=0, keepdims=True) + jnp.sum(p1 * dp1, axis=0, keepdims=True)
            ds0 = (p0 * (dp0 - delta)).astype(BF16)
            ds1 = (p1 * (dp1 - delta)).astype(BF16)
            if i == chunks - 1:
                d0_s[:keys, at] = mm(ds0, query)
                d1_s[:keys, at] = mm(ds1, query)
                d0_s[:keys, va] = mm(p0.astype(BF16), grad)
                d1_s[:keys, va] = mm(p1.astype(BF16), grad)
            else:
                d0_s[:keys, at] += mm(ds0, query)
                d1_s[:keys, at] += mm(ds1, query)
                d0_s[:keys, va] += mm(p0.astype(BF16), grad)
                d1_s[:keys, va] += mm(p1.astype(BF16), grad)
            dquery = mm_tn(ds0, kv0_s[:keys, at]) + mm_tn(ds1, kv1_s[:keys, at])
            dq_s[span, at] = (dquery * HEAD_DIM ** (-0.5)).astype(BF16)
    for j in range(blocks):
        piece = slice(j * block, (j + 1) * block)
        dq_ref[j ^ row] = dq_s[piece, :]
        own_ref[j ^ row] = d0_s[piece, :]
        other_ref[j ^ row] = d1_s[piece, :].astype(BF16)


def vmem():
    return pl.BlockSpec(memory_space=pltpu.VMEM)


def smem():
    return pl.BlockSpec(memory_space=pltpu.SMEM)


def attend_forward(scal, queries, kv_own, kv_other, heads):
    blocks, block, width = queries.shape
    tokens = blocks * block
    return pl.pallas_call(
        functools.partial(forward_kernel, blocks, block, heads),
        out_shape=(
            jax.ShapeDtypeStruct((blocks, block, width), BF16),
            jax.ShapeDtypeStruct((tokens, heads), F32),
        ),
        in_specs=[smem(), vmem(), vmem(), vmem()],
        out_specs=(vmem(), vmem()),
        scratch_shapes=[
            pltpu.VMEM((tokens, width), BF16),
            pltpu.VMEM((tokens, 2 * width), BF16),
            pltpu.VMEM((tokens, 2 * width), BF16),
            pltpu.VMEM((tokens, width), BF16),
        ],
        compiler_params=pltpu.CompilerParams(vmem_limit_bytes=40 * 2**20),
        cost_estimate=pl.CostEstimate(
            flops=4 * tokens * 3 * tokens // 2 * width, bytes_accessed=6 * tokens * width * 2, transcendentals=heads * tokens * tokens
        ),
        name="attend_forward",
    )(scal, queries, kv_own, kv_other)


def attend_backward(scal, queries, kv_own, kv_other, grads, lse, heads):
    blocks, block, width = queries.shape
    tokens = blocks * block
    return pl.pallas_call(
        functools.partial(backward_kernel, blocks, block, heads),
        out_shape=(
            jax.ShapeDtypeStruct((blocks, block, width), BF16),
            jax.ShapeDtypeStruct((blocks, block, 2 * width), F32),
            jax.ShapeDtypeStruct((blocks, block, 2 * width), BF16),
        ),
        in_specs=[smem(), vmem(), vmem(), vmem(), vmem(), vmem()],
        out_specs=(vmem(), vmem(), vmem()),
        scratch_shapes=[
            pltpu.VMEM((tokens, width), BF16),
            pltpu.VMEM((tokens, 2 * width), BF16),
            pltpu.VMEM((tokens, 2 * width), BF16),
            pltpu.VMEM((tokens, width), BF16),
            pltpu.VMEM((tokens, width), BF16),
            pltpu.VMEM((tokens, 2 * width), F32),
            pltpu.VMEM((tokens, 2 * width), F32),
        ],
        compiler_params=pltpu.CompilerParams(vmem_limit_bytes=44 * 2**20),
        cost_estimate=pl.CostEstimate(
            flops=10 * tokens * 3 * tokens // 2 * width, bytes_accessed=14 * tokens * width * 2, transcendentals=heads * tokens * tokens
        ),
        name="attend_backward",
    )(scal, queries, kv_own, kv_other, grads, lse)


def norm_parts(resid_in):
    mean_value = jnp.sum(resid_in, axis=1, keepdims=True) / D
    square = jnp.sum(resid_in * resid_in, axis=1, keepdims=True) / D
    inverse = lax.rsqrt(square - mean_value * mean_value + EPSILON)
    return ((resid_in - mean_value) * inverse, inverse)


def norm_back(grad_in, normal, inverse, norm_gain):
    scaled = grad_in * norm_gain
    mean_scaled = jnp.sum(scaled, axis=1, keepdims=True) / D
    mean_cross = jnp.sum(scaled * normal, axis=1, keepdims=True) / D
    return inverse * (scaled - mean_scaled - normal * mean_cross)


def gelu_tanh(pre_value):
    return jax.nn.gelu(pre_value, approximate=True)


def on_device(
    tokens,
    lengths,
    first_gain,
    first_shift,
    qkv_weight,
    query_bias,
    value_bias,
    out_weight,
    out_bias,
    second_gain,
    second_shift,
    up_weight,
    up_bias,
    down_weight,
    down_bias,
    cotangent,
):
    rows = lax.axis_size("row")
    row = lax.axis_index("row")
    col = lax.axis_index("col")
    half = tokens.shape[1]
    block = tokens.shape[0] // 2
    heads = most_heads(rows)
    width = heads * HEAD_DIM

    def halves(blocks):
        mine = jnp.concatenate([share_of(item, col, 2) for item in blocks], axis=0)
        other = jnp.concatenate([share_of(item, 1 - col, 2) for item in blocks], axis=0)
        return jnp.concatenate([mine, swap(other, "col", 1)], axis=1)

    def unhalves(matrix):
        mine = matrix[:, :half]
        other = swap(matrix[:, half:], "col", 1)
        return jnp.concatenate([jnp.where(col == 0, mine, other), jnp.where(col == 0, other, mine)], axis=0)

    dps = lax.axis_size("dp")
    dp = lax.axis_index("dp")

    def over_cols(left, right, *others):
        other = after(mm_tn(left[:, half:], right).astype(BF16), *others)
        other = swap(other, "col", 1)
        return (mm_tn(left[:, :half], right) + other.astype(F32)).astype(BF16)

    def over_dp(matrix, *others):
        shares = [share_of(matrix, dp ^ k, dps) for k in range(dps)]
        return scatter_sum([after(shares[0].astype(F32), *others)] + shares[1:], "dp")

    x_blocks = gather_blocks(tokens, "row", 4)
    x_first = halves(x_blocks[: rows // 2])
    x_own = x_first[:block]
    x_all = jnp.concatenate([x_first, halves(x_blocks[rows // 2 :])], axis=0).astype(F32)

    vectors = jnp.stack([first_gain, first_shift, out_bias, second_gain, second_shift, down_bias])
    vectors = jnp.concatenate([vectors, swap(after(vectors, x_blocks[1]), "col", 1)], axis=1)
    gain1, shift1, out_b, gain2, shift2, down_b = [vectors[i] for i in range(6)]

    qkv_moves = move_tables(rows, [(3, 0, 0)])
    share = share_of(qkv_weight, dp, dps)
    share, _ = move_columns(share, [m[1] for m in qkv_moves], [m[0] for m in qkv_moves], 3 * width, row)
    share = after(share, x_blocks[1])
    qkv_blocks = gather_blocks(share, "dp")
    qkv_head = by_index(qkv_blocks, dp)
    qkv_other = swap(qkv_head, "col", 1)
    w_qkv = jnp.concatenate([qkv_head, qkv_other], axis=0)

    if out_weight.shape[0] % dps == 0:
        out_all = lax.all_gather(share_of(out_weight, dp, dps), ("row", "dp"), axis=0, tiled=True)
    else:
        out_all = lax.all_gather(out_weight, "row", axis=0, tiled=True)
    windows = window_columns(rows, 1)
    out_shard = D // rows
    absolute = np.concatenate([windows[np.arange(rows) ^ k] for k in range(rows)], axis=1).astype(np.int32)
    shard_at = (absolute // out_shard) ^ np.arange(rows)[:, None]
    relative = np.where(absolute >= 0, shard_at * out_shard + absolute % out_shard, -1).astype(np.int32)

    starts = jnp.asarray(np.array(head_starts(rows), np.int32))
    head_at = starts[row] * HEAD_DIM
    live_cols = jnp.arange(width, dtype=jnp.int32) < (starts[row + 1] - starts[row]) * HEAD_DIM

    def bias_window(vector):
        padded = jnp.concatenate([vector, jnp.zeros((width,), F32)])
        return jnp.where(live_cols, lax.dynamic_slice_in_dim(padded, head_at, width), 0.0)

    normal1, inverse1 = norm_parts(x_all)
    normed1 = (normal1 * gain1 + shift1).astype(BF16)
    kv_own = mm(normed1, w_qkv[:, width:])
    bias_kv = jnp.concatenate([jnp.zeros((width,), F32), bias_window(value_bias)])
    kv_own = (kv_own + bias_kv).astype(BF16)
    kv_other = swap(kv_own, "col", 1)
    queries = mm(normed1, w_qkv[:, :width])
    queries = (queries + bias_window(query_bias)).astype(BF16) * BF16(HEAD_DIM ** (-0.5))
    queries = queries.reshape(rows, block, width)
    kv_own = kv_own.reshape(rows, block, 2 * width)
    kv_other = kv_other.reshape(rows, block, 2 * width)
    scal = jnp.stack([row.astype(jnp.int32), col.astype(jnp.int32), lengths[0, 0], lengths[0, 1]])

    def live_rows(matrix, start):
        live = start + jnp.arange(matrix.shape[0], dtype=jnp.int32) < lengths[0, 0] + lengths[0, 1]
        return jnp.where(live[:, None], matrix, 0.0)

    grad_out = live_rows(halves([after(cotangent, x_blocks[rows - 1])]), (row * 2 + col) * block)
    grad_out_low = grad_out.astype(BF16)
    g_blocks = lax.all_gather(grad_out_low, "row", tiled=True)
    queries = after(queries, grad_out_low)

    attention, lse = attend_forward(scal, queries, kv_own, kv_other, heads)

    att_blocks = send_blocks([attention[k] for k in range(rows)], "row")
    att_own = jnp.concatenate(att_blocks, axis=1)
    out_all = after(out_all, attention)
    w_out = jnp.concatenate([out_all.T, swap(out_all, "col", 1).T], axis=0)
    to_heads = one_hot(table_row(absolute, row), D)
    att_all = mm_nt(att_own, to_heads).astype(BF16)
    resid_mid = x_own.astype(F32) + (mm_nt(att_all, w_out) + out_b)

    normal2, inverse2 = norm_parts(resid_mid)
    normed2 = (normal2 * gain2 + shift2).astype(BF16)
    mlp_in = jnp.concatenate(gather_blocks(normed2, "row", 4), axis=0)
    up_own = after(up_weight, normed2)
    down_own = after(down_weight, normed2)
    w_up = jnp.concatenate([up_own, swap(up_own, "col", 1)], axis=0)
    w_down = jnp.concatenate([down_own, swap(down_own, "col", 1)], axis=1)
    g_blocks = after(g_blocks, normed2)
    g_all = jnp.concatenate([share_of(g_blocks, row ^ k, rows) for k in range(rows)], axis=0)
    down_bias_part = jnp.sum(grad_out_low.astype(F32), axis=0)

    pre_act = mm(mlp_in, w_up) + up_bias
    act, gelu_back = jax.vjp(gelu_tanh, pre_act)
    grad_act = mm_nt(g_all, w_down)
    act, grad_pre = lax.optimization_barrier((act.astype(BF16), gelu_back(grad_act)[0].astype(BF16)))
    up_bias_part = jnp.sum(grad_pre.astype(F32), axis=0)
    grad_normed2 = mm_nt(grad_pre, w_up)

    late_g, late_act, late_in, late_pre, _ = lax.optimization_barrier((g_all, act, mlp_in, grad_pre, grad_normed2))
    down_grad = over_cols(late_g, late_act)
    up_grad = over_cols(late_in, late_pre)

    blocks = rows_of(grad_normed2, rows)
    grad_normed2 = scatter_sum([after(blocks[0], down_grad, up_grad)] + blocks[1:], "row")
    second_gain_part = jnp.sum(grad_normed2 * normal2, axis=0)
    second_shift_part = jnp.sum(grad_normed2, axis=0)
    grad_mid = grad_out + norm_back(grad_normed2, normal2, inverse2, gain2)
    grad_mid_low = grad_mid.astype(BF16)
    out_bias_part = jnp.sum(grad_mid_low.astype(F32), axis=0)

    grad_att = mm(grad_mid_low, w_out).astype(BF16)
    grad_att = mm(grad_att, to_heads).astype(BF16)
    grad_att = jnp.stack(send_blocks([grad_att[:, k * width : (k + 1) * width] for k in range(rows)], "row"))
    att_shards = mm_nt(after(att_own, down_grad), one_hot(table_row(relative, row), D)).astype(BF16)
    out_other = mm_tn(grad_mid_low[:, half:], att_shards).astype(BF16)
    out_grad = mm_tn(grad_mid_low[:, :half], att_shards)
    out_grad = (out_grad + swap(out_other, "col", 1).astype(F32)).astype(BF16)
    grad_att = after(grad_att, out_grad, up_bias_part)
    up_grad, down_grad = lax.psum((up_grad, down_grad), "dp")

    dq, dkv_own, dkv_other = attend_backward(scal, queries, kv_own, kv_other, grad_att, lse.T, heads)
    dkv = (dkv_own + swap(dkv_other, "col", 1).astype(F32)).astype(BF16)
    grad_qkv = jnp.concatenate([dq, dkv], axis=2).reshape(-1, 3 * width)
    qkv_bias_part = jnp.sum(grad_qkv.astype(F32), axis=0)
    normed_part = mm_nt(grad_qkv, w_qkv)
    first_gain_part = jnp.sum(normed_part * normal1, axis=0)
    first_shift_part = jnp.sum(normed_part, axis=0)
    qkv_grad = over_cols(normed1, after(grad_qkv, normed_part))
    def place(vector):
        mine, other = vector[:half], vector[half:]
        return jnp.concatenate([jnp.where(col == 0, mine, other), jnp.where(col == 0, other, mine)])

    def place_window(vector):
        padded = lax.dynamic_update_slice_in_dim(jnp.zeros((D + width,), F32), vector, head_at, 0)
        return padded[:D]

    def place_rows(vector):
        return lax.dynamic_update_slice_in_dim(jnp.zeros((FF,), F32), vector, row * vector.shape[0], 0)

    small = jnp.concatenate(
        [
            place_rows(up_bias_part),
            place(down_bias_part),
            place(second_gain_part),
            place(second_shift_part),
            place(out_bias_part),
            place(first_gain_part),
            place(first_shift_part),
            place_window(qkv_bias_part[:width]),
            place_window(qkv_bias_part[2 * width :]),
        ]
    )
    blocks = rows_of(normed_part, rows)
    grad_normed1 = scatter_sum([after(blocks[0], qkv_grad)] + blocks[1:], "row")
    back1 = norm_back(grad_normed1, normal1[:block], inverse1[:block], gain1)
    input_grad = unhalves(grad_mid + back1)

    summed = over_dp(jnp.concatenate([qkv_grad, out_grad], axis=1)).astype(BF16)
    qkv_grad, out_grad = summed[:, : 3 * width], summed[:, 3 * width :]
    share_rows = qkv_grad.shape[0]
    small_width = -(-small.shape[0] // share_rows)
    small = jnp.pad(small, (0, small_width * share_rows - small.shape[0])).reshape(share_rows, small_width)
    riders = [
        jnp.concatenate([out_grad[:, k * out_shard : (k + 1) * out_shard], small.astype(BF16)], axis=1) for k in range(rows)
    ]
    qkv_grad, riders = move_columns(
        qkv_grad, [m[0] for m in qkv_moves], [m[1] for m in qkv_moves], 3 * out_shard, row, riders
    )
    rider = sum(item.astype(F32) for item in riders).astype(BF16)
    both = gather_blocks(jnp.concatenate([qkv_grad, rider], axis=1), "dp")
    both[1], up_grad, down_grad = lax.optimization_barrier((both[1], up_grad, down_grad))
    small = sum(item[:, 4 * out_shard :].astype(F32) for item in both)
    small = (small + swap(small, "col", 1)).reshape(-1)
    both = [item[:, : 4 * out_shard] for item in both]
    both = by_index([item.astype(F32) for item in both], dp)
    qkv_grad = both[:, : 3 * out_shard]
    out_grad = both[:, 3 * out_shard :].T

    down_out = mm(act, w_down)
    blocks = rows_of(down_out, rows)
    block_out = scatter_sum([after(blocks[0], rider)] + [after(item.astype(BF16), input_grad) for item in blocks[1:]], "row")
    block_out = unhalves((resid_mid + (block_out + down_b)).astype(BF16))

    def own_half(part):
        return lax.dynamic_slice_in_dim(small, FF + part * D + col * half, half)

    up_width = up_bias.shape[0]
    return (
        block_out,
        input_grad,
        own_half(4),
        own_half(5),
        qkv_grad,
        small[FF + 6 * D : FF + 7 * D],
        small[FF + 7 * D : FF + 8 * D],
        out_grad,
        own_half(3),
        own_half(1),
        own_half(2),
        up_grad.astype(F32),
        lax.dynamic_slice_in_dim(small, row * up_width, up_width),
        down_grad.T.astype(F32),
        own_half(0),
    )


def solution(mesh):
    in_specs = (
        P(("dp", "row"), "col"),
        P("dp", None),
        P("col"),
        P("col"),
        P("col", "row"),
        P(),
        P(),
        P("row", "col"),
        P("col"),
        P("col"),
        P("col"),
        P("col", "row"),
        P("row"),
        P("row", "col"),
        P("col"),
        P(("dp", "row"), "col"),
    )
    out_specs = (
        P(("dp", "row"), "col"),
        P(("dp", "row"), "col"),
        P("col"),
        P("col"),
        P("col", "row"),
        P(),
        P(),
        P("row", "col"),
        P("col"),
        P("col"),
        P("col"),
        P("col", "row"),
        P("row"),
        P("row", "col"),
        P("col"),
    )
    return jax.shard_map(
        on_device, mesh=mesh, in_specs=in_specs, out_specs=out_specs, check_vma=False
    )
```

```python
import functools

import jax
import jax.numpy as jnp
import numpy as np
from jax import lax
from jax.experimental import pallas as pl
from jax.experimental.pallas import tpu as pltpu
from jax.sharding import PartitionSpec as P

D = 1088
HEADS = 17
HEAD_DIM = 64
FF = 4352
TOK_G = 1024

EPSILON = 1e-05
MASKED = -1e30
CHUNK = 256
BF16 = jnp.bfloat16
F32 = jnp.float32


def swap(payload, axis, distance):
    size = lax.axis_size(axis)
    return lax.ppermute(payload, axis, [(i, i ^ distance) for i in range(size)])


def after(payload, *others):
    return lax.optimization_barrier((payload, *others))[0]


def gather_blocks(payload, axis, relay=0):
    if lax.axis_size(axis) == relay:
        far = swap(payload, axis, 2)
        near = swap(payload, axis, 1)
        return [payload, near, far, swap(far, axis, 1)]
    return [payload] + [swap(payload, axis, k) for k in range(1, lax.axis_size(axis))]


def send_blocks(blocks, axis):
    return [blocks[0]] + [swap(blocks[k], axis, k) for k in range(1, len(blocks))]


def scatter_sum(blocks, axis, relay=0):
    if lax.axis_size(axis) == relay:
        far = swap(blocks[3].astype(BF16), axis, 1).astype(F32)
        far = swap((blocks[2].astype(F32) + far).astype(BF16), axis, 2)
        near = swap(blocks[1].astype(BF16), axis, 1)
        return blocks[0] + near.astype(F32) + far.astype(F32)
    received = [swap(blocks[k].astype(BF16), axis, k) for k in range(1, len(blocks))]
    total = blocks[0]
    for item in received:
        total = total + item.astype(F32)
    return total


def share_of(matrix, index, parts):
    size = matrix.shape[0] // parts
    return lax.dynamic_slice_in_dim(matrix, index * size, size, 0)


def by_index(blocks, index):
    count = len(blocks)
    total = jnp.zeros((count,) + blocks[0].shape, blocks[0].dtype)
    for k, item in enumerate(blocks):
        total = lax.dynamic_update_index_in_dim(total, item, index ^ k, 0)
    return total.reshape((count * blocks[0].shape[0],) + blocks[0].shape[1:])


def rows_of(matrix, parts):
    size = matrix.shape[0] // parts
    return [matrix[k * size : (k + 1) * size] for k in range(parts)]


def head_starts(rows):
    return [int(np.floor(HEADS * r / rows + 0.5)) for r in range(rows + 1)]


def most_heads(rows):
    starts = head_starts(rows)
    return max(b - a for a, b in zip(starts[:-1], starts[1:]))


def window_columns(rows, copies):
    starts = head_starts(rows)
    width = most_heads(rows) * HEAD_DIM
    table = np.full((rows, copies * width), -1, np.int64)
    for r in range(rows):
        count = (starts[r + 1] - starts[r]) * HEAD_DIM
        for t in range(copies):
            table[r, t * width : t * width + count] = t * D + starts[r] * HEAD_DIM + np.arange(count)
    return table


def move_tables(rows, parts):
    moves = []
    for k in range(rows):
        places = [[] for _ in range(rows)]
        columns = [[] for _ in range(rows)]
        for copies, place_at, column_at in parts:
            windows = window_columns(rows, copies)
            shard = copies * D // rows
            for r in range(rows):
                for p in range(windows.shape[1]):
                    if windows[r, p] >= 0 and windows[r, p] // shard == r ^ k:
                        places[r].append(place_at + p)
                        columns[r].append(column_at + int(windows[r, p] % shard))
        longest = -(-max(len(place) for place in places) // 16) * 16
        at = np.full((rows, longest), -1, np.int32)
        frm = np.full((rows, longest), -1, np.int32)
        for r in range(rows):
            at[r, : len(places[r])] = places[r]
            frm[r ^ k, : len(columns[r])] = columns[r]
        moves.append((at, frm))
    return moves


def table_row(table, index):
    return lax.dynamic_index_in_dim(jnp.asarray(table), index, 0, keepdims=True)


def one_hot(places, size):
    return (lax.broadcasted_iota(jnp.int32, (size, places.shape[1]), 0) == places).astype(BF16)


def mm(a, b):
    return jnp.dot(a, b, preferred_element_type=F32)


def mm_nt(a, b):
    return lax.dot_general(a, b, (((1,), (1,)), ((), ())), preferred_element_type=F32)


def mm_tn(a, b):
    return lax.dot_general(a, b, (((0,), (0,)), ((), ())), preferred_element_type=F32)


def move_columns(matrix, from_tables, to_tables, width, row, riders=None):
    counts = [table.shape[1] for table in from_tables]
    picked = mm(matrix, one_hot(table_row(np.concatenate(from_tables, 1), row), matrix.shape[1])).astype(BF16)
    slabs, others, at = [], [], 0
    for k, count in enumerate(counts):
        slab = picked[:, at : at + count]
        at += count
        if k == 0:
            slabs.append(slab)
            others.append(riders and riders[0])
        elif riders is None:
            slabs.append(swap(slab, "row", k) if count else slab)
        else:
            both = swap(jnp.concatenate([riders[k], slab], axis=1), "row", k)
            others.append(both[:, : riders[k].shape[1]])
            slabs.append(both[:, riders[k].shape[1] :])
    moved = mm_nt(jnp.concatenate(slabs, axis=1), one_hot(table_row(np.concatenate(to_tables, 1), row), width))
    return moved.astype(BF16), others


def positions(start, shape, dim, block, col):
    at = lax.broadcasted_iota(jnp.int32, shape, dim) + start
    shift = block.bit_length() - 1
    return lax.shift_left(lax.shift_right_logical(at, shift), shift + 1) + (at & (block - 1)) + col * block


def segments(pos, scal_ref):
    first = scal_ref[2]
    return (pos >= first).astype(jnp.int32) + (pos >= first + scal_ref[3]).astype(jnp.int32)


def mask_bias(scal_ref, query_at, query_shape, query_dim, key_shape, key_dim, block, key_col):
    query_pos = positions(query_at, query_shape, query_dim, block, scal_ref[1])
    key_pos = positions(0, key_shape, key_dim, block, key_col)
    allowed = (key_pos <= query_pos) & (segments(key_pos, scal_ref) == segments(query_pos, scal_ref))
    return jnp.where(allowed, 0.0, MASKED)


def in_order(source_ref, target_ref, row, blocks, block):
    for j in range(blocks):
        target_ref[j * block : (j + 1) * block, :] = source_ref[j ^ row]


def forward_kernel(blocks, block, heads, scal_ref, q_ref, kv0_ref, kv1_ref, out_ref, lse_ref, q_s, kv0_s, kv1_s, o_s):
    row = scal_ref[0]
    width = heads * HEAD_DIM
    in_order(q_ref, q_s, row, blocks, block)
    in_order(kv0_ref, kv0_s, row, blocks, block)
    in_order(kv1_ref, kv1_s, row, blocks, block)
    own = scal_ref[1]
    for i in range(blocks * block // CHUNK):
        span = slice(i * CHUNK, (i + 1) * CHUNK)
        keys = (i + 1) * CHUNK
        shape = (CHUNK, keys)
        bias0 = mask_bias(scal_ref, i * CHUNK, (CHUNK, 1), 0, (1, keys), 1, block, own)
        bias1 = mask_bias(scal_ref, i * CHUNK, (CHUNK, 1), 0, (1, keys), 1, block, 1 - own)
        for h in range(heads):
            at = slice(h * HEAD_DIM, (h + 1) * HEAD_DIM)
            va = slice(width + h * HEAD_DIM, width + (h + 1) * HEAD_DIM)
            query = q_s[span, at]
            s0 = mm_nt(query, kv0_s[:keys, at]) + bias0
            s1 = mm_nt(query, kv1_s[:keys, at]) + bias1
            top = jnp.maximum(jnp.max(s0, axis=1, keepdims=True), jnp.max(s1, axis=1, keepdims=True))
            e0 = jnp.exp(s0 - top)
            e1 = jnp.exp(s1 - top)
            total = jnp.sum(e0, axis=1, keepdims=True) + jnp.sum(e1, axis=1, keepdims=True)
            result = mm(e0.astype(BF16), kv0_s[:keys, va]) + mm(e1.astype(BF16), kv1_s[:keys, va])
            o_s[span, at] = (result / total).astype(BF16)
            lse_ref[span, h : h + 1] = top + jnp.log(total)
    for j in range(blocks):
        out_ref[j ^ row] = o_s[j * block : (j + 1) * block, :]


def backward_kernel(
    blocks,
    block,
    heads,
    scal_ref,
    q_ref,
    kv0_ref,
    kv1_ref,
    g_ref,
    lse_ref,
    dq_ref,
    own_ref,
    other_ref,
    q_s,
    kv0_s,
    kv1_s,
    g_s,
    dq_s,
    d0_s,
    d1_s,
):
    row = scal_ref[0]
    width = heads * HEAD_DIM
    in_order(q_ref, q_s, row, blocks, block)
    in_order(kv0_ref, kv0_s, row, blocks, block)
    in_order(kv1_ref, kv1_s, row, blocks, block)
    in_order(g_ref, g_s, row, blocks, block)
    own = scal_ref[1]
    chunks = blocks * block // CHUNK
    for i in reversed(range(chunks)):
        span = slice(i * CHUNK, (i + 1) * CHUNK)
        keys = (i + 1) * CHUNK
        bias0 = mask_bias(scal_ref, i * CHUNK, (1, CHUNK), 1, (keys, 1), 0, block, own)
        bias1 = mask_bias(scal_ref, i * CHUNK, (1, CHUNK), 1, (keys, 1), 0, block, 1 - own)
        for h in range(heads):
            at = slice(h * HEAD_DIM, (h + 1) * HEAD_DIM)
            va = slice(width + h * HEAD_DIM, width + (h + 1) * HEAD_DIM)
            query = q_s[span, at]
            grad = g_s[span, at]
            lse = lse_ref[h : h + 1, span]
            p0 = jnp.exp(mm_nt(kv0_s[:keys, at], query) + bias0 - lse)
            p1 = jnp.exp(mm_nt(kv1_s[:keys, at], query) + bias1 - lse)
            dp0 = mm_nt(kv0_s[:keys, va], grad)
            dp1 = mm_nt(kv1_s[:keys, va], grad)
            delta = jnp.sum(p0 * dp0, axis=0, keepdims=True) + jnp.sum(p1 * dp1, axis=0, keepdims=True)
            ds0 = (p0 * (dp0 - delta)).astype(BF16)
            ds1 = (p1 * (dp1 - delta)).astype(BF16)
            if i == chunks - 1:
                d0_s[:keys, at] = mm(ds0, query)
                d1_s[:keys, at] = mm(ds1, query)
                d0_s[:keys, va] = mm(p0.astype(BF16), grad)
                d1_s[:keys, va] = mm(p1.astype(BF16), grad)
            else:
                d0_s[:keys, at] += mm(ds0, query)
                d1_s[:keys, at] += mm(ds1, query)
                d0_s[:keys, va] += mm(p0.astype(BF16), grad)
                d1_s[:keys, va] += mm(p1.astype(BF16), grad)
            dquery = mm_tn(ds0, kv0_s[:keys, at]) + mm_tn(ds1, kv1_s[:keys, at])
            dq_s[span, at] = (dquery * HEAD_DIM ** (-0.5)).astype(BF16)
    for j in range(blocks):
        piece = slice(j * block, (j + 1) * block)
        dq_ref[j ^ row] = dq_s[piece, :]
        own_ref[j ^ row] = d0_s[piece, :]
        other_ref[j ^ row] = d1_s[piece, :].astype(BF16)


def vmem():
    return pl.BlockSpec(memory_space=pltpu.VMEM)


def smem():
    return pl.BlockSpec(memory_space=pltpu.SMEM)


def attend_forward(scal, queries, kv_own, kv_other, heads):
    blocks, block, width = queries.shape
    tokens = blocks * block
    return pl.pallas_call(
        functools.partial(forward_kernel, blocks, block, heads),
        out_shape=(
            jax.ShapeDtypeStruct((blocks, block, width), BF16),
            jax.ShapeDtypeStruct((tokens, heads), F32),
        ),
        in_specs=[smem(), vmem(), vmem(), vmem()],
        out_specs=(vmem(), vmem()),
        scratch_shapes=[
            pltpu.VMEM((tokens, width), BF16),
            pltpu.VMEM((tokens, 2 * width), BF16),
            pltpu.VMEM((tokens, 2 * width), BF16),
            pltpu.VMEM((tokens, width), BF16),
        ],
        compiler_params=pltpu.CompilerParams(vmem_limit_bytes=40 * 2**20),
        cost_estimate=pl.CostEstimate(
            flops=4 * tokens * 3 * tokens // 2 * width, bytes_accessed=6 * tokens * width * 2, transcendentals=heads * tokens * tokens
        ),
        name="attend_forward",
    )(scal, queries, kv_own, kv_other)


def attend_backward(scal, queries, kv_own, kv_other, grads, lse, heads):
    blocks, block, width = queries.shape
    tokens = blocks * block
    return pl.pallas_call(
        functools.partial(backward_kernel, blocks, block, heads),
        out_shape=(
            jax.ShapeDtypeStruct((blocks, block, width), BF16),
            jax.ShapeDtypeStruct((blocks, block, 2 * width), F32),
            jax.ShapeDtypeStruct((blocks, block, 2 * width), BF16),
        ),
        in_specs=[smem(), vmem(), vmem(), vmem(), vmem(), vmem()],
        out_specs=(vmem(), vmem(), vmem()),
        scratch_shapes=[
            pltpu.VMEM((tokens, width), BF16),
            pltpu.VMEM((tokens, 2 * width), BF16),
            pltpu.VMEM((tokens, 2 * width), BF16),
            pltpu.VMEM((tokens, width), BF16),
            pltpu.VMEM((tokens, width), BF16),
            pltpu.VMEM((tokens, 2 * width), F32),
            pltpu.VMEM((tokens, 2 * width), F32),
        ],
        compiler_params=pltpu.CompilerParams(vmem_limit_bytes=44 * 2**20),
        cost_estimate=pl.CostEstimate(
            flops=10 * tokens * 3 * tokens // 2 * width, bytes_accessed=14 * tokens * width * 2, transcendentals=heads * tokens * tokens
        ),
        name="attend_backward",
    )(scal, queries, kv_own, kv_other, grads, lse)


def norm_parts(resid_in):
    mean_value = jnp.sum(resid_in, axis=1, keepdims=True) / D
    square = jnp.sum(resid_in * resid_in, axis=1, keepdims=True) / D
    inverse = lax.rsqrt(square - mean_value * mean_value + EPSILON)
    return ((resid_in - mean_value) * inverse, inverse)


def norm_back(grad_in, normal, inverse, norm_gain):
    scaled = grad_in * norm_gain
    mean_scaled = jnp.sum(scaled, axis=1, keepdims=True) / D
    mean_cross = jnp.sum(scaled * normal, axis=1, keepdims=True) / D
    return inverse * (scaled - mean_scaled - normal * mean_cross)


def gelu_tanh(pre_value):
    return jax.nn.gelu(pre_value, approximate=True)


def on_device(
    tokens,
    lengths,
    first_gain,
    first_shift,
    qkv_weight,
    query_bias,
    value_bias,
    out_weight,
    out_bias,
    second_gain,
    second_shift,
    up_weight,
    up_bias,
    down_weight,
    down_bias,
    cotangent,
):
    rows = lax.axis_size("row")
    row = lax.axis_index("row")
    col = lax.axis_index("col")
    half = tokens.shape[1]
    block = tokens.shape[0] // 2
    heads = most_heads(rows)
    width = heads * HEAD_DIM

    def halves(blocks):
        mine = jnp.concatenate([share_of(item, col, 2) for item in blocks], axis=0)
        other = jnp.concatenate([share_of(item, 1 - col, 2) for item in blocks], axis=0)
        return jnp.concatenate([mine, swap(other, "col", 1)], axis=1)

    def unhalves(matrix):
        mine = matrix[:, :half]
        other = swap(matrix[:, half:], "col", 1)
        return jnp.concatenate([jnp.where(col == 0, mine, other), jnp.where(col == 0, other, mine)], axis=0)

    dps = lax.axis_size("dp")
    dp = lax.axis_index("dp")

    def over_cols(left, right, *others):
        other = after(mm_tn(left[:, half:], right).astype(BF16), *others)
        other = swap(other, "col", 1)
        return (mm_tn(left[:, :half], right) + other.astype(F32)).astype(BF16)

    def dp_shares(matrix):
        return [share_of(matrix, dp ^ k, dps) for k in range(dps)]

    x_blocks = gather_blocks(tokens, "row", 4)
    x_first = halves(x_blocks[: rows // 2])
    x_own = x_first[:block]
    x_all = jnp.concatenate([x_first, halves(x_blocks[rows // 2 :])], axis=0).astype(F32)

    vectors = jnp.stack([first_gain, first_shift, out_bias, second_gain, second_shift, down_bias])
    vectors = jnp.concatenate([vectors, swap(after(vectors, x_blocks[1]), "col", 1)], axis=1)
    gain1, shift1, out_b, gain2, shift2, down_b = [vectors[i] for i in range(6)]

    qkv_moves = move_tables(rows, [(3, 0, 0)])
    share = share_of(qkv_weight, dp, dps)
    share, _ = move_columns(share, [m[1] for m in qkv_moves], [m[0] for m in qkv_moves], 3 * width, row)
    share = after(share, x_blocks[1])
    qkv_blocks = gather_blocks(share, "dp")
    qkv_head = by_index(qkv_blocks, dp)
    qkv_other = swap(qkv_head, "col", 1)
    w_qkv = jnp.concatenate([qkv_head, qkv_other], axis=0)

    if out_weight.shape[0] % dps == 0:
        out_all = lax.all_gather(share_of(out_weight, dp, dps), ("row", "dp"))
    else:
        out_all = lax.all_gather(out_weight, "row")
    windows = window_columns(rows, 1)
    out_shard = D // rows
    absolute = np.concatenate([windows[np.arange(rows) ^ k] for k in range(rows)], axis=1).astype(np.int32)
    shard_at = (absolute // out_shard) ^ np.arange(rows)[:, None]
    relative = np.where(absolute >= 0, shard_at * out_shard + absolute % out_shard, -1).astype(np.int32)

    starts = jnp.asarray(np.array(head_starts(rows), np.int32))
    head_at = starts[row] * HEAD_DIM
    live_cols = jnp.arange(width, dtype=jnp.int32) < (starts[row + 1] - starts[row]) * HEAD_DIM

    def bias_window(vector):
        padded = jnp.concatenate([vector, jnp.zeros((width,), F32)])
        return jnp.where(live_cols, lax.dynamic_slice_in_dim(padded, head_at, width), 0.0)

    normal1, inverse1 = norm_parts(x_all)
    normed1 = (normal1 * gain1 + shift1).astype(BF16)
    kv_own = mm(normed1, w_qkv[:, width:])
    bias_kv = jnp.concatenate([jnp.zeros((width,), F32), bias_window(value_bias)])
    kv_own = (kv_own + bias_kv).astype(BF16)
    kv_other = swap(kv_own, "col", 1)
    queries = mm(normed1, w_qkv[:, :width])
    queries = (queries + bias_window(query_bias)).astype(BF16) * BF16(HEAD_DIM ** (-0.5))
    queries = queries.reshape(rows, block, width)
    kv_own = kv_own.reshape(rows, block, 2 * width)
    kv_other = kv_other.reshape(rows, block, 2 * width)
    scal = jnp.stack([row.astype(jnp.int32), col.astype(jnp.int32), lengths[0, 0], lengths[0, 1]])

    def live_rows(matrix, start):
        live = start + jnp.arange(matrix.shape[0], dtype=jnp.int32) < lengths[0, 0] + lengths[0, 1]
        return jnp.where(live[:, None], matrix, 0.0)

    grad_out = live_rows(halves([after(cotangent, x_blocks[rows - 1])]), (row * 2 + col) * block)
    grad_out_low = grad_out.astype(BF16)
    g_blocks = lax.all_gather(grad_out_low, "row", tiled=True)

    queries = after(queries, grad_out_low)
    attention, lse = attend_forward(scal, queries, kv_own, kv_other, heads)

    att_blocks = send_blocks([attention[k] for k in range(rows)], "row")
    att_own = jnp.concatenate(att_blocks, axis=1)
    out_all = after(out_all, attention).reshape(D, half)
    w_out = jnp.concatenate([out_all.T, swap(out_all, "col", 1).T], axis=0)
    to_heads = one_hot(table_row(absolute, row), D)
    att_all = mm_nt(att_own, to_heads).astype(BF16)
    resid_mid = x_own.astype(F32) + (mm_nt(att_all, w_out) + out_b)

    normal2, inverse2 = norm_parts(resid_mid)
    normed2 = (normal2 * gain2 + shift2).astype(BF16)
    mlp_in = jnp.concatenate(gather_blocks(normed2, "row", 4), axis=0)
    up_own = after(up_weight, normed2)
    down_own = after(down_weight, normed2)
    w_up = jnp.concatenate([up_own, swap(up_own, "col", 1)], axis=0)
    w_down = jnp.concatenate([down_own, swap(down_own, "col", 1)], axis=1)
    g_blocks = after(g_blocks, normed2)
    g_all = jnp.concatenate([share_of(g_blocks, row ^ k, rows) for k in range(rows)], axis=0)
    down_bias_part = jnp.sum(grad_out_low.astype(F32), axis=0)

    pre_act = mm(mlp_in, w_up) + up_bias
    act, gelu_back = jax.vjp(gelu_tanh, pre_act)
    grad_act = mm_nt(g_all, w_down)
    act, grad_pre = lax.optimization_barrier((act.astype(BF16), gelu_back(grad_act)[0].astype(BF16)))
    up_bias_part = jnp.sum(grad_pre.astype(F32), axis=0)
    grad_normed2 = mm_nt(grad_pre, w_up)

    blocks = rows_of(grad_normed2, rows)
    sent = [item.astype(BF16) for item in blocks[1:]]
    late_g, late_act, late_in, late_pre, *sent = lax.optimization_barrier((g_all, act, mlp_in, grad_pre, *sent))
    down_grad = over_cols(late_g, late_act)
    up_grad = over_cols(late_in, late_pre)
    grad_normed2 = scatter_sum([after(blocks[0], down_grad, up_grad)] + sent, "row")
    second_gain_part = jnp.sum(grad_normed2 * normal2, axis=0)
    second_shift_part = jnp.sum(grad_normed2, axis=0)
    grad_mid = grad_out + norm_back(grad_normed2, normal2, inverse2, gain2)
    grad_mid_low = grad_mid.astype(BF16)
    out_bias_part = jnp.sum(grad_mid_low.astype(F32), axis=0)

    grad_att = mm(grad_mid_low, w_out).astype(BF16)
    grad_att = mm(grad_att, to_heads).astype(BF16)
    grad_att = [grad_att[:, k * width : (k + 1) * width] for k in range(rows)]
    late_act, late_att, late_mid, *grad_att = lax.optimization_barrier((act, att_own, grad_mid_low, *grad_att))
    grad_att = jnp.stack(send_blocks(grad_att, "row"))
    att_shards = mm_nt(late_att, one_hot(table_row(relative, row), D)).astype(BF16)
    out_grad = over_cols(late_mid, att_shards)
    down_out = mm(late_act, w_down)
    grad_att = after(grad_att, out_grad, up_bias_part)
    up_grad, down_grad = lax.psum((up_grad, down_grad), "dp")

    dq, dkv_own, dkv_other = attend_backward(scal, queries, kv_own, kv_other, grad_att, lse.T, heads)
    dkv = (dkv_own + swap(dkv_other, "col", 1).astype(F32)).astype(BF16)
    grad_qkv = jnp.concatenate([dq, dkv], axis=2).reshape(-1, 3 * width)
    qkv_bias_part = jnp.sum(grad_qkv.astype(F32), axis=0)
    normed_part = mm_nt(grad_qkv, w_qkv)
    first_gain_part = jnp.sum(normed_part * normal1, axis=0)
    first_shift_part = jnp.sum(normed_part, axis=0)
    qkv_grad = over_cols(normed1, after(grad_qkv, normed_part))
    def place(vector):
        mine, other = vector[:half], vector[half:]
        return jnp.concatenate([jnp.where(col == 0, mine, other), jnp.where(col == 0, other, mine)])

    def place_window(vector):
        padded = lax.dynamic_update_slice_in_dim(jnp.zeros((D + width,), F32), vector, head_at, 0)
        return padded[:D]

    def place_rows(vector):
        return lax.dynamic_update_slice_in_dim(jnp.zeros((FF,), F32), vector, row * vector.shape[0], 0)

    small = jnp.concatenate(
        [
            place_rows(up_bias_part),
            place(down_bias_part),
            place(second_gain_part),
            place(second_shift_part),
            place(out_bias_part),
            place(first_gain_part),
            place(first_shift_part),
            place_window(qkv_bias_part[:width]),
            place_window(qkv_bias_part[2 * width :]),
        ]
    )
    shares = dp_shares(jnp.concatenate([qkv_grad, out_grad], axis=1))
    blocks = rows_of(normed_part, rows)
    grad_normed1 = scatter_sum([after(blocks[0], *shares)] + blocks[1:], "row", 4)
    back1 = norm_back(grad_normed1, normal1[:block], inverse1[:block], gain1)
    input_grad = unhalves(grad_mid + back1)

    summed = scatter_sum([shares[0].astype(F32)] + shares[1:], "dp").astype(BF16)
    qkv_grad, out_grad = summed[:, : 3 * width], summed[:, 3 * width :]
    share_rows = qkv_grad.shape[0]
    small_width = -(-small.shape[0] // share_rows)
    small = jnp.pad(small, (0, small_width * share_rows - small.shape[0])).reshape(share_rows, small_width)
    riders = [
        jnp.concatenate([out_grad[:, k * out_shard : (k + 1) * out_shard], small.astype(BF16)], axis=1) for k in range(rows)
    ]
    qkv_grad, riders = move_columns(
        qkv_grad, [m[0] for m in qkv_moves], [m[1] for m in qkv_moves], 3 * out_shard, row, riders
    )
    rider = sum(item.astype(F32) for item in riders).astype(BF16)
    both = gather_blocks(jnp.concatenate([qkv_grad, rider], axis=1), "dp")
    both[1], up_grad, down_grad = lax.optimization_barrier((both[1], up_grad, down_grad))
    small = sum(item[:, 4 * out_shard :].astype(F32) for item in both)
    small = (small + swap(small, "col", 1)).reshape(-1)
    both = [item[:, : 4 * out_shard] for item in both]
    both = by_index([item.astype(F32) for item in both], dp)
    qkv_grad = both[:, : 3 * out_shard]
    out_grad = both[:, 3 * out_shard :].T

    blocks = rows_of(down_out, rows)
    block_out = scatter_sum([blocks[0]] + [after(item.astype(BF16), rider) for item in blocks[1:]], "row", 4)
    block_out = unhalves((resid_mid + (block_out + down_b)).astype(BF16))

    def own_half(part):
        return lax.dynamic_slice_in_dim(small, FF + part * D + col * half, half)

    up_width = up_bias.shape[0]
    return (
        block_out,
        input_grad,
        own_half(4),
        own_half(5),
        qkv_grad,
        small[FF + 6 * D : FF + 7 * D],
        small[FF + 7 * D : FF + 8 * D],
        out_grad,
        own_half(3),
        own_half(1),
        own_half(2),
        up_grad.astype(F32),
        lax.dynamic_slice_in_dim(small, row * up_width, up_width),
        down_grad.T.astype(F32),
        own_half(0),
    )


def solution(mesh):
    in_specs = (
        P(("dp", "row"), "col"),
        P("dp", None),
        P("col"),
        P("col"),
        P("col", "row"),
        P(),
        P(),
        P("row", "col"),
        P("col"),
        P("col"),
        P("col"),
        P("col", "row"),
        P("row"),
        P("row", "col"),
        P("col"),
        P(("dp", "row"), "col"),
    )
    out_specs = (
        P(("dp", "row"), "col"),
        P(("dp", "row"), "col"),
        P("col"),
        P("col"),
        P("col", "row"),
        P(),
        P(),
        P("row", "col"),
        P("col"),
        P("col"),
        P("col"),
        P("col", "row"),
        P("row"),
        P("row", "col"),
        P("col"),
    )
    return jax.shard_map(
        on_device, mesh=mesh, in_specs=in_specs, out_specs=out_specs, check_vma=False
    )
```

```python
import functools

import jax
import jax.numpy as jnp
import numpy as np
from jax import lax
from jax.experimental import pallas as pl
from jax.experimental.pallas import tpu as pltpu
from jax.sharding import PartitionSpec as P

D = 1088
HEADS = 17
HEAD_DIM = 64
FF = 4352
TOK_G = 1024

EPSILON = 1e-05
MASKED = -1e30
CHUNK = 256
BF16 = jnp.bfloat16
F32 = jnp.float32


def swap(payload, axis, distance):
    size = lax.axis_size(axis)
    return lax.ppermute(payload, axis, [(i, i ^ distance) for i in range(size)])


def after(payload, *others):
    return lax.optimization_barrier((payload, *others))[0]


def gather_blocks(payload, axis, relay=0):
    if lax.axis_size(axis) == relay:
        far = swap(payload, axis, 2)
        near = swap(payload, axis, 1)
        return [payload, near, far, swap(far, axis, 1)]
    return [payload] + [swap(payload, axis, k) for k in range(1, lax.axis_size(axis))]


def send_blocks(blocks, axis):
    return [blocks[0]] + [swap(blocks[k], axis, k) for k in range(1, len(blocks))]


def scatter_sum(blocks, axis, relay=0):
    if lax.axis_size(axis) == relay:
        far = swap(blocks[3].astype(BF16), axis, 1).astype(F32)
        far = swap((blocks[2].astype(F32) + far).astype(BF16), axis, 2)
        near = swap(blocks[1].astype(BF16), axis, 1)
        return blocks[0] + near.astype(F32) + far.astype(F32)
    received = [swap(blocks[k].astype(BF16), axis, k) for k in range(1, len(blocks))]
    total = blocks[0]
    for item in received:
        total = total + item.astype(F32)
    return total


def share_of(matrix, index, parts):
    size = matrix.shape[0] // parts
    return lax.dynamic_slice_in_dim(matrix, index * size, size, 0)


def by_index(blocks, index):
    count = len(blocks)
    total = jnp.zeros((count,) + blocks[0].shape, blocks[0].dtype)
    for k, item in enumerate(blocks):
        total = lax.dynamic_update_index_in_dim(total, item, index ^ k, 0)
    return total.reshape((count * blocks[0].shape[0],) + blocks[0].shape[1:])


def rows_of(matrix, parts):
    size = matrix.shape[0] // parts
    return [matrix[k * size : (k + 1) * size] for k in range(parts)]


def head_starts(rows):
    return [int(np.floor(HEADS * r / rows + 0.5)) for r in range(rows + 1)]


def most_heads(rows):
    starts = head_starts(rows)
    return max(b - a for a, b in zip(starts[:-1], starts[1:]))


def window_columns(rows, copies):
    starts = head_starts(rows)
    width = most_heads(rows) * HEAD_DIM
    table = np.full((rows, copies * width), -1, np.int64)
    for r in range(rows):
        count = (starts[r + 1] - starts[r]) * HEAD_DIM
        for t in range(copies):
            table[r, t * width : t * width + count] = t * D + starts[r] * HEAD_DIM + np.arange(count)
    return table


def move_tables(rows, parts):
    moves = []
    for k in range(rows):
        places = [[] for _ in range(rows)]
        columns = [[] for _ in range(rows)]
        for copies, place_at, column_at in parts:
            windows = window_columns(rows, copies)
            shard = copies * D // rows
            for r in range(rows):
                for p in range(windows.shape[1]):
                    if windows[r, p] >= 0 and windows[r, p] // shard == r ^ k:
                        places[r].append(place_at + p)
                        columns[r].append(column_at + int(windows[r, p] % shard))
        longest = -(-max(len(place) for place in places) // 16) * 16
        at = np.full((rows, longest), -1, np.int32)
        frm = np.full((rows, longest), -1, np.int32)
        for r in range(rows):
            at[r, : len(places[r])] = places[r]
            frm[r ^ k, : len(columns[r])] = columns[r]
        moves.append((at, frm))
    return moves


def table_row(table, index):
    return lax.dynamic_index_in_dim(jnp.asarray(table), index, 0, keepdims=True)


def one_hot(places, size):
    return (lax.broadcasted_iota(jnp.int32, (size, places.shape[1]), 0) == places).astype(BF16)


def mm(a, b):
    return jnp.dot(a, b, preferred_element_type=F32)


def mm_nt(a, b):
    return lax.dot_general(a, b, (((1,), (1,)), ((), ())), preferred_element_type=F32)


def mm_tn(a, b):
    return lax.dot_general(a, b, (((0,), (0,)), ((), ())), preferred_element_type=F32)


def move_columns(matrix, from_tables, to_tables, width, row, riders=None):
    counts = [table.shape[1] for table in from_tables]
    picked = mm(matrix, one_hot(table_row(np.concatenate(from_tables, 1), row), matrix.shape[1])).astype(BF16)
    slabs, others, at = [], [], 0
    for k, count in enumerate(counts):
        slab = picked[:, at : at + count]
        at += count
        if k == 0:
            slabs.append(slab)
            others.append(riders and riders[0])
        elif riders is None:
            slabs.append(swap(slab, "row", k) if count else slab)
        else:
            both = swap(jnp.concatenate([riders[k], slab], axis=1), "row", k)
            others.append(both[:, : riders[k].shape[1]])
            slabs.append(both[:, riders[k].shape[1] :])
    moved = mm_nt(jnp.concatenate(slabs, axis=1), one_hot(table_row(np.concatenate(to_tables, 1), row), width))
    return moved.astype(BF16), others


def positions(start, shape, dim, block, col):
    at = lax.broadcasted_iota(jnp.int32, shape, dim) + start
    shift = block.bit_length() - 1
    return lax.shift_left(lax.shift_right_logical(at, shift), shift + 1) + (at & (block - 1)) + col * block


def segments(pos, scal_ref):
    first = scal_ref[2]
    return (pos >= first).astype(jnp.int32) + (pos >= first + scal_ref[3]).astype(jnp.int32)


def mask_bias(scal_ref, query_at, query_shape, query_dim, key_shape, key_dim, block, key_col):
    query_pos = positions(query_at, query_shape, query_dim, block, scal_ref[1])
    key_pos = positions(0, key_shape, key_dim, block, key_col)
    allowed = (key_pos <= query_pos) & (segments(key_pos, scal_ref) == segments(query_pos, scal_ref))
    return jnp.where(allowed, 0.0, MASKED)


def in_order(source_ref, target_ref, row, blocks, block):
    for j in range(blocks):
        target_ref[j * block : (j + 1) * block, :] = source_ref[j ^ row]


def forward_kernel(blocks, block, heads, scal_ref, q_ref, kv0_ref, kv1_ref, out_ref, lse_ref, q_s, kv0_s, kv1_s, o_s):
    row = scal_ref[0]
    width = heads * HEAD_DIM
    in_order(q_ref, q_s, row, blocks, block)
    in_order(kv0_ref, kv0_s, row, blocks, block)
    in_order(kv1_ref, kv1_s, row, blocks, block)
    own = scal_ref[1]
    for i in range(blocks * block // CHUNK):
        span = slice(i * CHUNK, (i + 1) * CHUNK)
        keys = (i + 1) * CHUNK
        shape = (CHUNK, keys)
        bias0 = mask_bias(scal_ref, i * CHUNK, (CHUNK, 1), 0, (1, keys), 1, block, own)
        bias1 = mask_bias(scal_ref, i * CHUNK, (CHUNK, 1), 0, (1, keys), 1, block, 1 - own)
        for h in range(heads):
            at = slice(h * HEAD_DIM, (h + 1) * HEAD_DIM)
            va = slice(width + h * HEAD_DIM, width + (h + 1) * HEAD_DIM)
            query = q_s[span, at]
            s0 = mm_nt(query, kv0_s[:keys, at]) + bias0
            s1 = mm_nt(query, kv1_s[:keys, at]) + bias1
            top = jnp.maximum(jnp.max(s0, axis=1, keepdims=True), jnp.max(s1, axis=1, keepdims=True))
            e0 = jnp.exp(s0 - top)
            e1 = jnp.exp(s1 - top)
            total = jnp.sum(e0, axis=1, keepdims=True) + jnp.sum(e1, axis=1, keepdims=True)
            result = mm(e0.astype(BF16), kv0_s[:keys, va]) + mm(e1.astype(BF16), kv1_s[:keys, va])
            o_s[span, at] = (result / total).astype(BF16)
            lse_ref[span, h : h + 1] = top + jnp.log(total)
    for j in range(blocks):
        out_ref[j ^ row] = o_s[j * block : (j + 1) * block, :]


def backward_kernel(
    blocks,
    block,
    heads,
    scal_ref,
    q_ref,
    kv0_ref,
    kv1_ref,
    g_ref,
    lse_ref,
    dq_ref,
    own_ref,
    other_ref,
    q_s,
    kv0_s,
    kv1_s,
    g_s,
    dq_s,
    d0_s,
    d1_s,
):
    row = scal_ref[0]
    width = heads * HEAD_DIM
    in_order(q_ref, q_s, row, blocks, block)
    in_order(kv0_ref, kv0_s, row, blocks, block)
    in_order(kv1_ref, kv1_s, row, blocks, block)
    in_order(g_ref, g_s, row, blocks, block)
    own = scal_ref[1]
    chunks = blocks * block // CHUNK
    for i in reversed(range(chunks)):
        span = slice(i * CHUNK, (i + 1) * CHUNK)
        keys = (i + 1) * CHUNK
        bias0 = mask_bias(scal_ref, i * CHUNK, (1, CHUNK), 1, (keys, 1), 0, block, own)
        bias1 = mask_bias(scal_ref, i * CHUNK, (1, CHUNK), 1, (keys, 1), 0, block, 1 - own)
        for h in range(heads):
            at = slice(h * HEAD_DIM, (h + 1) * HEAD_DIM)
            va = slice(width + h * HEAD_DIM, width + (h + 1) * HEAD_DIM)
            query = q_s[span, at]
            grad = g_s[span, at]
            lse = lse_ref[h : h + 1, span]
            p0 = jnp.exp(mm_nt(kv0_s[:keys, at], query) + bias0 - lse)
            p1 = jnp.exp(mm_nt(kv1_s[:keys, at], query) + bias1 - lse)
            dp0 = mm_nt(kv0_s[:keys, va], grad)
            dp1 = mm_nt(kv1_s[:keys, va], grad)
            delta = jnp.sum(p0 * dp0, axis=0, keepdims=True) + jnp.sum(p1 * dp1, axis=0, keepdims=True)
            ds0 = (p0 * (dp0 - delta)).astype(BF16)
            ds1 = (p1 * (dp1 - delta)).astype(BF16)
            if i == chunks - 1:
                d0_s[:keys, at] = mm(ds0, query)
                d1_s[:keys, at] = mm(ds1, query)
                d0_s[:keys, va] = mm(p0.astype(BF16), grad)
                d1_s[:keys, va] = mm(p1.astype(BF16), grad)
            else:
                d0_s[:keys, at] += mm(ds0, query)
                d1_s[:keys, at] += mm(ds1, query)
                d0_s[:keys, va] += mm(p0.astype(BF16), grad)
                d1_s[:keys, va] += mm(p1.astype(BF16), grad)
            dquery = mm_tn(ds0, kv0_s[:keys, at]) + mm_tn(ds1, kv1_s[:keys, at])
            dq_s[span, at] = (dquery * HEAD_DIM ** (-0.5)).astype(BF16)
    for j in range(blocks):
        piece = slice(j * block, (j + 1) * block)
        dq_ref[j ^ row] = dq_s[piece, :]
        own_ref[j ^ row] = d0_s[piece, :]
        other_ref[j ^ row] = d1_s[piece, :].astype(BF16)


def vmem():
    return pl.BlockSpec(memory_space=pltpu.VMEM)


def smem():
    return pl.BlockSpec(memory_space=pltpu.SMEM)


def attend_forward(scal, queries, kv_own, kv_other, heads):
    blocks, block, width = queries.shape
    tokens = blocks * block
    return pl.pallas_call(
        functools.partial(forward_kernel, blocks, block, heads),
        out_shape=(
            jax.ShapeDtypeStruct((blocks, block, width), BF16),
            jax.ShapeDtypeStruct((tokens, heads), F32),
        ),
        in_specs=[smem(), vmem(), vmem(), vmem()],
        out_specs=(vmem(), vmem()),
        scratch_shapes=[
            pltpu.VMEM((tokens, width), BF16),
            pltpu.VMEM((tokens, 2 * width), BF16),
            pltpu.VMEM((tokens, 2 * width), BF16),
            pltpu.VMEM((tokens, width), BF16),
        ],
        compiler_params=pltpu.CompilerParams(vmem_limit_bytes=40 * 2**20),
        cost_estimate=pl.CostEstimate(
            flops=4 * tokens * 3 * tokens // 2 * width, bytes_accessed=6 * tokens * width * 2, transcendentals=heads * tokens * tokens
        ),
        name="attend_forward",
    )(scal, queries, kv_own, kv_other)


def attend_backward(scal, queries, kv_own, kv_other, grads, lse, heads):
    blocks, block, width = queries.shape
    tokens = blocks * block
    return pl.pallas_call(
        functools.partial(backward_kernel, blocks, block, heads),
        out_shape=(
            jax.ShapeDtypeStruct((blocks, block, width), BF16),
            jax.ShapeDtypeStruct((blocks, block, 2 * width), F32),
            jax.ShapeDtypeStruct((blocks, block, 2 * width), BF16),
        ),
        in_specs=[smem(), vmem(), vmem(), vmem(), vmem(), vmem()],
        out_specs=(vmem(), vmem(), vmem()),
        scratch_shapes=[
            pltpu.VMEM((tokens, width), BF16),
            pltpu.VMEM((tokens, 2 * width), BF16),
            pltpu.VMEM((tokens, 2 * width), BF16),
            pltpu.VMEM((tokens, width), BF16),
            pltpu.VMEM((tokens, width), BF16),
            pltpu.VMEM((tokens, 2 * width), F32),
            pltpu.VMEM((tokens, 2 * width), F32),
        ],
        compiler_params=pltpu.CompilerParams(vmem_limit_bytes=44 * 2**20),
        cost_estimate=pl.CostEstimate(
            flops=10 * tokens * 3 * tokens // 2 * width, bytes_accessed=14 * tokens * width * 2, transcendentals=heads * tokens * tokens
        ),
        name="attend_backward",
    )(scal, queries, kv_own, kv_other, grads, lse)


def norm_parts(resid_in):
    mean_value = jnp.sum(resid_in, axis=1, keepdims=True) / D
    square = jnp.sum(resid_in * resid_in, axis=1, keepdims=True) / D
    inverse = lax.rsqrt(square - mean_value * mean_value + EPSILON)
    return ((resid_in - mean_value) * inverse, inverse)


def norm_back(grad_in, normal, inverse, norm_gain):
    scaled = grad_in * norm_gain
    mean_scaled = jnp.sum(scaled, axis=1, keepdims=True) / D
    mean_cross = jnp.sum(scaled * normal, axis=1, keepdims=True) / D
    return inverse * (scaled - mean_scaled - normal * mean_cross)


def gelu_tanh(pre_value):
    return jax.nn.gelu(pre_value, approximate=True)


def on_device(
    tokens,
    lengths,
    first_gain,
    first_shift,
    qkv_weight,
    query_bias,
    value_bias,
    out_weight,
    out_bias,
    second_gain,
    second_shift,
    up_weight,
    up_bias,
    down_weight,
    down_bias,
    cotangent,
):
    rows = lax.axis_size("row")
    row = lax.axis_index("row")
    col = lax.axis_index("col")
    half = tokens.shape[1]
    block = tokens.shape[0] // 2
    heads = most_heads(rows)
    width = heads * HEAD_DIM

    def halves(blocks):
        mine = jnp.concatenate([share_of(item, col, 2) for item in blocks], axis=0)
        other = jnp.concatenate([share_of(item, 1 - col, 2) for item in blocks], axis=0)
        return jnp.concatenate([mine, swap(other, "col", 1)], axis=1)

    def unhalves(matrix):
        mine = matrix[:, :half]
        other = swap(matrix[:, half:], "col", 1)
        return jnp.concatenate([jnp.where(col == 0, mine, other), jnp.where(col == 0, other, mine)], axis=0)

    dps = lax.axis_size("dp")
    dp = lax.axis_index("dp")

    def over_cols(left, right, *others):
        other = after(mm_tn(left[:, half:], right).astype(BF16), *others)
        other = swap(other, "col", 1)
        return (mm_tn(left[:, :half], right) + other.astype(F32)).astype(BF16)

    def dp_shares(matrix):
        return [share_of(matrix, dp ^ k, dps) for k in range(dps)]

    x_blocks = gather_blocks(tokens, "row", 4)
    x_first = halves(x_blocks[: rows // 2])
    x_own = x_first[:block]
    x_all = jnp.concatenate([x_first, halves(x_blocks[rows // 2 :])], axis=0).astype(F32)

    vectors = jnp.stack([first_gain, first_shift, out_bias, second_gain, second_shift, down_bias])
    vectors = jnp.concatenate([vectors, swap(after(vectors, x_blocks[1]), "col", 1)], axis=1)
    gain1, shift1, out_b, gain2, shift2, down_b = [vectors[i] for i in range(6)]

    qkv_moves = move_tables(rows, [(3, 0, 0)])
    share = share_of(qkv_weight, dp, dps)
    share, _ = move_columns(share, [m[1] for m in qkv_moves], [m[0] for m in qkv_moves], 3 * width, row)
    share = after(share, x_blocks[1])
    qkv_blocks = gather_blocks(share, "dp")
    qkv_head = by_index(qkv_blocks, dp)
    qkv_other = swap(qkv_head, "col", 1)
    w_qkv = jnp.concatenate([qkv_head, qkv_other], axis=0)

    if out_weight.shape[0] % dps == 0:
        out_all = lax.all_gather(share_of(out_weight, dp, dps), ("row", "dp"))
    else:
        out_all = lax.all_gather(out_weight, "row")
    windows = window_columns(rows, 1)
    out_shard = D // rows
    absolute = np.concatenate([windows[np.arange(rows) ^ k] for k in range(rows)], axis=1).astype(np.int32)
    shard_at = (absolute // out_shard) ^ np.arange(rows)[:, None]
    relative = np.where(absolute >= 0, shard_at * out_shard + absolute % out_shard, -1).astype(np.int32)

    starts = jnp.asarray(np.array(head_starts(rows), np.int32))
    head_at = starts[row] * HEAD_DIM
    live_cols = jnp.arange(width, dtype=jnp.int32) < (starts[row + 1] - starts[row]) * HEAD_DIM

    def bias_window(vector):
        padded = jnp.concatenate([vector, jnp.zeros((width,), F32)])
        return jnp.where(live_cols, lax.dynamic_slice_in_dim(padded, head_at, width), 0.0)

    normal1, inverse1 = norm_parts(x_all)
    normed1 = (normal1 * gain1 + shift1).astype(BF16)
    kv_own = mm(normed1, w_qkv[:, width:])
    bias_kv = jnp.concatenate([jnp.zeros((width,), F32), bias_window(value_bias)])
    kv_own = (kv_own + bias_kv).astype(BF16)
    kv_other = swap(kv_own, "col", 1)
    queries = mm(normed1, w_qkv[:, :width])
    queries = (queries + bias_window(query_bias)).astype(BF16) * BF16(HEAD_DIM ** (-0.5))
    queries = queries.reshape(rows, block, width)
    kv_own = kv_own.reshape(rows, block, 2 * width)
    kv_other = kv_other.reshape(rows, block, 2 * width)
    scal = jnp.stack([row.astype(jnp.int32), col.astype(jnp.int32), lengths[0, 0], lengths[0, 1]])

    def live_rows(matrix, start):
        live = start + jnp.arange(matrix.shape[0], dtype=jnp.int32) < lengths[0, 0] + lengths[0, 1]
        return jnp.where(live[:, None], matrix, 0.0)

    grad_out = live_rows(halves([after(cotangent, x_blocks[rows - 1])]), (row * 2 + col) * block)
    grad_out_low = grad_out.astype(BF16)
    g_blocks = lax.all_gather(grad_out_low, "row", tiled=True)

    queries = after(queries, grad_out_low)
    attention, lse = attend_forward(scal, queries, kv_own, kv_other, heads)

    att_blocks = send_blocks([attention[k] for k in range(rows)], "row")
    att_own = jnp.concatenate(att_blocks, axis=1)
    out_all = after(out_all, *att_blocks[1:]).reshape(D, half)
    w_out = jnp.concatenate([out_all.T, swap(out_all, "col", 1).T], axis=0)
    to_heads = one_hot(table_row(absolute, row), D)
    att_all = mm_nt(att_own, to_heads).astype(BF16)
    resid_mid = x_own.astype(F32) + (mm_nt(att_all, w_out) + out_b)

    normal2, inverse2 = norm_parts(resid_mid)
    normed2 = (normal2 * gain2 + shift2).astype(BF16)
    mlp_blocks = gather_blocks(normed2, "row", 4)
    mlp_in = jnp.concatenate(mlp_blocks, axis=0)
    up_own = after(up_weight, normed2)
    down_own = after(down_weight, normed2)
    w_up = jnp.concatenate([up_own, swap(up_own, "col", 1)], axis=0)
    w_down = jnp.concatenate([down_own, swap(down_own, "col", 1)], axis=1)
    g_blocks = after(g_blocks, mlp_blocks[rows - 1])
    g_all = jnp.concatenate([share_of(g_blocks, row ^ k, rows) for k in range(rows)], axis=0)
    down_bias_part = jnp.sum(grad_out_low.astype(F32), axis=0)

    pre_act = mm(mlp_in, w_up) + up_bias
    act, gelu_back = jax.vjp(gelu_tanh, pre_act)
    grad_act = mm_nt(g_all, w_down)
    act, grad_pre = lax.optimization_barrier((act.astype(BF16), gelu_back(grad_act)[0].astype(BF16)))
    up_bias_part = jnp.sum(grad_pre.astype(F32), axis=0)
    grad_normed2 = mm_nt(grad_pre, w_up)

    blocks = rows_of(grad_normed2, rows)
    sent = [item.astype(BF16) for item in blocks[1:]]
    late_g, late_act, late_in, late_pre, *sent = lax.optimization_barrier((g_all, act, mlp_in, grad_pre, *sent))
    down_grad = over_cols(late_g, late_act)
    up_grad = over_cols(late_in, late_pre)
    att_shards = mm_nt(after(att_own, sent[0]), one_hot(table_row(relative, row), D)).astype(BF16)
    grad_normed2 = scatter_sum([after(blocks[0], down_grad, up_grad, att_shards, up_bias_part)] + sent, "row")
    second_gain_part = jnp.sum(grad_normed2 * normal2, axis=0)
    second_shift_part = jnp.sum(grad_normed2, axis=0)
    grad_mid = grad_out + norm_back(grad_normed2, normal2, inverse2, gain2)
    grad_mid_low = grad_mid.astype(BF16)
    out_bias_part = jnp.sum(grad_mid_low.astype(F32), axis=0)

    grad_att = mm(grad_mid_low, w_out).astype(BF16)
    grad_att = mm(grad_att, to_heads).astype(BF16)
    grad_att = [grad_att[:, k * width : (k + 1) * width] for k in range(rows)]
    late_act, late_mid, *grad_att = lax.optimization_barrier((act, grad_mid_low, *grad_att))
    grad_att = jnp.stack(send_blocks(grad_att, "row"))
    out_grad = over_cols(late_mid, att_shards)
    down_out = mm(late_act, w_down)
    grad_att = after(grad_att, out_grad)
    up_grad, down_grad = lax.psum((up_grad, down_grad), "dp")

    dq, dkv_own, dkv_other = attend_backward(scal, queries, kv_own, kv_other, grad_att, lse.T, heads)
    dkv = (dkv_own + swap(dkv_other, "col", 1).astype(F32)).astype(BF16)
    grad_qkv = jnp.concatenate([dq, dkv], axis=2).reshape(-1, 3 * width)
    qkv_bias_part = jnp.sum(grad_qkv.astype(F32), axis=0)
    normed_part = mm_nt(grad_qkv, w_qkv)
    first_gain_part = jnp.sum(normed_part * normal1, axis=0)
    first_shift_part = jnp.sum(normed_part, axis=0)
    qkv_grad = over_cols(normed1, after(grad_qkv, normed_part))
    def place(vector):
        mine, other = vector[:half], vector[half:]
        return jnp.concatenate([jnp.where(col == 0, mine, other), jnp.where(col == 0, other, mine)])

    def place_window(vector):
        padded = lax.dynamic_update_slice_in_dim(jnp.zeros((D + width,), F32), vector, head_at, 0)
        return padded[:D]

    def place_rows(vector):
        return lax.dynamic_update_slice_in_dim(jnp.zeros((FF,), F32), vector, row * vector.shape[0], 0)

    small = jnp.concatenate(
        [
            place_rows(up_bias_part),
            place(down_bias_part),
            place(second_gain_part),
            place(second_shift_part),
            place(out_bias_part),
            place(first_gain_part),
            place(first_shift_part),
            place_window(qkv_bias_part[:width]),
            place_window(qkv_bias_part[2 * width :]),
        ]
    )
    shares = dp_shares(jnp.concatenate([qkv_grad, out_grad], axis=1))
    blocks = rows_of(normed_part, rows)
    grad_normed1 = scatter_sum([after(blocks[0], *shares)] + blocks[1:], "row", 4)
    back1 = norm_back(grad_normed1, normal1[:block], inverse1[:block], gain1)
    input_grad = unhalves(grad_mid + back1)

    summed = scatter_sum([shares[0].astype(F32)] + shares[1:], "dp").astype(BF16)
    qkv_grad, out_grad = summed[:, : 3 * width], summed[:, 3 * width :]
    share_rows = qkv_grad.shape[0]
    small_width = -(-small.shape[0] // share_rows)
    small = jnp.pad(small, (0, small_width * share_rows - small.shape[0])).reshape(share_rows, small_width)
    riders = [
        jnp.concatenate([out_grad[:, k * out_shard : (k + 1) * out_shard], small.astype(BF16)], axis=1) for k in range(rows)
    ]
    qkv_grad, riders = move_columns(
        qkv_grad, [m[0] for m in qkv_moves], [m[1] for m in qkv_moves], 3 * out_shard, row, riders
    )
    rider = sum(item.astype(F32) for item in riders).astype(BF16)
    both, up_grad, down_grad = lax.optimization_barrier((jnp.concatenate([qkv_grad, rider], axis=1), up_grad, down_grad))
    both = gather_blocks(both, "dp")
    small = sum(item[:, 4 * out_shard :].astype(F32) for item in both)
    small = (small + swap(small, "col", 1)).reshape(-1)
    both = [item[:, : 4 * out_shard] for item in both]
    both = by_index([item.astype(F32) for item in both], dp)
    qkv_grad = both[:, : 3 * out_shard]
    out_grad = both[:, 3 * out_shard :].T

    blocks = rows_of(down_out, rows)
    block_out = scatter_sum([blocks[0]] + [after(item.astype(BF16), rider) for item in blocks[1:]], "row", 4)
    block_out = unhalves((resid_mid + (block_out + down_b)).astype(BF16))

    def own_half(part):
        return lax.dynamic_slice_in_dim(small, FF + part * D + col * half, half)

    up_width = up_bias.shape[0]
    return (
        block_out,
        input_grad,
        own_half(4),
        own_half(5),
        qkv_grad,
        small[FF + 6 * D : FF + 7 * D],
        small[FF + 7 * D : FF + 8 * D],
        out_grad,
        own_half(3),
        own_half(1),
        own_half(2),
        up_grad.astype(F32),
        lax.dynamic_slice_in_dim(small, row * up_width, up_width),
        down_grad.T.astype(F32),
        own_half(0),
    )


def solution(mesh):
    in_specs = (
        P(("dp", "row"), "col"),
        P("dp", None),
        P("col"),
        P("col"),
        P("col", "row"),
        P(),
        P(),
        P("row", "col"),
        P("col"),
        P("col"),
        P("col"),
        P("col", "row"),
        P("row"),
        P("row", "col"),
        P("col"),
        P(("dp", "row"), "col"),
    )
    out_specs = (
        P(("dp", "row"), "col"),
        P(("dp", "row"), "col"),
        P("col"),
        P("col"),
        P("col", "row"),
        P(),
        P(),
        P("row", "col"),
        P("col"),
        P("col"),
        P("col"),
        P("col", "row"),
        P("row"),
        P("row", "col"),
        P("col"),
    )
    return jax.shard_map(
        on_device, mesh=mesh, in_specs=in_specs, out_specs=out_specs, check_vma=False
    )
```

```python
import functools

import jax
import jax.numpy as jnp
import numpy as np
from jax import lax
from jax.experimental import pallas as pl
from jax.experimental.pallas import tpu as pltpu
from jax.sharding import PartitionSpec as P

D = 1088
HEADS = 17
HEAD_DIM = 64
FF = 4352
TOK_G = 1024

EPSILON = 1e-05
MASKED = -1e30
CHUNK = 256
BF16 = jnp.bfloat16
F32 = jnp.float32


def swap(payload, axis, distance):
    size = lax.axis_size(axis)
    return lax.ppermute(payload, axis, [(i, i ^ distance) for i in range(size)])


def after(payload, *others):
    return lax.optimization_barrier((payload, *others))[0]


def gather_blocks(payload, axis, relay=0, behind=()):
    if lax.axis_size(axis) == relay:
        far = swap(payload, axis, 2)
        near = swap(payload, axis, 1)
        return [payload, near, far, swap(after(far, *behind), axis, 1)]
    return [payload] + [swap(payload, axis, k) for k in range(1, lax.axis_size(axis))]


def send_blocks(blocks, axis):
    return [blocks[0]] + [swap(blocks[k], axis, k) for k in range(1, len(blocks))]


def scatter_sum(blocks, axis, relay=0):
    if lax.axis_size(axis) == relay:
        far = swap(blocks[3].astype(BF16), axis, 1).astype(F32)
        far = swap((blocks[2].astype(F32) + far).astype(BF16), axis, 2)
        near = swap(blocks[1].astype(BF16), axis, 1)
        return blocks[0] + near.astype(F32) + far.astype(F32)
    received = [swap(blocks[k].astype(BF16), axis, k) for k in range(1, len(blocks))]
    total = blocks[0]
    for item in received:
        total = total + item.astype(F32)
    return total


def share_of(matrix, index, parts):
    size = matrix.shape[0] // parts
    return lax.dynamic_slice_in_dim(matrix, index * size, size, 0)


def by_index(blocks, index):
    count = len(blocks)
    total = jnp.zeros((count,) + blocks[0].shape, blocks[0].dtype)
    for k, item in enumerate(blocks):
        total = lax.dynamic_update_index_in_dim(total, item, index ^ k, 0)
    return total.reshape((count * blocks[0].shape[0],) + blocks[0].shape[1:])


def rows_of(matrix, parts):
    size = matrix.shape[0] // parts
    return [matrix[k * size : (k + 1) * size] for k in range(parts)]


def head_starts(rows):
    return [int(np.floor(HEADS * r / rows + 0.5)) for r in range(rows + 1)]


def most_heads(rows):
    starts = head_starts(rows)
    return max(b - a for a, b in zip(starts[:-1], starts[1:]))


def window_columns(rows, copies):
    starts = head_starts(rows)
    width = most_heads(rows) * HEAD_DIM
    table = np.full((rows, copies * width), -1, np.int64)
    for r in range(rows):
        count = (starts[r + 1] - starts[r]) * HEAD_DIM
        for t in range(copies):
            table[r, t * width : t * width + count] = t * D + starts[r] * HEAD_DIM + np.arange(count)
    return table


def move_tables(rows, parts):
    moves = []
    for k in range(rows):
        places = [[] for _ in range(rows)]
        columns = [[] for _ in range(rows)]
        for copies, place_at, column_at in parts:
            windows = window_columns(rows, copies)
            shard = copies * D // rows
            for r in range(rows):
                for p in range(windows.shape[1]):
                    if windows[r, p] >= 0 and windows[r, p] // shard == r ^ k:
                        places[r].append(place_at + p)
                        columns[r].append(column_at + int(windows[r, p] % shard))
        longest = -(-max(len(place) for place in places) // 16) * 16
        at = np.full((rows, longest), -1, np.int32)
        frm = np.full((rows, longest), -1, np.int32)
        for r in range(rows):
            at[r, : len(places[r])] = places[r]
            frm[r ^ k, : len(columns[r])] = columns[r]
        moves.append((at, frm))
    return moves


def table_row(table, index):
    return lax.dynamic_index_in_dim(jnp.asarray(table), index, 0, keepdims=True)


def one_hot(places, size):
    return (lax.broadcasted_iota(jnp.int32, (size, places.shape[1]), 0) == places).astype(BF16)


def mm(a, b):
    return jnp.dot(a, b, preferred_element_type=F32)


def mm_nt(a, b):
    return lax.dot_general(a, b, (((1,), (1,)), ((), ())), preferred_element_type=F32)


def mm_tn(a, b):
    return lax.dot_general(a, b, (((0,), (0,)), ((), ())), preferred_element_type=F32)


def move_columns(matrix, from_tables, to_tables, width, row, riders=None):
    counts = [table.shape[1] for table in from_tables]
    picked = mm(matrix, one_hot(table_row(np.concatenate(from_tables, 1), row), matrix.shape[1])).astype(BF16)
    slabs, others, at = [], [], 0
    for k, count in enumerate(counts):
        slab = picked[:, at : at + count]
        at += count
        if k == 0:
            slabs.append(slab)
            others.append(riders and riders[0])
        elif riders is None:
            slabs.append(swap(slab, "row", k) if count else slab)
        else:
            both = swap(jnp.concatenate([riders[k], slab], axis=1), "row", k)
            others.append(both[:, : riders[k].shape[1]])
            slabs.append(both[:, riders[k].shape[1] :])
    moved = mm_nt(jnp.concatenate(slabs, axis=1), one_hot(table_row(np.concatenate(to_tables, 1), row), width))
    return moved.astype(BF16), others


def positions(start, shape, dim, block, col):
    at = lax.broadcasted_iota(jnp.int32, shape, dim) + start
    shift = block.bit_length() - 1
    return lax.shift_left(lax.shift_right_logical(at, shift), shift + 1) + (at & (block - 1)) + col * block


def segments(pos, scal_ref):
    first = scal_ref[2]
    return (pos >= first).astype(jnp.int32) + (pos >= first + scal_ref[3]).astype(jnp.int32)


def mask_bias(scal_ref, query_at, query_shape, query_dim, key_shape, key_dim, block, key_col):
    query_pos = positions(query_at, query_shape, query_dim, block, scal_ref[1])
    key_pos = positions(0, key_shape, key_dim, block, key_col)
    allowed = (key_pos <= query_pos) & (segments(key_pos, scal_ref) == segments(query_pos, scal_ref))
    return jnp.where(allowed, 0.0, MASKED)


def in_order(source_ref, target_ref, row, blocks, block):
    for j in range(blocks):
        target_ref[j * block : (j + 1) * block, :] = source_ref[j ^ row]


def forward_kernel(blocks, block, heads, scal_ref, q_ref, kv0_ref, kv1_ref, out_ref, lse_ref, q_s, kv0_s, kv1_s, o_s):
    row = scal_ref[0]
    width = heads * HEAD_DIM
    in_order(q_ref, q_s, row, blocks, block)
    in_order(kv0_ref, kv0_s, row, blocks, block)
    in_order(kv1_ref, kv1_s, row, blocks, block)
    own = scal_ref[1]
    for i in range(blocks * block // CHUNK):
        span = slice(i * CHUNK, (i + 1) * CHUNK)
        keys = (i + 1) * CHUNK
        shape = (CHUNK, keys)
        bias0 = mask_bias(scal_ref, i * CHUNK, (CHUNK, 1), 0, (1, keys), 1, block, own)
        bias1 = mask_bias(scal_ref, i * CHUNK, (CHUNK, 1), 0, (1, keys), 1, block, 1 - own)
        for h in range(heads):
            at = slice(h * HEAD_DIM, (h + 1) * HEAD_DIM)
            va = slice(width + h * HEAD_DIM, width + (h + 1) * HEAD_DIM)
            query = q_s[span, at]
            s0 = mm_nt(query, kv0_s[:keys, at]) + bias0
            s1 = mm_nt(query, kv1_s[:keys, at]) + bias1
            top = jnp.maximum(jnp.max(s0, axis=1, keepdims=True), jnp.max(s1, axis=1, keepdims=True))
            e0 = jnp.exp(s0 - top)
            e1 = jnp.exp(s1 - top)
            total = jnp.sum(e0, axis=1, keepdims=True) + jnp.sum(e1, axis=1, keepdims=True)
            result = mm(e0.astype(BF16), kv0_s[:keys, va]) + mm(e1.astype(BF16), kv1_s[:keys, va])
            o_s[span, at] = (result / total).astype(BF16)
            lse_ref[span, h : h + 1] = top + jnp.log(total)
    for j in range(blocks):
        out_ref[j ^ row] = o_s[j * block : (j + 1) * block, :]


def backward_kernel(
    blocks,
    block,
    heads,
    scal_ref,
    q_ref,
    kv0_ref,
    kv1_ref,
    g_ref,
    lse_ref,
    dq_ref,
    own_ref,
    other_ref,
    q_s,
    kv0_s,
    kv1_s,
    g_s,
    dq_s,
    d0_s,
    d1_s,
):
    row = scal_ref[0]
    width = heads * HEAD_DIM
    in_order(q_ref, q_s, row, blocks, block)
    in_order(kv0_ref, kv0_s, row, blocks, block)
    in_order(kv1_ref, kv1_s, row, blocks, block)
    in_order(g_ref, g_s, row, blocks, block)
    own = scal_ref[1]
    chunks = blocks * block // CHUNK
    for i in reversed(range(chunks)):
        span = slice(i * CHUNK, (i + 1) * CHUNK)
        keys = (i + 1) * CHUNK
        bias0 = mask_bias(scal_ref, i * CHUNK, (1, CHUNK), 1, (keys, 1), 0, block, own)
        bias1 = mask_bias(scal_ref, i * CHUNK, (1, CHUNK), 1, (keys, 1), 0, block, 1 - own)
        for h in range(heads):
            at = slice(h * HEAD_DIM, (h + 1) * HEAD_DIM)
            va = slice(width + h * HEAD_DIM, width + (h + 1) * HEAD_DIM)
            query = q_s[span, at]
            grad = g_s[span, at]
            lse = lse_ref[h : h + 1, span]
            p0 = jnp.exp(mm_nt(kv0_s[:keys, at], query) + bias0 - lse)
            p1 = jnp.exp(mm_nt(kv1_s[:keys, at], query) + bias1 - lse)
            dp0 = mm_nt(kv0_s[:keys, va], grad)
            dp1 = mm_nt(kv1_s[:keys, va], grad)
            delta = jnp.sum(p0 * dp0, axis=0, keepdims=True) + jnp.sum(p1 * dp1, axis=0, keepdims=True)
            ds0 = (p0 * (dp0 - delta)).astype(BF16)
            ds1 = (p1 * (dp1 - delta)).astype(BF16)
            if i == chunks - 1:
                d0_s[:keys, at] = mm(ds0, query)
                d1_s[:keys, at] = mm(ds1, query)
                d0_s[:keys, va] = mm(p0.astype(BF16), grad)
                d1_s[:keys, va] = mm(p1.astype(BF16), grad)
            else:
                d0_s[:keys, at] += mm(ds0, query)
                d1_s[:keys, at] += mm(ds1, query)
                d0_s[:keys, va] += mm(p0.astype(BF16), grad)
                d1_s[:keys, va] += mm(p1.astype(BF16), grad)
            dquery = mm_tn(ds0, kv0_s[:keys, at]) + mm_tn(ds1, kv1_s[:keys, at])
            dq_s[span, at] = (dquery * HEAD_DIM ** (-0.5)).astype(BF16)
    for j in range(blocks):
        piece = slice(j * block, (j + 1) * block)
        dq_ref[j ^ row] = dq_s[piece, :]
        own_ref[j ^ row] = d0_s[piece, :]
        other_ref[j ^ row] = d1_s[piece, :].astype(BF16)


def vmem():
    return pl.BlockSpec(memory_space=pltpu.VMEM)


def smem():
    return pl.BlockSpec(memory_space=pltpu.SMEM)


def attend_forward(scal, queries, kv_own, kv_other, heads):
    blocks, block, width = queries.shape
    tokens = blocks * block
    return pl.pallas_call(
        functools.partial(forward_kernel, blocks, block, heads),
        out_shape=(
            jax.ShapeDtypeStruct((blocks, block, width), BF16),
            jax.ShapeDtypeStruct((tokens, heads), F32),
        ),
        in_specs=[smem(), vmem(), vmem(), vmem()],
        out_specs=(vmem(), vmem()),
        scratch_shapes=[
            pltpu.VMEM((tokens, width), BF16),
            pltpu.VMEM((tokens, 2 * width), BF16),
            pltpu.VMEM((tokens, 2 * width), BF16),
            pltpu.VMEM((tokens, width), BF16),
        ],
        compiler_params=pltpu.CompilerParams(vmem_limit_bytes=40 * 2**20),
        cost_estimate=pl.CostEstimate(
            flops=4 * tokens * 3 * tokens // 2 * width, bytes_accessed=6 * tokens * width * 2, transcendentals=heads * tokens * tokens
        ),
        name="attend_forward",
    )(scal, queries, kv_own, kv_other)


def attend_backward(scal, queries, kv_own, kv_other, grads, lse, heads):
    blocks, block, width = queries.shape
    tokens = blocks * block
    return pl.pallas_call(
        functools.partial(backward_kernel, blocks, block, heads),
        out_shape=(
            jax.ShapeDtypeStruct((blocks, block, width), BF16),
            jax.ShapeDtypeStruct((blocks, block, 2 * width), F32),
            jax.ShapeDtypeStruct((blocks, block, 2 * width), BF16),
        ),
        in_specs=[smem(), vmem(), vmem(), vmem(), vmem(), vmem()],
        out_specs=(vmem(), vmem(), vmem()),
        scratch_shapes=[
            pltpu.VMEM((tokens, width), BF16),
            pltpu.VMEM((tokens, 2 * width), BF16),
            pltpu.VMEM((tokens, 2 * width), BF16),
            pltpu.VMEM((tokens, width), BF16),
            pltpu.VMEM((tokens, width), BF16),
            pltpu.VMEM((tokens, 2 * width), F32),
            pltpu.VMEM((tokens, 2 * width), F32),
        ],
        compiler_params=pltpu.CompilerParams(vmem_limit_bytes=44 * 2**20),
        cost_estimate=pl.CostEstimate(
            flops=10 * tokens * 3 * tokens // 2 * width, bytes_accessed=14 * tokens * width * 2, transcendentals=heads * tokens * tokens
        ),
        name="attend_backward",
    )(scal, queries, kv_own, kv_other, grads, lse)


def norm_parts(resid_in):
    mean_value = jnp.sum(resid_in, axis=1, keepdims=True) / D
    square = jnp.sum(resid_in * resid_in, axis=1, keepdims=True) / D
    inverse = lax.rsqrt(square - mean_value * mean_value + EPSILON)
    return ((resid_in - mean_value) * inverse, inverse)


def norm_back(grad_in, normal, inverse, norm_gain):
    scaled = grad_in * norm_gain
    mean_scaled = jnp.sum(scaled, axis=1, keepdims=True) / D
    mean_cross = jnp.sum(scaled * normal, axis=1, keepdims=True) / D
    return inverse * (scaled - mean_scaled - normal * mean_cross)


def gelu_tanh(pre_value):
    return jax.nn.gelu(pre_value, approximate=True)


def on_device(
    tokens,
    lengths,
    first_gain,
    first_shift,
    qkv_weight,
    query_bias,
    value_bias,
    out_weight,
    out_bias,
    second_gain,
    second_shift,
    up_weight,
    up_bias,
    down_weight,
    down_bias,
    cotangent,
):
    rows = lax.axis_size("row")
    row = lax.axis_index("row")
    col = lax.axis_index("col")
    half = tokens.shape[1]
    block = tokens.shape[0] // 2
    heads = most_heads(rows)
    width = heads * HEAD_DIM

    def halves(blocks):
        mine = jnp.concatenate([share_of(item, col, 2) for item in blocks], axis=0)
        other = jnp.concatenate([share_of(item, 1 - col, 2) for item in blocks], axis=0)
        return jnp.concatenate([mine, swap(other, "col", 1)], axis=1)

    def unhalves(matrix):
        mine = matrix[:, :half]
        other = swap(matrix[:, half:], "col", 1)
        return jnp.concatenate([jnp.where(col == 0, mine, other), jnp.where(col == 0, other, mine)], axis=0)

    dps = lax.axis_size("dp")
    dp = lax.axis_index("dp")

    def over_cols(left, right, *others):
        other = after(mm_tn(left[:, half:], right).astype(BF16), *others)
        other = swap(other, "col", 1)
        return (mm_tn(left[:, :half], right) + other.astype(F32)).astype(BF16)

    def dp_shares(matrix):
        return [share_of(matrix, dp ^ k, dps) for k in range(dps)]

    x_blocks = gather_blocks(tokens, "row", 4)
    x_first = halves(x_blocks[: rows // 2])
    x_own = x_first[:block]
    x_all = jnp.concatenate([x_first, halves(x_blocks[rows // 2 :])], axis=0).astype(F32)

    vectors = jnp.stack([first_gain, first_shift, out_bias, second_gain, second_shift, down_bias])
    vectors = jnp.concatenate([vectors, swap(after(vectors, x_blocks[1]), "col", 1)], axis=1)
    gain1, shift1, out_b, gain2, shift2, down_b = [vectors[i] for i in range(6)]

    qkv_moves = move_tables(rows, [(3, 0, 0)])
    share = share_of(qkv_weight, dp, dps)
    share, _ = move_columns(share, [m[1] for m in qkv_moves], [m[0] for m in qkv_moves], 3 * width, row)
    share = after(share, x_blocks[1])
    qkv_blocks = gather_blocks(share, "dp")
    qkv_head = by_index(qkv_blocks, dp)
    qkv_other = swap(qkv_head, "col", 1)
    w_qkv = jnp.concatenate([qkv_head, qkv_other], axis=0)

    if out_weight.shape[0] % dps == 0:
        out_all = lax.all_gather(share_of(out_weight, dp, dps), ("row", "dp"))
    else:
        out_all = lax.all_gather(out_weight, "row")
    windows = window_columns(rows, 1)
    out_shard = D // rows
    absolute = np.concatenate([windows[np.arange(rows) ^ k] for k in range(rows)], axis=1).astype(np.int32)
    shard_at = (absolute // out_shard) ^ np.arange(rows)[:, None]
    relative = np.where(absolute >= 0, shard_at * out_shard + absolute % out_shard, -1).astype(np.int32)

    starts = jnp.asarray(np.array(head_starts(rows), np.int32))
    head_at = starts[row] * HEAD_DIM
    live_cols = jnp.arange(width, dtype=jnp.int32) < (starts[row + 1] - starts[row]) * HEAD_DIM

    def bias_window(vector):
        padded = jnp.concatenate([vector, jnp.zeros((width,), F32)])
        return jnp.where(live_cols, lax.dynamic_slice_in_dim(padded, head_at, width), 0.0)

    normal1, inverse1 = norm_parts(x_all)
    normed1 = (normal1 * gain1 + shift1).astype(BF16)
    kv_own = mm(normed1, w_qkv[:, width:])
    bias_kv = jnp.concatenate([jnp.zeros((width,), F32), bias_window(value_bias)])
    kv_own = (kv_own + bias_kv).astype(BF16)
    kv_other = swap(kv_own, "col", 1)
    queries = mm(normed1, w_qkv[:, :width])
    queries = (queries + bias_window(query_bias)).astype(BF16) * BF16(HEAD_DIM ** (-0.5))
    queries = queries.reshape(rows, block, width)
    kv_own = kv_own.reshape(rows, block, 2 * width)
    kv_other = kv_other.reshape(rows, block, 2 * width)
    scal = jnp.stack([row.astype(jnp.int32), col.astype(jnp.int32), lengths[0, 0], lengths[0, 1]])

    def live_rows(matrix, start):
        live = start + jnp.arange(matrix.shape[0], dtype=jnp.int32) < lengths[0, 0] + lengths[0, 1]
        return jnp.where(live[:, None], matrix, 0.0)

    grad_out = live_rows(halves([after(cotangent, x_blocks[rows - 1])]), (row * 2 + col) * block)
    grad_out_low = grad_out.astype(BF16)

    queries = after(queries, grad_out_low)
    attention, lse = attend_forward(scal, queries, kv_own, kv_other, heads)

    g_blocks = gather_blocks(grad_out_low, "row", 4, (attention,))
    attention = after(attention, g_blocks[1], g_blocks[2])
    att_blocks = send_blocks([attention[k] for k in range(rows)], "row")
    att_own = jnp.concatenate(att_blocks, axis=1)
    out_all = after(out_all, *att_blocks[1:], *g_blocks[3:]).reshape(D, half)
    w_out = jnp.concatenate([out_all.T, swap(out_all, "col", 1).T], axis=0)
    to_heads = one_hot(table_row(absolute, row), D)
    att_all = mm_nt(att_own, to_heads).astype(BF16)
    resid_mid = x_own.astype(F32) + (mm_nt(att_all, w_out) + out_b)

    normal2, inverse2 = norm_parts(resid_mid)
    normed2 = (normal2 * gain2 + shift2).astype(BF16)
    mlp_blocks = gather_blocks(normed2, "row", 4)
    up_own = after(up_weight, normed2)
    down_own = after(down_weight, normed2)
    w_up = jnp.concatenate([up_own, swap(up_own, "col", 1)], axis=0)
    w_down = jnp.concatenate([down_own, swap(down_own, "col", 1)], axis=1)
    w_up, w_down, mlp_blocks[0] = lax.optimization_barrier((w_up, w_down, mlp_blocks[0]))
    mlp_in = jnp.concatenate(mlp_blocks, axis=0)
    g_all = jnp.concatenate(g_blocks, axis=0)
    down_bias_part = jnp.sum(grad_out_low.astype(F32), axis=0)

    pre_act = mm(mlp_in, w_up) + up_bias
    act, gelu_back = jax.vjp(gelu_tanh, pre_act)
    grad_act = mm_nt(g_all, w_down)
    act, grad_pre = lax.optimization_barrier((act.astype(BF16), gelu_back(grad_act)[0].astype(BF16)))
    up_bias_part = jnp.sum(grad_pre.astype(F32), axis=0)
    grad_normed2 = mm_nt(grad_pre, w_up)

    blocks = rows_of(grad_normed2, rows)
    sent = [item.astype(BF16) for item in blocks[1:]]
    late_g, late_act, late_in, late_pre, *sent = lax.optimization_barrier((g_all, act, mlp_in, grad_pre, *sent))
    down_grad = over_cols(late_g, late_act)
    up_grad = over_cols(late_in, late_pre)
    att_shards = mm_nt(after(att_own, sent[0]), one_hot(table_row(relative, row), D)).astype(BF16)
    grad_normed2 = scatter_sum([after(blocks[0], down_grad, up_grad, att_shards, up_bias_part)] + sent, "row")
    second_gain_part = jnp.sum(grad_normed2 * normal2, axis=0)
    second_shift_part = jnp.sum(grad_normed2, axis=0)
    grad_mid = grad_out + norm_back(grad_normed2, normal2, inverse2, gain2)
    grad_mid_low = grad_mid.astype(BF16)
    out_bias_part = jnp.sum(grad_mid_low.astype(F32), axis=0)

    grad_att = mm(grad_mid_low, w_out).astype(BF16)
    grad_att = mm(grad_att, to_heads).astype(BF16)
    grad_att = [grad_att[:, k * width : (k + 1) * width] for k in range(rows)]
    late_act, late_mid, *grad_att = lax.optimization_barrier((act, grad_mid_low, *grad_att))
    grad_att = jnp.stack(send_blocks(grad_att, "row"))
    out_grad = over_cols(late_mid, att_shards)
    down_out = mm(late_act, w_down)
    grad_att = after(grad_att, out_grad)
    up_grad, down_grad = lax.psum((up_grad, down_grad), "dp")

    dq, dkv_own, dkv_other = attend_backward(scal, queries, kv_own, kv_other, grad_att, lse.T, heads)
    dkv = (dkv_own + swap(dkv_other, "col", 1).astype(F32)).astype(BF16)
    grad_qkv = jnp.concatenate([dq, dkv], axis=2).reshape(-1, 3 * width)
    qkv_bias_part = jnp.sum(grad_qkv.astype(F32), axis=0)
    normed_part = mm_nt(grad_qkv, w_qkv)
    first_gain_part = jnp.sum(normed_part * normal1, axis=0)
    first_shift_part = jnp.sum(normed_part, axis=0)
    qkv_grad = over_cols(normed1, after(grad_qkv, normed_part))
    def place(vector):
        mine, other = vector[:half], vector[half:]
        return jnp.concatenate([jnp.where(col == 0, mine, other), jnp.where(col == 0, other, mine)])

    def place_window(vector):
        padded = lax.dynamic_update_slice_in_dim(jnp.zeros((D + width,), F32), vector, head_at, 0)
        return padded[:D]

    def place_rows(vector):
        return lax.dynamic_update_slice_in_dim(jnp.zeros((FF,), F32), vector, row * vector.shape[0], 0)

    small = jnp.concatenate(
        [
            place_rows(up_bias_part),
            place(down_bias_part),
            place(second_gain_part),
            place(second_shift_part),
            place(out_bias_part),
            place(first_gain_part),
            place(first_shift_part),
            place_window(qkv_bias_part[:width]),
            place_window(qkv_bias_part[2 * width :]),
        ]
    )
    shares = dp_shares(jnp.concatenate([qkv_grad, out_grad], axis=1))
    blocks = rows_of(normed_part, rows)
    grad_normed1 = scatter_sum([after(blocks[0], *shares)] + blocks[1:], "row", 4)
    back1 = norm_back(grad_normed1, normal1[:block], inverse1[:block], gain1)
    input_grad = unhalves(grad_mid + back1)

    summed = scatter_sum([shares[0].astype(F32)] + shares[1:], "dp").astype(BF16)
    qkv_grad, out_grad = summed[:, : 3 * width], summed[:, 3 * width :]
    share_rows = qkv_grad.shape[0]
    small_width = -(-small.shape[0] // share_rows)
    small = jnp.pad(small, (0, small_width * share_rows - small.shape[0])).reshape(share_rows, small_width)
    riders = [
        jnp.concatenate([out_grad[:, k * out_shard : (k + 1) * out_shard], small.astype(BF16)], axis=1) for k in range(rows)
    ]
    qkv_grad, riders = move_columns(
        qkv_grad, [m[0] for m in qkv_moves], [m[1] for m in qkv_moves], 3 * out_shard, row, riders
    )
    rider = sum(item.astype(F32) for item in riders).astype(BF16)
    both, up_grad, down_grad = lax.optimization_barrier((jnp.concatenate([qkv_grad, rider], axis=1), up_grad, down_grad))
    both = gather_blocks(both, "dp")
    small = sum(item[:, 4 * out_shard :].astype(F32) for item in both)
    small = (small + swap(small, "col", 1)).reshape(-1)
    both = [item[:, : 4 * out_shard] for item in both]
    both = by_index([item.astype(F32) for item in both], dp)
    qkv_grad = both[:, : 3 * out_shard]
    out_grad = both[:, 3 * out_shard :].T

    blocks = rows_of(down_out, rows)
    block_out = scatter_sum([blocks[0]] + [after(item.astype(BF16), rider) for item in blocks[1:]], "row", 4)
    block_out = unhalves((resid_mid + (block_out + down_b)).astype(BF16))

    def own_half(part):
        return lax.dynamic_slice_in_dim(small, FF + part * D + col * half, half)

    up_width = up_bias.shape[0]
    return (
        block_out,
        input_grad,
        own_half(4),
        own_half(5),
        qkv_grad,
        small[FF + 6 * D : FF + 7 * D],
        small[FF + 7 * D : FF + 8 * D],
        out_grad,
        own_half(3),
        own_half(1),
        own_half(2),
        up_grad.astype(F32),
        lax.dynamic_slice_in_dim(small, row * up_width, up_width),
        down_grad.T.astype(F32),
        own_half(0),
    )


def solution(mesh):
    in_specs = (
        P(("dp", "row"), "col"),
        P("dp", None),
        P("col"),
        P("col"),
        P("col", "row"),
        P(),
        P(),
        P("row", "col"),
        P("col"),
        P("col"),
        P("col"),
        P("col", "row"),
        P("row"),
        P("row", "col"),
        P("col"),
        P(("dp", "row"), "col"),
    )
    out_specs = (
        P(("dp", "row"), "col"),
        P(("dp", "row"), "col"),
        P("col"),
        P("col"),
        P("col", "row"),
        P(),
        P(),
        P("row", "col"),
        P("col"),
        P("col"),
        P("col"),
        P("col", "row"),
        P("row"),
        P("row", "col"),
        P("col"),
    )
    return jax.shard_map(
        on_device, mesh=mesh, in_specs=in_specs, out_specs=out_specs, check_vma=False
    )
```

```python
import functools

import jax
import jax.numpy as jnp
import numpy as np
from jax import lax
from jax.experimental import pallas as pl
from jax.experimental.pallas import tpu as pltpu
from jax.sharding import PartitionSpec as P

D = 1088
HEADS = 17
HEAD_DIM = 64
FF = 4352
TOK_G = 1024

EPSILON = 1e-05
MASKED = -1e30
CHUNK = 256
BF16 = jnp.bfloat16
F32 = jnp.float32


def swap(payload, axis, distance):
    size = lax.axis_size(axis)
    return lax.ppermute(payload, axis, [(i, i ^ distance) for i in range(size)])


def after(payload, *others):
    return lax.optimization_barrier((payload, *others))[0]


def gather_blocks(payload, axis, relay=0, behind=()):
    if lax.axis_size(axis) == relay:
        far = swap(payload, axis, 2)
        near = swap(payload, axis, 1)
        return [payload, near, far, swap(after(far, *behind), axis, 1)]
    return [payload] + [swap(payload, axis, k) for k in range(1, lax.axis_size(axis))]


def send_blocks(blocks, axis):
    return [blocks[0]] + [swap(blocks[k], axis, k) for k in range(1, len(blocks))]


def scatter_sum(blocks, axis, relay=0):
    if lax.axis_size(axis) == relay:
        far = swap(blocks[3].astype(BF16), axis, 1).astype(F32)
        far = swap((blocks[2].astype(F32) + far).astype(BF16), axis, 2)
        near = swap(blocks[1].astype(BF16), axis, 1)
        return blocks[0] + near.astype(F32) + far.astype(F32)
    received = [swap(blocks[k].astype(BF16), axis, k) for k in range(1, len(blocks))]
    total = blocks[0]
    for item in received:
        total = total + item.astype(F32)
    return total


def share_of(matrix, index, parts):
    size = matrix.shape[0] // parts
    return lax.dynamic_slice_in_dim(matrix, index * size, size, 0)


def by_index(blocks, index):
    count = len(blocks)
    total = jnp.zeros((count,) + blocks[0].shape, blocks[0].dtype)
    for k, item in enumerate(blocks):
        total = lax.dynamic_update_index_in_dim(total, item, index ^ k, 0)
    return total.reshape((count * blocks[0].shape[0],) + blocks[0].shape[1:])


def rows_of(matrix, parts):
    size = matrix.shape[0] // parts
    return [matrix[k * size : (k + 1) * size] for k in range(parts)]


def head_starts(rows):
    return [int(np.floor(HEADS * r / rows + 0.5)) for r in range(rows + 1)]


def most_heads(rows):
    starts = head_starts(rows)
    return max(b - a for a, b in zip(starts[:-1], starts[1:]))


def window_columns(rows, copies):
    starts = head_starts(rows)
    width = most_heads(rows) * HEAD_DIM
    table = np.full((rows, copies * width), -1, np.int64)
    for r in range(rows):
        count = (starts[r + 1] - starts[r]) * HEAD_DIM
        for t in range(copies):
            table[r, t * width : t * width + count] = t * D + starts[r] * HEAD_DIM + np.arange(count)
    return table


def move_tables(rows, parts):
    moves = []
    for k in range(rows):
        places = [[] for _ in range(rows)]
        columns = [[] for _ in range(rows)]
        for copies, place_at, column_at in parts:
            windows = window_columns(rows, copies)
            shard = copies * D // rows
            for r in range(rows):
                for p in range(windows.shape[1]):
                    if windows[r, p] >= 0 and windows[r, p] // shard == r ^ k:
                        places[r].append(place_at + p)
                        columns[r].append(column_at + int(windows[r, p] % shard))
        longest = -(-max(len(place) for place in places) // 16) * 16
        at = np.full((rows, longest), -1, np.int32)
        frm = np.full((rows, longest), -1, np.int32)
        for r in range(rows):
            at[r, : len(places[r])] = places[r]
            frm[r ^ k, : len(columns[r])] = columns[r]
        moves.append((at, frm))
    return moves


def table_row(table, index):
    return lax.dynamic_index_in_dim(jnp.asarray(table), index, 0, keepdims=True)


def one_hot(places, size):
    return (lax.broadcasted_iota(jnp.int32, (size, places.shape[1]), 0) == places).astype(BF16)


def mm(a, b):
    return jnp.dot(a, b, preferred_element_type=F32)


def mm_nt(a, b):
    return lax.dot_general(a, b, (((1,), (1,)), ((), ())), preferred_element_type=F32)


def mm_tn(a, b):
    return lax.dot_general(a, b, (((0,), (0,)), ((), ())), preferred_element_type=F32)


def move_columns(matrix, from_tables, to_tables, width, row, riders=None):
    counts = [table.shape[1] for table in from_tables]
    picked = mm(matrix, one_hot(table_row(np.concatenate(from_tables, 1), row), matrix.shape[1])).astype(BF16)
    slabs, others, at = [], [], 0
    for k, count in enumerate(counts):
        slab = picked[:, at : at + count]
        at += count
        if k == 0:
            slabs.append(slab)
            others.append(riders and riders[0])
        elif riders is None:
            slabs.append(swap(slab, "row", k) if count else slab)
        else:
            both = swap(jnp.concatenate([riders[k], slab], axis=1), "row", k)
            others.append(both[:, : riders[k].shape[1]])
            slabs.append(both[:, riders[k].shape[1] :])
    moved = mm_nt(jnp.concatenate(slabs, axis=1), one_hot(table_row(np.concatenate(to_tables, 1), row), width))
    return moved.astype(BF16), others


def positions(start, shape, dim, block, col):
    at = lax.broadcasted_iota(jnp.int32, shape, dim) + start
    shift = block.bit_length() - 1
    return lax.shift_left(lax.shift_right_logical(at, shift), shift + 1) + (at & (block - 1)) + col * block


def segments(pos, scal_ref):
    first = scal_ref[2]
    return (pos >= first).astype(jnp.int32) + (pos >= first + scal_ref[3]).astype(jnp.int32)


def mask_bias(scal_ref, query_at, query_shape, query_dim, key_shape, key_dim, block, key_col):
    query_pos = positions(query_at, query_shape, query_dim, block, scal_ref[1])
    key_pos = positions(0, key_shape, key_dim, block, key_col)
    allowed = (key_pos <= query_pos) & (segments(key_pos, scal_ref) == segments(query_pos, scal_ref))
    return jnp.where(allowed, 0.0, MASKED)


def in_order(source_ref, target_ref, row, blocks, block):
    for j in range(blocks):
        target_ref[j * block : (j + 1) * block, :] = source_ref[j ^ row]


def forward_kernel(blocks, block, heads, scal_ref, q_ref, kv0_ref, kv1_ref, out_ref, lse_ref, q_s, kv0_s, kv1_s, o_s):
    row = scal_ref[0]
    width = heads * HEAD_DIM
    in_order(q_ref, q_s, row, blocks, block)
    in_order(kv0_ref, kv0_s, row, blocks, block)
    in_order(kv1_ref, kv1_s, row, blocks, block)
    own = scal_ref[1]
    for i in range(blocks * block // CHUNK):
        span = slice(i * CHUNK, (i + 1) * CHUNK)
        keys = (i + 1) * CHUNK
        shape = (CHUNK, keys)
        bias0 = mask_bias(scal_ref, i * CHUNK, (CHUNK, 1), 0, (1, keys), 1, block, own)
        bias1 = mask_bias(scal_ref, i * CHUNK, (CHUNK, 1), 0, (1, keys), 1, block, 1 - own)
        for h in range(heads):
            at = slice(h * HEAD_DIM, (h + 1) * HEAD_DIM)
            va = slice(width + h * HEAD_DIM, width + (h + 1) * HEAD_DIM)
            query = q_s[span, at]
            s0 = mm_nt(query, kv0_s[:keys, at]) + bias0
            s1 = mm_nt(query, kv1_s[:keys, at]) + bias1
            top = jnp.maximum(jnp.max(s0, axis=1, keepdims=True), jnp.max(s1, axis=1, keepdims=True))
            e0 = jnp.exp(s0 - top)
            e1 = jnp.exp(s1 - top)
            total = jnp.sum(e0, axis=1, keepdims=True) + jnp.sum(e1, axis=1, keepdims=True)
            result = mm(e0.astype(BF16), kv0_s[:keys, va]) + mm(e1.astype(BF16), kv1_s[:keys, va])
            o_s[span, at] = (result / total).astype(BF16)
            lse_ref[span, h : h + 1] = top + jnp.log(total)
    for j in range(blocks):
        out_ref[j ^ row] = o_s[j * block : (j + 1) * block, :]


def backward_kernel(
    blocks,
    block,
    heads,
    scal_ref,
    q_ref,
    kv0_ref,
    kv1_ref,
    g_ref,
    lse_ref,
    dq_ref,
    own_ref,
    other_ref,
    q_s,
    kv0_s,
    kv1_s,
    g_s,
    dq_s,
    d0_s,
    d1_s,
):
    row = scal_ref[0]
    width = heads * HEAD_DIM
    in_order(q_ref, q_s, row, blocks, block)
    in_order(kv0_ref, kv0_s, row, blocks, block)
    in_order(kv1_ref, kv1_s, row, blocks, block)
    in_order(g_ref, g_s, row, blocks, block)
    own = scal_ref[1]
    chunks = blocks * block // CHUNK
    for i in reversed(range(chunks)):
        span = slice(i * CHUNK, (i + 1) * CHUNK)
        keys = (i + 1) * CHUNK
        bias0 = mask_bias(scal_ref, i * CHUNK, (1, CHUNK), 1, (keys, 1), 0, block, own)
        bias1 = mask_bias(scal_ref, i * CHUNK, (1, CHUNK), 1, (keys, 1), 0, block, 1 - own)
        for h in range(heads):
            at = slice(h * HEAD_DIM, (h + 1) * HEAD_DIM)
            va = slice(width + h * HEAD_DIM, width + (h + 1) * HEAD_DIM)
            query = q_s[span, at]
            grad = g_s[span, at]
            lse = lse_ref[h : h + 1, span]
            p0 = jnp.exp(mm_nt(kv0_s[:keys, at], query) + bias0 - lse)
            p1 = jnp.exp(mm_nt(kv1_s[:keys, at], query) + bias1 - lse)
            dp0 = mm_nt(kv0_s[:keys, va], grad)
            dp1 = mm_nt(kv1_s[:keys, va], grad)
            delta = jnp.sum(p0 * dp0, axis=0, keepdims=True) + jnp.sum(p1 * dp1, axis=0, keepdims=True)
            ds0 = (p0 * (dp0 - delta)).astype(BF16)
            ds1 = (p1 * (dp1 - delta)).astype(BF16)
            if i == chunks - 1:
                d0_s[:keys, at] = mm(ds0, query)
                d1_s[:keys, at] = mm(ds1, query)
                d0_s[:keys, va] = mm(p0.astype(BF16), grad)
                d1_s[:keys, va] = mm(p1.astype(BF16), grad)
            else:
                d0_s[:keys, at] += mm(ds0, query)
                d1_s[:keys, at] += mm(ds1, query)
                d0_s[:keys, va] += mm(p0.astype(BF16), grad)
                d1_s[:keys, va] += mm(p1.astype(BF16), grad)
            dquery = mm_tn(ds0, kv0_s[:keys, at]) + mm_tn(ds1, kv1_s[:keys, at])
            dq_s[span, at] = (dquery * HEAD_DIM ** (-0.5)).astype(BF16)
    for j in range(blocks):
        piece = slice(j * block, (j + 1) * block)
        dq_ref[j ^ row] = dq_s[piece, :]
        own_ref[j ^ row] = d0_s[piece, :]
        other_ref[j ^ row] = d1_s[piece, :].astype(BF16)


def vmem():
    return pl.BlockSpec(memory_space=pltpu.VMEM)


def smem():
    return pl.BlockSpec(memory_space=pltpu.SMEM)


def attend_forward(scal, queries, kv_own, kv_other, heads):
    blocks, block, width = queries.shape
    tokens = blocks * block
    return pl.pallas_call(
        functools.partial(forward_kernel, blocks, block, heads),
        out_shape=(
            jax.ShapeDtypeStruct((blocks, block, width), BF16),
            jax.ShapeDtypeStruct((tokens, heads), F32),
        ),
        in_specs=[smem(), vmem(), vmem(), vmem()],
        out_specs=(vmem(), vmem()),
        scratch_shapes=[
            pltpu.VMEM((tokens, width), BF16),
            pltpu.VMEM((tokens, 2 * width), BF16),
            pltpu.VMEM((tokens, 2 * width), BF16),
            pltpu.VMEM((tokens, width), BF16),
        ],
        compiler_params=pltpu.CompilerParams(vmem_limit_bytes=40 * 2**20),
        cost_estimate=pl.CostEstimate(
            flops=4 * tokens * 3 * tokens // 2 * width, bytes_accessed=6 * tokens * width * 2, transcendentals=heads * tokens * tokens
        ),
        name="attend_forward",
    )(scal, queries, kv_own, kv_other)


def attend_backward(scal, queries, kv_own, kv_other, grads, lse, heads):
    blocks, block, width = queries.shape
    tokens = blocks * block
    return pl.pallas_call(
        functools.partial(backward_kernel, blocks, block, heads),
        out_shape=(
            jax.ShapeDtypeStruct((blocks, block, width), BF16),
            jax.ShapeDtypeStruct((blocks, block, 2 * width), F32),
            jax.ShapeDtypeStruct((blocks, block, 2 * width), BF16),
        ),
        in_specs=[smem(), vmem(), vmem(), vmem(), vmem(), vmem()],
        out_specs=(vmem(), vmem(), vmem()),
        scratch_shapes=[
            pltpu.VMEM((tokens, width), BF16),
            pltpu.VMEM((tokens, 2 * width), BF16),
            pltpu.VMEM((tokens, 2 * width), BF16),
            pltpu.VMEM((tokens, width), BF16),
            pltpu.VMEM((tokens, width), BF16),
            pltpu.VMEM((tokens, 2 * width), F32),
            pltpu.VMEM((tokens, 2 * width), F32),
        ],
        compiler_params=pltpu.CompilerParams(vmem_limit_bytes=44 * 2**20),
        cost_estimate=pl.CostEstimate(
            flops=10 * tokens * 3 * tokens // 2 * width, bytes_accessed=14 * tokens * width * 2, transcendentals=heads * tokens * tokens
        ),
        name="attend_backward",
    )(scal, queries, kv_own, kv_other, grads, lse)


def norm_parts(resid_in):
    mean_value = jnp.sum(resid_in, axis=1, keepdims=True) / D
    square = jnp.sum(resid_in * resid_in, axis=1, keepdims=True) / D
    inverse = lax.rsqrt(square - mean_value * mean_value + EPSILON)
    return ((resid_in - mean_value) * inverse, inverse)


def norm_back(grad_in, normal, inverse, norm_gain):
    scaled = grad_in * norm_gain
    mean_scaled = jnp.sum(scaled, axis=1, keepdims=True) / D
    mean_cross = jnp.sum(scaled * normal, axis=1, keepdims=True) / D
    return inverse * (scaled - mean_scaled - normal * mean_cross)


def gelu_tanh(pre_value):
    return jax.nn.gelu(pre_value, approximate=True)


def on_device(
    tokens,
    lengths,
    first_gain,
    first_shift,
    qkv_weight,
    query_bias,
    value_bias,
    out_weight,
    out_bias,
    second_gain,
    second_shift,
    up_weight,
    up_bias,
    down_weight,
    down_bias,
    cotangent,
):
    rows = lax.axis_size("row")
    row = lax.axis_index("row")
    col = lax.axis_index("col")
    half = tokens.shape[1]
    block = tokens.shape[0] // 2
    heads = most_heads(rows)
    width = heads * HEAD_DIM

    def halves(blocks):
        mine = jnp.concatenate([share_of(item, col, 2) for item in blocks], axis=0)
        other = jnp.concatenate([share_of(item, 1 - col, 2) for item in blocks], axis=0)
        return jnp.concatenate([mine, swap(other, "col", 1)], axis=1)

    def unhalves(matrix):
        mine = matrix[:, :half]
        other = swap(matrix[:, half:], "col", 1)
        return jnp.concatenate([jnp.where(col == 0, mine, other), jnp.where(col == 0, other, mine)], axis=0)

    dps = lax.axis_size("dp")
    dp = lax.axis_index("dp")

    def over_cols(left, right, *others):
        other = after(mm_tn(left[:, half:], right).astype(BF16), *others)
        other = swap(other, "col", 1)
        return (mm_tn(left[:, :half], right) + other.astype(F32)).astype(BF16)

    def dp_shares(matrix):
        return [share_of(matrix, dp ^ k, dps) for k in range(dps)]

    x_blocks = gather_blocks(tokens, "row", 4)
    x_first = halves(x_blocks[: rows // 2])
    x_own = x_first[:block]
    x_all = jnp.concatenate([x_first, halves(x_blocks[rows // 2 :])], axis=0).astype(F32)

    vectors = jnp.stack([first_gain, first_shift, out_bias, second_gain, second_shift, down_bias])
    vectors = jnp.concatenate([vectors, swap(after(vectors, x_blocks[1]), "col", 1)], axis=1)
    gain1, shift1, out_b, gain2, shift2, down_b = [vectors[i] for i in range(6)]

    qkv_moves = move_tables(rows, [(3, 0, 0)])
    share = share_of(qkv_weight, dp, dps)
    share, _ = move_columns(share, [m[1] for m in qkv_moves], [m[0] for m in qkv_moves], 3 * width, row)
    share = after(share, x_blocks[1])
    qkv_blocks = gather_blocks(share, "dp")
    qkv_head = by_index(qkv_blocks, dp)
    qkv_other = swap(qkv_head, "col", 1)
    w_qkv = jnp.concatenate([qkv_head, qkv_other], axis=0)

    if out_weight.shape[0] % dps == 0:
        out_all = lax.all_gather(share_of(out_weight, dp, dps), ("row", "dp"))
    else:
        out_all = lax.all_gather(out_weight, "row")
    windows = window_columns(rows, 1)
    out_shard = D // rows
    absolute = np.concatenate([windows[np.arange(rows) ^ k] for k in range(rows)], axis=1).astype(np.int32)
    shard_at = (absolute // out_shard) ^ np.arange(rows)[:, None]
    relative = np.where(absolute >= 0, shard_at * out_shard + absolute % out_shard, -1).astype(np.int32)

    starts = jnp.asarray(np.array(head_starts(rows), np.int32))
    head_at = starts[row] * HEAD_DIM
    live_cols = jnp.arange(width, dtype=jnp.int32) < (starts[row + 1] - starts[row]) * HEAD_DIM

    def bias_window(vector):
        padded = jnp.concatenate([vector, jnp.zeros((width,), F32)])
        return jnp.where(live_cols, lax.dynamic_slice_in_dim(padded, head_at, width), 0.0)

    normal1, inverse1 = norm_parts(x_all)
    normed1 = (normal1 * gain1 + shift1).astype(BF16)
    kv_own = mm(normed1, w_qkv[:, width:])
    bias_kv = jnp.concatenate([jnp.zeros((width,), F32), bias_window(value_bias)])
    kv_own = (kv_own + bias_kv).astype(BF16)
    kv_other = swap(kv_own, "col", 1)
    queries = mm(normed1, w_qkv[:, :width])
    queries = (queries + bias_window(query_bias)).astype(BF16) * BF16(HEAD_DIM ** (-0.5))
    queries = queries.reshape(rows, block, width)
    kv_own = kv_own.reshape(rows, block, 2 * width)
    kv_other = kv_other.reshape(rows, block, 2 * width)
    scal = jnp.stack([row.astype(jnp.int32), col.astype(jnp.int32), lengths[0, 0], lengths[0, 1]])

    def live_rows(matrix, start):
        live = start + jnp.arange(matrix.shape[0], dtype=jnp.int32) < lengths[0, 0] + lengths[0, 1]
        return jnp.where(live[:, None], matrix, 0.0)

    grad_out = live_rows(halves([after(cotangent, x_blocks[rows - 1])]), (row * 2 + col) * block)
    grad_out_low = grad_out.astype(BF16)

    queries = after(queries, grad_out_low)
    attention, lse = attend_forward(scal, queries, kv_own, kv_other, heads)

    g_blocks = gather_blocks(grad_out_low, "row", 4, (attention,))
    att_blocks = send_blocks([attention[k] for k in range(rows)], "row")
    att_own = jnp.concatenate(att_blocks, axis=1)
    out_all = after(out_all, *att_blocks[1:], g_blocks[1], g_blocks[2]).reshape(D, half)
    w_out = jnp.concatenate([out_all.T, swap(out_all, "col", 1).T], axis=0)
    to_heads = one_hot(table_row(absolute, row), D)
    att_all = mm_nt(att_own, to_heads).astype(BF16)
    resid_mid = x_own.astype(F32) + (mm_nt(att_all, w_out) + out_b)

    normal2, inverse2 = norm_parts(resid_mid)
    normed2 = (normal2 * gain2 + shift2).astype(BF16)
    mlp_blocks = gather_blocks(normed2, "row", 4)
    up_own = after(up_weight, normed2)
    down_own = after(down_weight, normed2)
    w_up = jnp.concatenate([up_own, swap(up_own, "col", 1)], axis=0)
    w_down = jnp.concatenate([down_own, swap(down_own, "col", 1)], axis=1)
    w_up, w_down, mlp_blocks[0] = lax.optimization_barrier((w_up, w_down, mlp_blocks[0]))
    mlp_in = jnp.concatenate(mlp_blocks, axis=0)
    g_all = jnp.concatenate(g_blocks, axis=0)
    down_bias_part = jnp.sum(grad_out_low.astype(F32), axis=0)

    pre_act = mm(mlp_in, w_up) + up_bias
    act, gelu_back = jax.vjp(gelu_tanh, pre_act)
    grad_act = mm_nt(g_all, w_down)
    act, grad_pre = lax.optimization_barrier((act.astype(BF16), gelu_back(grad_act)[0].astype(BF16)))
    up_bias_part = jnp.sum(grad_pre.astype(F32), axis=0)
    grad_normed2 = mm_nt(grad_pre, w_up)

    blocks = rows_of(grad_normed2, rows)
    sent = [item.astype(BF16) for item in blocks[1:]]
    late_g, late_act, late_in, late_pre, *sent = lax.optimization_barrier((g_all, act, mlp_in, grad_pre, *sent))
    down_grad = over_cols(late_g, late_act)
    up_grad = over_cols(late_in, late_pre)
    att_shards = mm_nt(after(att_own, sent[0]), one_hot(table_row(relative, row), D)).astype(BF16)
    grad_normed2 = scatter_sum([after(blocks[0], down_grad, up_grad, att_shards, up_bias_part)] + sent, "row")
    second_gain_part = jnp.sum(grad_normed2 * normal2, axis=0)
    second_shift_part = jnp.sum(grad_normed2, axis=0)
    grad_mid = grad_out + norm_back(grad_normed2, normal2, inverse2, gain2)
    grad_mid_low = grad_mid.astype(BF16)
    out_bias_part = jnp.sum(grad_mid_low.astype(F32), axis=0)

    grad_att = mm(grad_mid_low, w_out).astype(BF16)
    grad_att = mm(grad_att, to_heads).astype(BF16)
    grad_att = [grad_att[:, k * width : (k + 1) * width] for k in range(rows)]
    late_act, late_mid, *grad_att = lax.optimization_barrier((act, grad_mid_low, *grad_att))
    grad_att = jnp.stack(send_blocks(grad_att, "row"))
    out_grad = over_cols(late_mid, att_shards)
    down_out = mm(late_act, w_down)
    grad_att = after(grad_att, out_grad)
    up_grad, down_grad = lax.psum((up_grad, down_grad), "dp")

    dq, dkv_own, dkv_other = attend_backward(scal, queries, kv_own, kv_other, grad_att, lse.T, heads)
    dkv = (dkv_own + swap(dkv_other, "col", 1).astype(F32)).astype(BF16)
    grad_qkv = jnp.concatenate([dq, dkv], axis=2).reshape(-1, 3 * width)
    qkv_bias_part = jnp.sum(grad_qkv.astype(F32), axis=0)
    normed_part = mm_nt(grad_qkv, w_qkv)
    first_gain_part = jnp.sum(normed_part * normal1, axis=0)
    first_shift_part = jnp.sum(normed_part, axis=0)
    qkv_grad = over_cols(normed1, after(grad_qkv, normed_part))
    def place(vector):
        mine, other = vector[:half], vector[half:]
        return jnp.concatenate([jnp.where(col == 0, mine, other), jnp.where(col == 0, other, mine)])

    def place_window(vector):
        padded = lax.dynamic_update_slice_in_dim(jnp.zeros((D + width,), F32), vector, head_at, 0)
        return padded[:D]

    def place_rows(vector):
        return lax.dynamic_update_slice_in_dim(jnp.zeros((FF,), F32), vector, row * vector.shape[0], 0)

    small = jnp.concatenate(
        [
            place_rows(up_bias_part),
            place(down_bias_part),
            place(second_gain_part),
            place(second_shift_part),
            place(out_bias_part),
            place(first_gain_part),
            place(first_shift_part),
            place_window(qkv_bias_part[:width]),
            place_window(qkv_bias_part[2 * width :]),
        ]
    )
    shares = dp_shares(jnp.concatenate([qkv_grad, out_grad], axis=1))
    blocks = rows_of(normed_part, rows)
    grad_normed1 = scatter_sum([after(blocks[0], *shares)] + blocks[1:], "row", 4)
    back1 = norm_back(grad_normed1, normal1[:block], inverse1[:block], gain1)
    input_grad = unhalves(grad_mid + back1)

    summed = scatter_sum([shares[0].astype(F32)] + shares[1:], "dp").astype(BF16)
    qkv_grad, out_grad = summed[:, : 3 * width], summed[:, 3 * width :]
    share_rows = qkv_grad.shape[0]
    small_width = -(-small.shape[0] // share_rows)
    small = jnp.pad(small, (0, small_width * share_rows - small.shape[0])).reshape(share_rows, small_width)
    riders = [
        jnp.concatenate([out_grad[:, k * out_shard : (k + 1) * out_shard], small.astype(BF16)], axis=1) for k in range(rows)
    ]
    qkv_grad, riders = move_columns(
        qkv_grad, [m[0] for m in qkv_moves], [m[1] for m in qkv_moves], 3 * out_shard, row, riders
    )
    rider = sum(item.astype(F32) for item in riders).astype(BF16)
    both, up_grad, down_grad = lax.optimization_barrier((jnp.concatenate([qkv_grad, rider], axis=1), up_grad, down_grad))
    both = gather_blocks(both, "dp")
    small = sum(item[:, 4 * out_shard :].astype(F32) for item in both)
    small = (small + swap(small, "col", 1)).reshape(-1)
    both = [item[:, : 4 * out_shard] for item in both]
    both = by_index([item.astype(F32) for item in both], dp)
    qkv_grad = both[:, : 3 * out_shard]
    out_grad = both[:, 3 * out_shard :].T

    blocks = rows_of(down_out, rows)
    block_out = scatter_sum([blocks[0]] + [after(item.astype(BF16), rider) for item in blocks[1:]], "row", 4)
    block_out = unhalves((resid_mid + (block_out + down_b)).astype(BF16))

    def own_half(part):
        return lax.dynamic_slice_in_dim(small, FF + part * D + col * half, half)

    up_width = up_bias.shape[0]
    return (
        block_out,
        input_grad,
        own_half(4),
        own_half(5),
        qkv_grad,
        small[FF + 6 * D : FF + 7 * D],
        small[FF + 7 * D : FF + 8 * D],
        out_grad,
        own_half(3),
        own_half(1),
        own_half(2),
        up_grad.astype(F32),
        lax.dynamic_slice_in_dim(small, row * up_width, up_width),
        down_grad.T.astype(F32),
        own_half(0),
    )


def solution(mesh):
    in_specs = (
        P(("dp", "row"), "col"),
        P("dp", None),
        P("col"),
        P("col"),
        P("col", "row"),
        P(),
        P(),
        P("row", "col"),
        P("col"),
        P("col"),
        P("col"),
        P("col", "row"),
        P("row"),
        P("row", "col"),
        P("col"),
        P(("dp", "row"), "col"),
    )
    out_specs = (
        P(("dp", "row"), "col"),
        P(("dp", "row"), "col"),
        P("col"),
        P("col"),
        P("col", "row"),
        P(),
        P(),
        P("row", "col"),
        P("col"),
        P("col"),
        P("col"),
        P("col", "row"),
        P("row"),
        P("row", "col"),
        P("col"),
    )
    return jax.shard_map(
        on_device, mesh=mesh, in_specs=in_specs, out_specs=out_specs, check_vma=False
    )
```
